32 devices in a mesh: ctx: 4 (over z), exp: 8 (over y, x, core).
Axes of the slice: x: 2, y: 2, z: 4, core: 2. Of those that a mesh axis runs over, the one named last changes fastest.
Arguments:
- tokens_in: bfloat16 [16, 1024, 768], P('exp', 'ctx'), may hold values from -6 to 6
- first_gain: bfloat16 [768], P('exp'), may hold values from 0.099609375 to 1.8984375
- joint_projection: bfloat16 [768, 2304], P('exp'), may hold values from -0.21875 to 0.21875
- out_projection: bfloat16 [768, 768], P('exp'), may hold values from -2.5 to 2.5
- bias_table: bfloat16 [32, 12], P('exp'), may hold values from -4 to 4
- second_gain: bfloat16 [768], P('exp'), may hold values from 0.099609375 to 1.8984375
- router_weight: bfloat16 [768, 8], P('exp'), may hold values from -0.15625 to 0.15625
- expert_up: bfloat16 [8, 768, 3072], P('exp', None, 'ctx'), may hold values from -0.21875 to 0.21875
- expert_down: bfloat16 [8, 3072, 768], P('exp', 'ctx'), may hold values from -0.95703125 to 0.95703125
- expert_index: int32 [16, 1024, 1], P('exp', 'ctx'), may hold values from 0 to 7; in each aligned block of 256 rows (0 to 255, 256 to 511, ..., all dimensions but the last counted through in order) at most 40 rows name the same one
- keep_mask: int32 [16, 1024], P('exp', 'ctx'), may hold values 0 or 1
- buckets: int32 [2047], replicated, may hold values from 0 to 31
- cotangent: bfloat16 [16, 1024, 768], P('exp', 'ctx'), may hold values from -6 to 6
Outputs:
- layer_out: bfloat16 [16, 1024, 768], P('exp', 'ctx')
- grad_tokens: float32 [16, 1024, 768], P('exp', 'ctx')
- grad_first_gain: float32 [768], P('exp')
- grad_joint: float32 [768, 2304], P('exp')
- grad_out_projection: float32 [768, 768], P('exp')
- grad_bias_table: float32 [32, 12], P('exp')
- grad_second_gain: float32 [768], P('exp')
- grad_router: float32 [768, 8], P('exp')
- grad_expert_up: float32 [8, 768, 3072], P('exp', None, 'ctx')
- grad_expert_down: float32 [8, 3072, 768], P('exp', 'ctx')
The draws below stay inside these ranges and needn't reach their ends.
Inputs may be any that keep to these rules, and one draw needn't show every extreme that they name: `expert_index`: within each aligned block of 256 positions of a sequence, no expert is named by more than 40 tokens.
All inputs are finite; a program needn't handle non-finite values. No bound on the sum of `keep_mask` on one device may be relied on, other than what follows from the above.
Results may differ from the reference program's by a relative error of at most 0.02.
Values may be sent and summed in bfloat16 or wider, within the bound.
No kernel may reach another device: no remote copies, remote signals or barrier semaphores. Data moves between devices by JAX's collectives and lax.ppermute only.
A program may use at most 256 MiB of HBM per device.

```python
import math
import jax
import jax.numpy as jnp
import numpy as np
from jax import lax

D = 768
HEADS = 12
FF = 3072
BUCKETS = 32
BLOCK = 256
EXPERTS = 8
MOST = 40
SEQS = 16
LENGTH = 1024
N_CTX = 4


def plant(array, key, low, top_value):
    index_at = [jax.random.randint(jax.random.fold_in(key, axis), (), 0, length) for axis, length in enumerate(array.shape)]
    widest = array.shape.index(max(array.shape))
    beside = index_at[:widest] + [(index_at[widest] + 1) % array.shape[widest]] + index_at[widest + 1:]
    return array.at[tuple(index_at)].set(low).at[tuple(beside)].set(top_value)


def levels(stream_key, dims, shards, smallest, largest):
    def one(position, shards_of):
        heights = jax.random.uniform(jax.random.fold_in(jax.random.fold_in(stream_key, 6), position), (shards_of,), jnp.float32, smallest / len(shards), largest / len(shards))
        return jnp.repeat(jnp.exp(heights), dims[position] // shards_of).reshape((-1,) + (1,) * (len(dims) - position - 1))

    factor_of = one(*shards[0])
    for cut in shards[1:]:
        factor_of = factor_of * one(*cut)
    return factor_of


def routed_block(key, own, number, rows, number_of, top, bound, skew):
    order = jax.random.permutation(key, number_of)
    packed, common = shares(number_of, rows * top, bound, skew, True), shares(number_of, rows * top, bound, skew, False)
    places = jnp.arange(number_of)

    def named(tallies, turn):
        used = int((tallies > 0).sum())
        fixed = max(1, used // 4)
        passed = fixed + (places - fixed + turn * (used - fixed)) % max(1, number_of - fixed)
        return jnp.zeros((number_of,), jnp.int32).at[order[jnp.where(places < fixed, places, passed)]].set(jnp.asarray(tallies, jnp.int32))

    tallies = jnp.where(number % 4 == 0, named(packed, number // 4), named(common, number - number // 4 - 1))
    mixed = jax.random.permutation(jax.random.fold_in(own, 3), number_of)
    source_of, receiver = mixed[0:number_of // 2 * 2:2], mixed[1:number_of // 2 * 2:2]
    slack = jnp.minimum(tallies[source_of] - 1, bound - tallies[receiver]) // 2
    slack = jnp.where((source_of == order[0]) | (receiver == order[0]) | (tallies[receiver] == 0), 0, jnp.maximum(slack, 0))
    passed = jax.random.randint(jax.random.fold_in(own, 4), (number_of // 2,), 0, 1 << 20) % (slack + 1)
    tallies = tallies.at[source_of].add(-passed).at[receiver].add(passed)
    items = jnp.searchsorted(jnp.cumsum(tallies), jnp.arange(rows * top), side="right").astype(jnp.int32)
    listing = items.reshape(top, rows).T
    listing = listing[jax.random.permutation(jax.random.fold_in(own, 1), rows)]
    turn = jax.random.randint(jax.random.fold_in(own, 2), (rows, 1), 0, top)
    return jnp.take_along_axis(listing, (jnp.arange(top)[None, :] + turn) % top, axis=1)


def shares(count, total, bound, lean, full):
    weights = [(1 << 20) // math.isqrt(rank ** lean) + 1 for rank in range(1, count + 1)]
    largest = bound if full else min(bound, max(-(-total // count), total * weights[0] // sum(weights)))
    least = 1 if total - largest >= count - 1 else 0
    holding, rest = [largest] + [least] * (count - 1), total - largest - least * (count - 1)
    while rest > 0:
        candidates = [i for i in range(1, count) if holding[i] < largest] or [i for i in range(1, count) if holding[i] < bound]
        pool, budget = sum([weights[i] for i in candidates]), rest
        for i in candidates:
            more = min(bound - holding[i], max(1, budget * weights[i] // pool), rest)
            holding[i] = holding[i] + more
            rest = rest - more
    return np.array(holding)


def scatter_about(rng, dims, scale, reach, split=(), held_as=jnp.bfloat16):
    drawn = scale * jax.random.normal(rng, dims, jnp.float32)
    if split:
        drawn = drawn * levels(rng, dims, split, -0.22, 0.18)
    return jnp.clip(drawn, -reach, reach).astype(held_as)


def setup_inputs(seed: int = 0) -> dict:
    splits = jax.random.split(jax.random.key(seed), 14)
    tokens_in = scatter_about(splits[0], (SEQS, LENGTH, D), 1.0, 6.0, ((0, 8), (1, 4)))
    first_gain = jnp.clip(1.0 + 0.18 * jax.random.normal(splits[1], (D,), jnp.float32), 0.099609375, 1.8984375).astype(jnp.bfloat16)
    joint_projection = scatter_about(splits[2], (D, 3 * D), D ** -0.5, 0.21875, ((0, 8),))
    out_projection = scatter_about(splits[3], (D, D), (max(4, D // 128)) ** -0.5, 2.5, ((0, 8),))
    bias_table = scatter_about(splits[4], (BUCKETS, HEADS), 1.0, 4.0, ((0, 8),))
    second_gain = jnp.clip(1.0 + 0.18 * jax.random.normal(splits[5], (D,), jnp.float32), 0.099609375, 1.8984375).astype(jnp.bfloat16)
    router_weight = scatter_about(splits[6], (D, EXPERTS), (2 * D) ** -0.5, 0.15625, ((0, 8),))
    expert_up = scatter_about(splits[7], (EXPERTS, D, FF), D ** -0.5, 0.21875, ((0, 8), (2, 4)))
    expert_down = scatter_about(splits[8], (EXPERTS, FF, D), (0.02 * EXPERTS), 0.95703125, ((0, 8), (1, 4)))
    expert_index_keys = jax.random.split(jax.random.fold_in(splits[9], 1), SEQS * LENGTH // BLOCK)
    expert_index_turns = jax.random.permutation(jax.random.fold_in(splits[9], 3), SEQS * LENGTH // BLOCK)
    expert_index = jax.vmap(lambda own, number: routed_block(jax.random.fold_in(splits[9], 2), own, number, BLOCK, EXPERTS, 1, MOST, 1))(expert_index_keys, expert_index_turns).reshape((SEQS, LENGTH, 1))
    keep_mask = plant((jax.random.randint(splits[10], (SEQS, LENGTH), 0, 8) < 7).astype(jnp.int32), jax.random.fold_in(splits[10], 1), 0, 1)
    buckets = plant(jax.random.randint(splits[11], (2 * LENGTH - 1,), 0, BUCKETS), jax.random.fold_in(splits[11], 1), 0, BUCKETS - 1).astype(jnp.int32)
    cotangent = scatter_about(splits[12], (SEQS, LENGTH, D), 1.0, 6.0, ((0, 8), (1, 4)))
    return {"tokens_in": tokens_in, "first_gain": first_gain, "joint_projection": joint_projection, "out_projection": out_projection, "bias_table": bias_table, "second_gain": second_gain, "router_weight": router_weight, "expert_up": expert_up, "expert_down": expert_down, "expert_index": expert_index, "keep_mask": keep_mask, "buckets": buckets, "cotangent": cotangent}


HIGHEST = lax.Precision.HIGHEST
EPSILON = 1e-06
SCORE_SCALE = 0.125

@jax.custom_vjp
def low(v):
    return lax.optimization_barrier(v.astype(jnp.bfloat16)).astype(jnp.float32)

@jax.custom_vjp
def low_back(v):
    return v

def low_keep(v):
    return (low(v), None)

def low_pass(kept, grad):
    return (grad,)

def back_keep(v):
    return (v, None)

def back_low(kept, grad):
    return (low(grad),)
low.defvjp(low_keep, low_pass)
low_back.defvjp(back_keep, back_low)

def rms_norm(row_data, gain_vec):
    return row_data * lax.rsqrt(lax.optimization_barrier(jnp.mean(row_data * row_data, axis=-1, keepdims=True)) + EPSILON) * gain_vec

def attend_sequence(seq_parts, offset_values):
    queries, key_rows, value_rows = seq_parts
    seq_len = queries.shape[0]
    query_block = math.gcd(512, seq_len)
    starts = jnp.arange(seq_len // query_block, dtype=jnp.int32) * query_block
    positions = jnp.arange(seq_len, dtype=jnp.int32)

    def one_block(block_start):
        block_queries = lax.dynamic_slice_in_dim(queries, block_start, query_block, 0)
        scores = jnp.einsum('ihe,jhe->hij', block_queries, key_rows, precision=HIGHEST) * SCORE_SCALE
        row_pos = block_start + jnp.arange(query_block, dtype=jnp.int32)
        offsets = positions[None, :] - row_pos[:, None] + (seq_len - 1)
        scores = low_back(scores + offset_values[:, offsets])
        weights = low(jax.nn.softmax(scores, axis=-1))
        return jnp.einsum('hij,jhe->ihe', weights, value_rows, precision=HIGHEST)
    outputs = lax.map(jax.checkpoint(one_block), starts)
    return outputs.reshape(seq_len, queries.shape[1], queries.shape[2])

def reference(tokens_in, first_gain, joint_projection, out_projection, bias_table, second_gain, router_weight, expert_up, expert_down, expert_index, keep_mask, buckets, cotangent):
    seq_count, seq_len, model_width = tokens_in.shape
    head_count = bias_table.shape[1]
    head_size = model_width // head_count
    expert_count = router_weight.shape[1]
    token_count = seq_count * seq_len
    chosen = expert_index.reshape(seq_count, seq_len)
    choice_hot = (chosen[..., None] == jnp.arange(expert_count, dtype=jnp.int32)).astype(jnp.int32)
    blocked = choice_hot.reshape(seq_count, N_CTX, BLOCK, expert_count)
    running = jnp.cumsum(blocked, axis=2).astype(jnp.int32)
    slot_rank = lax.optimization_barrier(jnp.sum(running * blocked, axis=-1)).astype(jnp.int32) - 1
    block_id = jnp.arange(seq_count, dtype=jnp.int32)[:, None] * N_CTX + jnp.arange(N_CTX, dtype=jnp.int32)[None, :]
    region = seq_count * N_CTX * MOST
    local_slot = (block_id[:, :, None] * MOST + slot_rank).astype(jnp.int32).reshape(seq_count, seq_len)
    flat_slot = (chosen * region + local_slot).reshape(token_count).astype(jnp.int32)
    is_live = keep_mask.reshape(token_count) > 0
    total_slots = expert_count * region
    target = jnp.where(is_live, flat_slot, total_slots).astype(jnp.int32)
    source_row = jnp.full((total_slots,), token_count, jnp.int32).at[target].set(jnp.arange(token_count, dtype=jnp.int32), mode='drop')
    kept_rows = keep_mask.reshape(token_count).astype(jnp.float32)
    flat_hot = choice_hot.reshape(token_count, expert_count).astype(jnp.float32)
    bucket_hot = (buckets[None, :] == jnp.arange(BUCKETS, dtype=jnp.int32)[:, None]).astype(jnp.float32)

    def layer_forward(tokens, gain_one, weight_joint, weight_out, table, gain_two, weight_router, weight_up, weight_down):
        hidden_one = low(rms_norm(tokens, gain_one)).reshape(token_count, model_width)
        projected = low(low_back(jnp.dot(hidden_one, weight_joint, precision=HIGHEST)))
        split_joint = projected.reshape(seq_count, seq_len, 3, head_count, head_size)
        offset_values = jnp.dot(table.T, bucket_hot, precision=HIGHEST)
        attended = lax.map(lambda seq_parts: attend_sequence(seq_parts, offset_values), (split_joint[:, :, 0], split_joint[:, :, 1], split_joint[:, :, 2]))
        attended = low(low_back(attended.reshape(token_count, model_width)))
        mixed_rows = low_back(jnp.dot(attended, weight_out, precision=HIGHEST))
        residual = tokens.reshape(token_count, model_width) + mixed_rows
        hidden_two = low(rms_norm(residual, gain_two))
        logits = low_back(jnp.dot(hidden_two, weight_router, precision=HIGHEST))
        router_prob = jax.nn.softmax(logits, axis=-1)
        gate_value = kept_rows * lax.optimization_barrier(jnp.sum(router_prob * flat_hot, axis=-1))
        padded = jnp.concatenate([hidden_two, jnp.zeros((1, model_width), jnp.float32)], axis=0)
        expert_inputs = low_back(padded[source_row]).reshape(expert_count, region, model_width)

        def one_expert(expert_parts):
            rows_in, matrix_up, matrix_down = expert_parts
            before = low_back(jnp.dot(rows_in, matrix_up, precision=HIGHEST))
            acted = low(jax.nn.gelu(before))
            return low(low_back(jnp.dot(acted, matrix_down, precision=HIGHEST)))
        produced = lax.map(jax.checkpoint(one_expert), (expert_inputs, weight_up, weight_down))
        produced = jnp.concatenate([produced.reshape(total_slots, model_width), jnp.zeros((1, model_width), jnp.float32)], axis=0)
        expert_rows = produced[target]
        combined = residual + gate_value[:, None] * expert_rows
        return combined.reshape(seq_count, seq_len, model_width)
    primal, back_fn = jax.vjp(layer_forward, tokens_in.astype(jnp.float32), first_gain.astype(jnp.float32), joint_projection.astype(jnp.float32), out_projection.astype(jnp.float32), bias_table.astype(jnp.float32), second_gain.astype(jnp.float32), router_weight.astype(jnp.float32), expert_up.astype(jnp.float32), expert_down.astype(jnp.float32))
    grads = back_fn(cotangent.astype(jnp.float32))
    return (primal.astype(jnp.bfloat16), grads[0], grads[1], grads[2], grads[3], grads[4], grads[5], grads[6], grads[7], grads[8])
```

```python
import functools

import jax
import jax.numpy as jnp
from jax import lax
from jax.experimental import pallas as pl
from jax.experimental.pallas import tpu as pltpu
from jax.sharding import PartitionSpec as P

EPSILON = 1e-06
HALF = 64
TILE = 128
GROUP = 256
VMEM_BYTES = 50 * 1024 * 1024
SCORE_SCALE = 0.125
HIGHEST = lax.Precision.HIGHEST
BOTH = ("ctx", "exp")


def contract_last(left, right):
    return lax.dot_general(
        left, right, (((1,), (1,)), ((), ())), preferred_element_type=jnp.float32
    )


def matmul(left, right):
    return lax.dot_general(
        left, right, (((1,), (0,)), ((), ())), preferred_element_type=jnp.float32
    )


def skew_kernel(offset_ref, skew_ref):
    padded = offset_ref.shape[-1]
    kept = skew_ref.shape[1]
    rows = jnp.broadcast_to(offset_ref[0], (TILE, padded))
    rolled = pltpu.roll(rows, padded - (TILE - 1), 1, stride=1, stride_axis=0)
    skew_ref[0] = rolled[:, :kept].T.astype(skew_ref.dtype)


def make_skew(offset_values):
    head_count, padded = offset_values.shape
    kept = padded - TILE
    return pl.pallas_call(
        skew_kernel,
        grid=(head_count,),
        in_specs=[pl.BlockSpec((1, 1, padded), lambda h: (h, 0, 0))],
        out_specs=pl.BlockSpec((1, kept, TILE), lambda h: (h, 0, 0)),
        out_shape=jax.ShapeDtypeStruct((head_count, kept, TILE), jnp.bfloat16),
        compiler_params=pltpu.CompilerParams(vmem_limit_bytes=VMEM_BYTES),
        name="skew_bias",
    )(offset_values.reshape(head_count, 1, padded))


def half_mask(rows, half):
    lanes = lax.broadcasted_iota(jnp.int32, (rows, TILE), 1)
    return (lanes // HALF) == half


def bias_rows(key_base, query_base, seq_len):
    return key_base - query_base + seq_len - TILE


def forward_kernel(
    base_ref, q_ref, k_ref, v_ref, skew_ref, out_ref, lse_ref, score_ref, prob_ref, *, chunk
):
    query_rows = q_ref.shape[0]
    key_rows = k_ref.shape[0]
    seq_len = key_rows
    mask = [half_mask(GROUP, 0), half_mask(GROUP, 1)]
    value_t = v_ref[...].T
    for group in range(query_rows // GROUP):
        rows = slice(group * GROUP, (group + 1) * GROUP)
        query_base = base_ref[0] + group * GROUP
        halves = []
        for half in range(2):
            queries = jnp.where(mask[half], q_ref[rows], 0).astype(jnp.bfloat16)
            score_ref[half] = contract_last(k_ref[...], queries)
            top = jnp.full((8, GROUP), -jnp.inf, jnp.float32)
            for start in range(0, key_rows, chunk):
                key_base = base_ref[start // query_rows] + start % query_rows
                place = pl.multiple_of(bias_rows(key_base, query_base, seq_len), TILE)
                left = skew_ref[half, pl.ds(place, chunk), :]
                right = skew_ref[half, pl.ds(place - TILE, chunk), :]
                bias = jnp.concatenate([left, right], axis=1).astype(jnp.float32)
                piece = score_ref[half, start : start + chunk] + bias
                score_ref[half, start : start + chunk] = piece
                top = jnp.maximum(top, jnp.max(piece.reshape(chunk // 8, 8, GROUP), axis=0))
            top = jnp.max(top, axis=0, keepdims=True)
            total = jnp.zeros((8, GROUP), jnp.float32)
            for start in range(0, key_rows, chunk):
                piece = jnp.exp(score_ref[half, start : start + chunk] - top)
                total = total + jnp.sum(piece.reshape(chunk // 8, 8, GROUP), axis=0)
                prob_ref[half, start : start + chunk] = piece.astype(jnp.bfloat16)
            total = jnp.sum(total, axis=0, keepdims=True)
            lse_ref[0, half : half + 1, rows] = top + jnp.log(total)
            mixed = matmul(value_t[half * HALF : (half + 1) * HALF], prob_ref[half])
            halves.append(mixed / total)
        out_ref[rows] = jnp.concatenate(halves, axis=0).T


def attend_forward(bases, queries, key_values, skew):
    query_rows, width = queries.shape
    key_rows = key_values.shape[0]
    kept = skew.shape[1]
    pairs = width // TILE
    chunk = TILE
    return pl.pallas_call(
        functools.partial(forward_kernel, chunk=chunk),
        grid_spec=pltpu.PrefetchScalarGridSpec(
            num_scalar_prefetch=1,
            grid=(pairs,),
            in_specs=[
                pl.BlockSpec((query_rows, TILE), lambda p, _: (0, p)),
                pl.BlockSpec((key_rows, TILE), lambda p, _: (0, p)),
                pl.BlockSpec((key_rows, TILE), lambda p, _: (0, p + pairs)),
                pl.BlockSpec((2, kept, TILE), lambda p, _: (p, 0, 0)),
            ],
            out_specs=[
                pl.BlockSpec((query_rows, TILE), lambda p, _: (0, p)),
                pl.BlockSpec((1, 2, query_rows), lambda p, _: (p, 0, 0)),
            ],
            scratch_shapes=[
                pltpu.VMEM((2, key_rows, GROUP), jnp.float32),
                pltpu.VMEM((2, key_rows, GROUP), jnp.bfloat16),
            ],
        ),
        out_shape=[
            jax.ShapeDtypeStruct((query_rows, width), jnp.float32),
            jax.ShapeDtypeStruct((pairs, 2, query_rows), jnp.float32),
        ],
        compiler_params=pltpu.CompilerParams(vmem_limit_bytes=VMEM_BYTES),
        name="attend_forward",
    )(bases, queries, key_values, key_values, skew)


def backward_kernel(
    base_ref, q_ref, do_ref, o_ref, k_ref, v_ref, skew_ref, lse_ref,
    dq_ref, dk_ref, dv_ref, off_ref,
    score_ref, gradp_ref, prob_ref, grads_ref, accum_k, accum_v, accum_skew,
    *, chunk,
):
    query_rows = q_ref.shape[0]
    key_rows = k_ref.shape[0]
    seq_len = key_rows
    mask = [half_mask(GROUP, 0), half_mask(GROUP, 1)]
    key_t = k_ref[...].T
    accum_skew[...] = jnp.zeros_like(accum_skew)
    for group in range(query_rows // GROUP):
        rows = slice(group * GROUP, (group + 1) * GROUP)
        query_base = base_ref[0] + group * GROUP
        product = (do_ref[rows].astype(jnp.float32) * o_ref[rows]).T
        halves = []
        sum_k = None
        for half in range(2):
            queries = jnp.where(mask[half], q_ref[rows], 0).astype(jnp.bfloat16)
            grads_out = jnp.where(mask[half], do_ref[rows], 0).astype(jnp.bfloat16)
            score_ref[half] = contract_last(k_ref[...], queries)
            gradp_ref[half] = contract_last(v_ref[...], grads_out)
            logsum = lse_ref[0, half : half + 1, rows]
            delta = jnp.sum(product[half * HALF : (half + 1) * HALF], axis=0, keepdims=True)
            for start in range(0, key_rows, chunk):
                key_base = base_ref[start // query_rows] + start % query_rows
                place = pl.multiple_of(bias_rows(key_base, query_base, seq_len), TILE)
                here = pl.ds(start, chunk)
                left = skew_ref[half, pl.ds(place, chunk), :]
                right = skew_ref[half, pl.ds(place - TILE, chunk), :]
                bias = jnp.concatenate([left, right], axis=1).astype(jnp.float32)
                prob = jnp.exp(score_ref[half, here] + bias - logsum)
                grads = prob * (gradp_ref[half, here] - delta)
                prob_ref[half, here] = prob.astype(jnp.bfloat16)
                grads_ref[half, here] = grads.astype(jnp.bfloat16)
                accum_skew[half, pl.ds(place, chunk), :] += grads[:, :TILE]
                accum_skew[half, pl.ds(place - TILE, chunk), :] += grads[:, TILE:]
            part_k = matmul(grads_ref[half], queries)
            part_v = matmul(prob_ref[half], grads_out)
            sum_k = part_k if sum_k is None else sum_k + part_k
            sum_v = part_v if half == 0 else sum_v + part_v
            halves.append(matmul(key_t[half * HALF : (half + 1) * HALF], grads_ref[half]))
        if group == 0:
            accum_k[...] = sum_k
            accum_v[...] = sum_v
        else:
            accum_k[...] += sum_k
            accum_v[...] += sum_v
        dq_ref[rows] = (jnp.concatenate(halves, axis=0) * 0.125).T.astype(dq_ref.dtype)
    dk_ref[...] = accum_k[...].astype(dk_ref.dtype)
    dv_ref[...] = accum_v[...].astype(dv_ref.dtype)
    for half in range(2):
        turned = accum_skew[half].T
        padded = turned.shape[1]
        count = TILE // 2
        while count:
            turned = turned[:count] + pltpu.roll(turned[count : 2 * count], padded - count, 1)
            count //= 2
        off_ref[0, half : half + 1] = pltpu.roll(turned, TILE - 1, 1)


def attend_backward(bases, queries, grads_out, outputs, key_values, skew, logsum):
    query_rows, width = queries.shape
    key_rows = key_values.shape[0]
    kept = skew.shape[1]
    pairs = width // TILE
    chunk = TILE
    column = lambda count: pl.BlockSpec((count, TILE), lambda p, _: (0, p))
    return pl.pallas_call(
        functools.partial(backward_kernel, chunk=chunk),
        grid_spec=pltpu.PrefetchScalarGridSpec(
            num_scalar_prefetch=1,
            grid=(pairs,),
            in_specs=[
                column(query_rows), column(query_rows), column(query_rows),
                column(key_rows),
                pl.BlockSpec((key_rows, TILE), lambda p, _: (0, p + pairs)),
                pl.BlockSpec((2, kept, TILE), lambda p, _: (p, 0, 0)),
                pl.BlockSpec((1, 2, query_rows), lambda p, _: (p, 0, 0)),
            ],
            out_specs=[
                column(query_rows), column(key_rows), column(key_rows),
                pl.BlockSpec((1, 2, kept + TILE), lambda p, _: (p, 0, 0)),
            ],
            scratch_shapes=[
                pltpu.VMEM((2, key_rows, GROUP), jnp.float32),
                pltpu.VMEM((2, key_rows, GROUP), jnp.float32),
                pltpu.VMEM((2, key_rows, GROUP), jnp.bfloat16),
                pltpu.VMEM((2, key_rows, GROUP), jnp.bfloat16),
                pltpu.VMEM((key_rows, TILE), jnp.float32),
                pltpu.VMEM((key_rows, TILE), jnp.float32),
                pltpu.VMEM((2, kept + TILE, TILE), jnp.float32),
            ],
        ),
        out_shape=[
            jax.ShapeDtypeStruct((query_rows, width), jnp.bfloat16),
            jax.ShapeDtypeStruct((key_rows, width), jnp.bfloat16),
            jax.ShapeDtypeStruct((key_rows, width), jnp.bfloat16),
            jax.ShapeDtypeStruct((pairs, 2, kept + TILE), jnp.float32),
        ],
        compiler_params=pltpu.CompilerParams(vmem_limit_bytes=VMEM_BYTES),
        name="attend_backward",
    )(bases, queries, grads_out, outputs, key_values, key_values, skew, logsum)


def rms_forward(row_data, gain_vec):
    inverse = lax.rsqrt(jnp.mean(row_data * row_data, axis=-1, keepdims=True) + EPSILON)
    return (row_data * inverse * gain_vec, inverse)


def rms_backward(row_data, inverse, gain_vec, grad_out):
    normed = row_data * inverse
    grad_gain = jnp.sum(grad_out * normed, axis=0)
    scaled = grad_out * gain_vec
    spread = jnp.mean(scaled * normed, axis=-1, keepdims=True)
    return (inverse * (scaled - normed * spread), grad_gain)


class Layout:
    def __init__(self):
        self.ctx_count = lax.axis_size("ctx")
        self.exp_count = lax.axis_size("exp")
        self.span = self.ctx_count // 4
        self.members = 2 * self.span
        self.ctx = lax.axis_index("ctx")
        self.core = lax.axis_index("exp") % 2
        self.member = (self.ctx % self.span) * 2 + self.core
        self.side = (self.ctx // self.span) % 2

    def number(self, ctx, exp):
        return ctx * self.exp_count + exp

    def round_pairs(self, turn):
        pairs = []
        for ctx in range(self.ctx_count):
            for exp in range(self.exp_count):
                seq = 2 * (exp % 2) + (turn + ctx) % 2
                member = ctx // 2
                target = self.number(seq * self.span + member // 2, exp // 2 * 2 + member % 2)
                pairs.append((self.number(ctx, exp), target))
        return pairs

    def member_pairs(self, shift):
        pairs = []
        for ctx in range(self.ctx_count):
            for exp in range(self.exp_count):
                start = ctx // self.span * self.span
                member = ((ctx - start) * 2 + exp % 2 + shift) % self.members
                target = self.number(start + member // 2, exp // 2 * 2 + member % 2)
                pairs.append((self.number(ctx, exp), target))
        return pairs

    def gather_blocks(self, blocks):
        got = [
            lax.ppermute(
                lax.dynamic_index_in_dim(blocks, (turn + self.ctx) % 2, 0, keepdims=False),
                BOTH,
                self.round_pairs(turn),
            )
            for turn in range(2)
        ]
        first = jnp.where(self.side == 0, got[0], got[1])
        second = jnp.where(self.side == 0, got[1], got[0])
        return jnp.concatenate([first, second], axis=0)

    def return_blocks(self, rows):
        blocks = rows.reshape((2, rows.shape[0] // 2) + rows.shape[1:])
        got = [
            lax.ppermute(
                lax.dynamic_index_in_dim(blocks, (turn + self.side) % 2, 0, keepdims=False),
                BOTH,
                [(target, source) for source, target in self.round_pairs(turn)],
            )
            for turn in range(2)
        ]
        even = self.ctx % 2 == 0
        return jnp.stack([jnp.where(even, got[0], got[1]), jnp.where(even, got[1], got[0])])

    def all_rows(self, rows):
        return jnp.concatenate(
            [rows]
            + [lax.ppermute(rows, BOTH, self.member_pairs(shift)) for shift in range(1, self.members)],
            axis=0,
        )

    def sum_rows(self, partial):
        parts = partial.reshape((self.members, partial.shape[0] // self.members) + partial.shape[1:])
        total = parts[0]
        for shift in range(1, self.members):
            moved = lax.ppermute(
                parts[shift].astype(jnp.bfloat16), BOTH, self.member_pairs(self.members - shift)
            )
            total = total + moved.astype(jnp.float32)
        return total

    def bases(self, row_count):
        return jnp.stack(
            [(self.member - shift) % self.members * row_count for shift in range(self.members)]
        ).astype(jnp.int32)

    def swap(self, rows, distance):
        pairs = [(ctx, ctx ^ distance) for ctx in range(self.ctx_count)]
        return lax.ppermute(rows, "ctx", pairs)


def per_device(
    tokens_in,
    first_gain,
    joint_projection,
    out_projection,
    bias_table,
    second_gain,
    router_weight,
    expert_up,
    expert_down,
    expert_index,
    keep_mask,
    buckets,
    cotangent,
):
    layout = Layout()
    shards = layout.exp_count
    seq_count, block_len, model_width = tokens_in.shape
    token_count = seq_count * block_len
    expert_count = router_weight.shape[1]
    bucket_count = bias_table.shape[0] * shards
    head_count = bias_table.shape[1]

    small = [first_gain, second_gain, router_weight, bias_table]
    small_sizes = [part.size for part in small]
    small_full = lax.all_gather(
        jnp.concatenate([part.reshape(-1) for part in small]), "exp", axis=0, tiled=False
    )
    small_cuts = [sum(small_sizes[:place]) for place in range(1, len(small))]
    gain_one, gain_two, weight_router, table = jnp.split(small_full, small_cuts, axis=1)
    weight_router = weight_router.reshape(model_width, expert_count)
    table = table.reshape(bucket_count, head_count)
    gain_first = gain_one.reshape(model_width).astype(jnp.float32)
    gain_second = gain_two.reshape(model_width).astype(jnp.float32)
    weight_joint = lax.all_gather(joint_projection, "exp", axis=0, tiled=True)
    weight_out = lax.all_gather(out_projection, "exp", axis=0, tiled=True)

    tokens = layout.gather_blocks(tokens_in)
    every_token = layout.all_rows(tokens)
    codes = layout.gather_blocks(expert_index.reshape(seq_count, block_len) * 2 + keep_mask)
    grad_out_low = layout.gather_blocks(cotangent)
    chosen = codes // 2
    kept = codes % 2

    held_up, held_down, _ = lax.optimization_barrier((expert_up[0], expert_down[0], every_token))
    distances = range(0, layout.ctx_count, 2)
    ups = [held_up if step == 0 else layout.swap(held_up, step) for step in distances]
    downs = [held_down if step == 0 else layout.swap(held_down, step) for step in distances]

    offset_count = buckets.shape[0]
    bucket_hot = buckets[None, :] == jnp.arange(bucket_count, dtype=jnp.int32)[:, None]
    offset_values = lax.dot_general(
        table,
        bucket_hot.astype(jnp.bfloat16),
        (((0,), (0,)), ((), ())),
        preferred_element_type=jnp.float32,
    )
    skew = make_skew(jnp.pad(offset_values, ((0, 0), (0, 1))))

    every_float = every_token.astype(jnp.float32)
    tokens_f = every_float[:token_count]
    normed_one, every_inverse = rms_forward(every_float, gain_first)
    inverse_one = every_inverse[:token_count]
    hidden_one = normed_one.astype(jnp.bfloat16)
    queries = jnp.dot(
        hidden_one[:token_count], weight_joint[:, :model_width], preferred_element_type=jnp.float32
    ).astype(jnp.bfloat16) * jnp.bfloat16(SCORE_SCALE)
    key_values = jnp.dot(
        hidden_one, weight_joint[:, model_width:], preferred_element_type=jnp.float32
    ).astype(jnp.bfloat16)
    bases = layout.bases(token_count)
    attended, logsum = attend_forward(bases, queries, key_values, skew)
    attended_low = attended.astype(jnp.bfloat16)
    residual = tokens_f + jnp.dot(attended_low, weight_out, preferred_element_type=jnp.float32)
    normed_two, inverse_two = rms_forward(residual, gain_second)
    hidden_two = normed_two.astype(jnp.bfloat16)

    logits = jnp.dot(hidden_two, weight_router, preferred_element_type=jnp.float32)
    router_prob = jax.nn.softmax(logits, axis=-1)
    is_choice = chosen[:, None] == jnp.arange(expert_count, dtype=jnp.int32)
    choice_hot = is_choice.astype(jnp.float32)
    picked = jnp.sum(router_prob * choice_hot, axis=-1)
    gate_value = kept.astype(jnp.float32) * picked
    most_rows = max(2, (5 * block_len + 4 * expert_count - 1) // (4 * expert_count))
    capacity = seq_count * most_rows
    place = jnp.arange(token_count, dtype=jnp.int32)
    earlier = (place[:, None] >= place[None, :]) & (
        place[:, None] // block_len == place[None, :] // block_len
    )
    running = jnp.dot(
        earlier.astype(jnp.bfloat16),
        is_choice.astype(jnp.bfloat16),
        preferred_element_type=jnp.float32,
    )
    slot_rank = (jnp.sum(running * choice_hot, axis=-1) - 1.0).astype(jnp.int32)
    token_slot = chosen * capacity + place // block_len * most_rows + slot_rank
    slot_hot = (
        (token_slot[:, None] == jnp.arange(expert_count * capacity, dtype=jnp.int32))
        & (kept[:, None] > 0)
    ).astype(jnp.bfloat16)

    def to_experts(row_data):
        sent = lax.dot_general(
            slot_hot, row_data, (((0,), (0,)), ((), ())), preferred_element_type=jnp.float32
        ).astype(jnp.bfloat16)
        arrived = lax.all_to_all(
            sent.reshape(shards, -1, model_width), "exp", split_axis=0, concat_axis=0, tiled=True
        ).reshape(-1, model_width)
        return jnp.concatenate([arrived, layout.swap(arrived, 1)], axis=0)

    def from_experts(partial):
        own_count = partial.shape[0] // 2
        other = layout.swap(partial[own_count:].astype(jnp.bfloat16), 1)
        summed = (partial[:own_count] + other.astype(jnp.float32)).astype(jnp.bfloat16)
        returned = lax.all_to_all(
            summed.reshape(shards, -1, model_width), "exp", split_axis=0, concat_axis=0, tiled=True
        )
        return jnp.dot(
            slot_hot, returned.reshape(-1, model_width), preferred_element_type=jnp.float32
        )

    rows_in = to_experts(hidden_two)
    grad_top = grad_out_low.astype(jnp.float32)
    grad_result = to_experts((gate_value[:, None] * grad_top).astype(jnp.bfloat16))

    acted, gelu_backs = [], []
    produced = 0.0
    for matrix_up, matrix_down in zip(ups, downs):
        before = jnp.dot(rows_in, matrix_up, preferred_element_type=jnp.float32)
        activated, gelu_back = jax.vjp(jax.nn.gelu, before)
        acted.append(activated.astype(jnp.bfloat16))
        gelu_backs.append(gelu_back)
        produced = produced + jnp.dot(acted[-1], matrix_down, preferred_element_type=jnp.float32)
    expert_rows = from_experts(produced)

    grad_inputs = 0.0
    grad_ups, grad_downs = [], []
    for part, (matrix_up, matrix_down) in enumerate(zip(ups, downs)):
        grad_acted = lax.dot_general(
            grad_result, matrix_down, (((1,), (1,)), ((), ())), preferred_element_type=jnp.float32
        )
        grad_before = gelu_backs[part](grad_acted)[0].astype(jnp.bfloat16)
        grad_inputs = grad_inputs + lax.dot_general(
            grad_before, matrix_up, (((1,), (1,)), ((), ())), preferred_element_type=jnp.float32
        )
        grad_ups.append(
            lax.dot_general(
                rows_in, grad_before, (((0,), (0,)), ((), ())), preferred_element_type=jnp.float32
            )
        )
        grad_downs.append(
            lax.dot_general(
                acted[part], grad_result, (((0,), (0,)), ((), ())), preferred_element_type=jnp.float32
            )
        )
    grad_back = from_experts(grad_inputs)

    def own_slice(parts):
        total = parts[0]
        for part, step in zip(parts[1:], list(distances)[1:]):
            total = total + layout.swap(part.astype(jnp.bfloat16), step).astype(jnp.float32)
        return total[None]

    grad_expert_up = own_slice(grad_ups)
    grad_expert_down = own_slice(grad_downs)

    combined = residual + gate_value[:, None] * expert_rows
    layer_out = layout.return_blocks(combined.astype(jnp.bfloat16))

    grad_picked = jnp.sum(grad_top * expert_rows, axis=-1)
    grad_logits = (picked[:, None] * (choice_hot - router_prob) * grad_picked[:, None]).astype(
        jnp.bfloat16
    )
    grad_router = lax.dot_general(
        hidden_two, grad_logits, (((0,), (0,)), ((), ())), preferred_element_type=jnp.float32
    )
    grad_hidden_two = grad_back + lax.dot_general(
        grad_logits, weight_router, (((1,), (1,)), ((), ())), preferred_element_type=jnp.float32
    )
    grad_residual, grad_gain_two = rms_backward(residual, inverse_two, gain_second, grad_hidden_two)
    grad_residual = grad_residual + grad_top
    grad_mixed = grad_residual.astype(jnp.bfloat16)
    grad_weight_out = lax.dot_general(
        attended_low, grad_mixed, (((0,), (0,)), ((), ())), preferred_element_type=jnp.float32
    )
    grad_attended = lax.dot_general(
        grad_mixed, weight_out, (((1,), (1,)), ((), ())), preferred_element_type=jnp.float32
    ).astype(jnp.bfloat16)
    grad_q, grad_k, grad_v, grad_off = attend_backward(
        bases, queries, grad_attended, attended, key_values, skew, logsum
    )

    def back_through(grad_part, first_column):
        return lax.dot_general(
            grad_part,
            weight_joint[:, first_column : first_column + model_width],
            (((1,), (1,)), ((), ())),
            preferred_element_type=jnp.float32,
        )

    grad_hidden_one = layout.sum_rows(
        back_through(grad_k, model_width) + back_through(grad_v, 2 * model_width)
    ) + back_through(grad_q, 0)
    grad_input_norm, grad_gain_one = rms_backward(
        tokens_f, inverse_one, gain_first, grad_hidden_one
    )
    grad_tokens = layout.return_blocks((grad_input_norm + grad_residual).astype(jnp.bfloat16)).astype(
        jnp.float32
    )
    joint_parts = [
        lax.dot_general(
            hidden_one[: part.shape[0]], part, (((0,), (0,)), ((), ())), preferred_element_type=jnp.float32
        ).astype(jnp.bfloat16)
        for part in (grad_q, grad_k, grad_v)
    ]
    grad_table = jnp.dot(
        bucket_hot.astype(jnp.float32),
        grad_off.reshape(head_count, -1)[:, :offset_count].T,
        precision=HIGHEST,
    )

    def scatter(part):
        return lax.psum_scatter(part.astype(jnp.bfloat16), "exp", scatter_dimension=0, tiled=True)

    small_grads = [grad_gain_one, grad_gain_two, grad_router, grad_table]
    small_sum = scatter(
        jnp.concatenate([part.reshape(shards, -1) for part in small_grads], axis=1)
    )
    out_sum = scatter(grad_weight_out)
    joint_sum = scatter(jnp.concatenate(joint_parts, axis=1))
    small_sum, out_sum, joint_sum = lax.psum((small_sum, out_sum, joint_sum), "ctx")
    small_sum = small_sum[0].astype(jnp.float32)
    sum_gain_one, sum_gain_two, sum_router, sum_table = jnp.split(small_sum, small_cuts)
    return (
        layer_out,
        grad_tokens,
        sum_gain_one,
        joint_sum.astype(jnp.float32),
        out_sum.astype(jnp.float32),
        sum_table.reshape(bias_table.shape),
        sum_gain_two,
        sum_router.reshape(router_weight.shape),
        grad_expert_up,
        grad_expert_down,
    )


def solution(mesh):
    in_specs = (
        P("exp", "ctx", None),
        P("exp"),
        P("exp", None),
        P("exp", None),
        P("exp", None),
        P("exp"),
        P("exp", None),
        P("exp", None, "ctx"),
        P("exp", "ctx", None),
        P("exp", "ctx", None),
        P("exp", "ctx"),
        P(),
        P("exp", "ctx", None),
    )
    out_specs = (
        P("exp", "ctx", None),
        P("exp", "ctx", None),
        P("exp"),
        P("exp", None),
        P("exp", None),
        P("exp", None),
        P("exp"),
        P("exp", None),
        P("exp", None, "ctx"),
        P("exp", "ctx", None),
    )
    return jax.shard_map(
        per_device, mesh=mesh, in_specs=in_specs, out_specs=out_specs, check_vma=False
    )
```

```python
import functools

import jax
import jax.numpy as jnp
from jax import lax
from jax.experimental import pallas as pl
from jax.experimental.pallas import tpu as pltpu
from jax.sharding import PartitionSpec as P

EPSILON = 1e-06
HALF = 64
TILE = 128
GROUP = 256
VMEM_BYTES = 50 * 1024 * 1024
SCORE_SCALE = 0.125
HIGHEST = lax.Precision.HIGHEST
BOTH = ("ctx", "exp")


def contract_last(left, right):
    return lax.dot_general(
        left, right, (((1,), (1,)), ((), ())), preferred_element_type=jnp.float32
    )


def matmul(left, right):
    return lax.dot_general(
        left, right, (((1,), (0,)), ((), ())), preferred_element_type=jnp.float32
    )


def skew_kernel(offset_ref, skew_ref):
    padded = offset_ref.shape[-1]
    kept = skew_ref.shape[1]
    rows = jnp.broadcast_to(offset_ref[0], (TILE, padded))
    rolled = pltpu.roll(rows, padded - (TILE - 1), 1, stride=1, stride_axis=0)
    skew_ref[0] = rolled[:, :kept].T.astype(skew_ref.dtype)


def make_skew(offset_values):
    head_count, padded = offset_values.shape
    kept = padded - TILE
    return pl.pallas_call(
        skew_kernel,
        grid=(head_count,),
        in_specs=[pl.BlockSpec((1, 1, padded), lambda h: (h, 0, 0))],
        out_specs=pl.BlockSpec((1, kept, TILE), lambda h: (h, 0, 0)),
        out_shape=jax.ShapeDtypeStruct((head_count, kept, TILE), jnp.bfloat16),
        compiler_params=pltpu.CompilerParams(vmem_limit_bytes=VMEM_BYTES),
        name="skew_bias",
    )(offset_values.reshape(head_count, 1, padded))


def half_mask(rows, half):
    lanes = lax.broadcasted_iota(jnp.int32, (rows, TILE), 1)
    return (lanes // HALF) == half


def bias_rows(key_base, query_base, seq_len):
    return key_base - query_base + seq_len - TILE


def forward_kernel(
    base_ref, q_ref, k_ref, v_ref, skew_ref, out_ref, lse_ref, score_ref, prob_ref, *, chunk
):
    query_rows = q_ref.shape[0]
    key_rows = k_ref.shape[0]
    seq_len = key_rows
    mask = [half_mask(GROUP, 0), half_mask(GROUP, 1)]
    value_t = v_ref[...].T
    for group in range(query_rows // GROUP):
        rows = slice(group * GROUP, (group + 1) * GROUP)
        query_base = base_ref[0] + group * GROUP
        halves = []
        for half in range(2):
            queries = jnp.where(mask[half], q_ref[rows], 0).astype(jnp.bfloat16)
            score_ref[half] = contract_last(k_ref[...], queries)
            top = jnp.full((8, GROUP), -jnp.inf, jnp.float32)
            for start in range(0, key_rows, chunk):
                key_base = base_ref[start // query_rows] + start % query_rows
                place = pl.multiple_of(bias_rows(key_base, query_base, seq_len), TILE)
                left = skew_ref[half, pl.ds(place, chunk), :]
                right = skew_ref[half, pl.ds(place - TILE, chunk), :]
                bias = jnp.concatenate([left, right], axis=1).astype(jnp.float32)
                piece = score_ref[half, start : start + chunk] + bias
                score_ref[half, start : start + chunk] = piece
                top = jnp.maximum(top, jnp.max(piece.reshape(chunk // 8, 8, GROUP), axis=0))
            top = jnp.max(top, axis=0, keepdims=True)
            total = jnp.zeros((8, GROUP), jnp.float32)
            for start in range(0, key_rows, chunk):
                piece = jnp.exp(score_ref[half, start : start + chunk] - top)
                total = total + jnp.sum(piece.reshape(chunk // 8, 8, GROUP), axis=0)
                prob_ref[half, start : start + chunk] = piece.astype(jnp.bfloat16)
            total = jnp.sum(total, axis=0, keepdims=True)
            lse_ref[0, half : half + 1, rows] = top + jnp.log(total)
            mixed = matmul(value_t[half * HALF : (half + 1) * HALF], prob_ref[half])
            halves.append(mixed / total)
        out_ref[rows] = jnp.concatenate(halves, axis=0).T


def attend_forward(bases, queries, key_values, skew):
    query_rows, width = queries.shape
    key_rows = key_values.shape[0]
    kept = skew.shape[1]
    pairs = width // TILE
    chunk = TILE
    return pl.pallas_call(
        functools.partial(forward_kernel, chunk=chunk),
        grid_spec=pltpu.PrefetchScalarGridSpec(
            num_scalar_prefetch=1,
            grid=(pairs,),
            in_specs=[
                pl.BlockSpec((query_rows, TILE), lambda p, _: (0, p)),
                pl.BlockSpec((key_rows, TILE), lambda p, _: (0, p)),
                pl.BlockSpec((key_rows, TILE), lambda p, _: (0, p + pairs)),
                pl.BlockSpec((2, kept, TILE), lambda p, _: (p, 0, 0)),
            ],
            out_specs=[
                pl.BlockSpec((query_rows, TILE), lambda p, _: (0, p)),
                pl.BlockSpec((1, 2, query_rows), lambda p, _: (p, 0, 0)),
            ],
            scratch_shapes=[
                pltpu.VMEM((2, key_rows, GROUP), jnp.float32),
                pltpu.VMEM((2, key_rows, GROUP), jnp.bfloat16),
            ],
        ),
        out_shape=[
            jax.ShapeDtypeStruct((query_rows, width), jnp.float32),
            jax.ShapeDtypeStruct((pairs, 2, query_rows), jnp.float32),
        ],
        compiler_params=pltpu.CompilerParams(vmem_limit_bytes=VMEM_BYTES),
        name="attend_forward",
    )(bases, queries, key_values, key_values, skew)


def backward_kernel(
    base_ref, q_ref, do_ref, o_ref, k_ref, v_ref, skew_ref, lse_ref,
    dq_ref, dk_ref, dv_ref, off_ref,
    score_ref, gradp_ref, prob_ref, grads_ref, accum_k, accum_v, accum_skew,
    *, chunk,
):
    query_rows = q_ref.shape[0]
    key_rows = k_ref.shape[0]
    seq_len = key_rows
    mask = [half_mask(GROUP, 0), half_mask(GROUP, 1)]
    key_t = k_ref[...].T
    accum_skew[...] = jnp.zeros_like(accum_skew)
    for group in range(query_rows // GROUP):
        rows = slice(group * GROUP, (group + 1) * GROUP)
        query_base = base_ref[0] + group * GROUP
        product = (do_ref[rows].astype(jnp.float32) * o_ref[rows]).T
        halves = []
        sum_k = None
        for half in range(2):
            queries = jnp.where(mask[half], q_ref[rows], 0).astype(jnp.bfloat16)
            grads_out = jnp.where(mask[half], do_ref[rows], 0).astype(jnp.bfloat16)
            score_ref[half] = contract_last(k_ref[...], queries)
            gradp_ref[half] = contract_last(v_ref[...], grads_out)
            logsum = lse_ref[0, half : half + 1, rows]
            delta = jnp.sum(product[half * HALF : (half + 1) * HALF], axis=0, keepdims=True)
            for start in range(0, key_rows, chunk):
                key_base = base_ref[start // query_rows] + start % query_rows
                place = pl.multiple_of(bias_rows(key_base, query_base, seq_len), TILE)
                here = pl.ds(start, chunk)
                left = skew_ref[half, pl.ds(place, chunk), :]
                right = skew_ref[half, pl.ds(place - TILE, chunk), :]
                bias = jnp.concatenate([left, right], axis=1).astype(jnp.float32)
                prob = jnp.exp(score_ref[half, here] + bias - logsum)
                grads = prob * (gradp_ref[half, here] - delta)
                prob_ref[half, here] = prob.astype(jnp.bfloat16)
                grads_ref[half, here] = grads.astype(jnp.bfloat16)
                accum_skew[half, pl.ds(place, chunk), :] += grads[:, :TILE]
                accum_skew[half, pl.ds(place - TILE, chunk), :] += grads[:, TILE:]
            part_k = matmul(grads_ref[half], queries)
            part_v = matmul(prob_ref[half], grads_out)
            sum_k = part_k if sum_k is None else sum_k + part_k
            sum_v = part_v if half == 0 else sum_v + part_v
            halves.append(matmul(key_t[half * HALF : (half + 1) * HALF], grads_ref[half]))
        if group == 0:
            accum_k[...] = sum_k
            accum_v[...] = sum_v
        else:
            accum_k[...] += sum_k
            accum_v[...] += sum_v
        dq_ref[rows] = (jnp.concatenate(halves, axis=0) * 0.125).T.astype(dq_ref.dtype)
    dk_ref[...] = accum_k[...].astype(dk_ref.dtype)
    dv_ref[...] = accum_v[...].astype(dv_ref.dtype)
    for half in range(2):
        turned = accum_skew[half].T
        padded = turned.shape[1]
        count = TILE // 2
        while count:
            turned = turned[:count] + pltpu.roll(turned[count : 2 * count], padded - count, 1)
            count //= 2
        off_ref[0, half : half + 1] = pltpu.roll(turned, TILE - 1, 1)


def attend_backward(bases, queries, grads_out, outputs, key_values, skew, logsum):
    query_rows, width = queries.shape
    key_rows = key_values.shape[0]
    kept = skew.shape[1]
    pairs = width // TILE
    chunk = TILE
    column = lambda count: pl.BlockSpec((count, TILE), lambda p, _: (0, p))
    return pl.pallas_call(
        functools.partial(backward_kernel, chunk=chunk),
        grid_spec=pltpu.PrefetchScalarGridSpec(
            num_scalar_prefetch=1,
            grid=(pairs,),
            in_specs=[
                column(query_rows), column(query_rows), column(query_rows),
                column(key_rows),
                pl.BlockSpec((key_rows, TILE), lambda p, _: (0, p + pairs)),
                pl.BlockSpec((2, kept, TILE), lambda p, _: (p, 0, 0)),
                pl.BlockSpec((1, 2, query_rows), lambda p, _: (p, 0, 0)),
            ],
            out_specs=[
                column(query_rows), column(key_rows), column(key_rows),
                pl.BlockSpec((1, 2, kept + TILE), lambda p, _: (p, 0, 0)),
            ],
            scratch_shapes=[
                pltpu.VMEM((2, key_rows, GROUP), jnp.float32),
                pltpu.VMEM((2, key_rows, GROUP), jnp.float32),
                pltpu.VMEM((2, key_rows, GROUP), jnp.bfloat16),
                pltpu.VMEM((2, key_rows, GROUP), jnp.bfloat16),
                pltpu.VMEM((key_rows, TILE), jnp.float32),
                pltpu.VMEM((key_rows, TILE), jnp.float32),
                pltpu.VMEM((2, kept + TILE, TILE), jnp.float32),
            ],
        ),
        out_shape=[
            jax.ShapeDtypeStruct((query_rows, width), jnp.bfloat16),
            jax.ShapeDtypeStruct((key_rows, width), jnp.bfloat16),
            jax.ShapeDtypeStruct((key_rows, width), jnp.bfloat16),
            jax.ShapeDtypeStruct((pairs, 2, kept + TILE), jnp.float32),
        ],
        compiler_params=pltpu.CompilerParams(vmem_limit_bytes=VMEM_BYTES),
        name="attend_backward",
    )(bases, queries, grads_out, outputs, key_values, key_values, skew, logsum)


def rms_forward(row_data, gain_vec):
    inverse = lax.rsqrt(jnp.mean(row_data * row_data, axis=-1, keepdims=True) + EPSILON)
    return (row_data * inverse * gain_vec, inverse)


def rms_backward(row_data, inverse, gain_vec, grad_out):
    normed = row_data * inverse
    grad_gain = jnp.sum(grad_out * normed, axis=0)
    scaled = grad_out * gain_vec
    spread = jnp.mean(scaled * normed, axis=-1, keepdims=True)
    return (inverse * (scaled - normed * spread), grad_gain)


class Layout:
    def __init__(self):
        self.ctx_count = lax.axis_size("ctx")
        self.exp_count = lax.axis_size("exp")
        self.span = self.ctx_count // 4
        self.members = 2 * self.span
        self.ctx = lax.axis_index("ctx")
        self.core = lax.axis_index("exp") % 2
        self.member = (self.ctx % self.span) * 2 + self.core
        self.side = (self.ctx // self.span) % 2

    def number(self, ctx, exp):
        return ctx * self.exp_count + exp

    def round_pairs(self, turn):
        pairs = []
        for ctx in range(self.ctx_count):
            for exp in range(self.exp_count):
                seq = 2 * (exp % 2) + (turn + ctx) % 2
                member = ctx // 2
                target = self.number(seq * self.span + member // 2, exp // 2 * 2 + member % 2)
                pairs.append((self.number(ctx, exp), target))
        return pairs

    def member_pairs(self, shift):
        pairs = []
        for ctx in range(self.ctx_count):
            for exp in range(self.exp_count):
                start = ctx // self.span * self.span
                member = ((ctx - start) * 2 + exp % 2 + shift) % self.members
                target = self.number(start + member // 2, exp // 2 * 2 + member % 2)
                pairs.append((self.number(ctx, exp), target))
        return pairs

    def gather_blocks(self, blocks):
        got = [
            lax.ppermute(
                lax.dynamic_index_in_dim(blocks, (turn + self.ctx) % 2, 0, keepdims=False),
                BOTH,
                self.round_pairs(turn),
            )
            for turn in range(2)
        ]
        first = jnp.where(self.side == 0, got[0], got[1])
        second = jnp.where(self.side == 0, got[1], got[0])
        return jnp.concatenate([first, second], axis=0)

    def return_blocks(self, rows):
        blocks = rows.reshape((2, rows.shape[0] // 2) + rows.shape[1:])
        got = [
            lax.ppermute(
                lax.dynamic_index_in_dim(blocks, (turn + self.side) % 2, 0, keepdims=False),
                BOTH,
                [(target, source) for source, target in self.round_pairs(turn)],
            )
            for turn in range(2)
        ]
        even = self.ctx % 2 == 0
        return jnp.stack([jnp.where(even, got[0], got[1]), jnp.where(even, got[1], got[0])])

    def all_rows(self, rows):
        return jnp.concatenate(
            [rows]
            + [lax.ppermute(rows, BOTH, self.member_pairs(shift)) for shift in range(1, self.members)],
            axis=0,
        )

    def sum_rows(self, partial):
        parts = partial.reshape((self.members, partial.shape[0] // self.members) + partial.shape[1:])
        total = parts[0]
        for shift in range(1, self.members):
            moved = lax.ppermute(
                parts[shift].astype(jnp.bfloat16), BOTH, self.member_pairs(self.members - shift)
            )
            total = total + moved.astype(jnp.float32)
        return total

    def bases(self, row_count):
        return jnp.stack(
            [(self.member - shift) % self.members * row_count for shift in range(self.members)]
        ).astype(jnp.int32)

    def swap(self, rows, distance, axis="ctx"):
        pairs = [(place, place ^ distance) for place in range(lax.axis_size(axis))]
        return lax.ppermute(rows, axis, pairs)

    def gather_small(self, part):
        held = part[None]
        place = lax.axis_index("exp")
        distance = 1
        while distance < self.exp_count:
            other = self.swap(held, distance, "exp")
            upper = (place // distance) % 2 == 1
            held = jnp.where(
                upper,
                jnp.concatenate([other, held], axis=0),
                jnp.concatenate([held, other], axis=0),
            )
            distance *= 2
        return held

    def reduce_dense(self, part):
        rows = part.shape[0] // self.exp_count
        pair_count = self.exp_count // 2
        blocks = part.reshape(pair_count, 2, rows, part.shape[1])
        sent = lax.dynamic_index_in_dim(blocks, 1 - self.core, 1, keepdims=False)
        kept = lax.dynamic_index_in_dim(blocks, self.core, 1, keepdims=False)
        both = add_low([kept, self.swap(sent, 1, "exp")])
        pair = lax.axis_index("exp") // 2
        parts = [lax.dynamic_index_in_dim(both, pair, 0, keepdims=False)]
        for step in range(1, pair_count):
            block = lax.dynamic_index_in_dim(both, pair ^ step, 0, keepdims=False)
            parts.append(self.swap(block, 2 * step, "exp"))
        total = add_low(parts)
        cuts = total.reshape(self.ctx_count, rows // self.ctx_count, part.shape[1])
        parts = [lax.dynamic_index_in_dim(cuts, self.ctx, 0, keepdims=False)]
        for step in range(1, self.ctx_count):
            block = lax.dynamic_index_in_dim(cuts, self.ctx ^ step, 0, keepdims=False)
            parts.append(self.swap(block, step))
        own = add_low(parts)
        every = jnp.stack([own] + [self.swap(own, step) for step in range(1, self.ctx_count)])
        return jnp.concatenate(
            [
                lax.dynamic_index_in_dim(every, self.ctx ^ place, 0, keepdims=False)
                for place in range(self.ctx_count)
            ],
            axis=0,
        )


def add_low(parts):
    total = parts[0].astype(jnp.float32)
    for part in parts[1:]:
        total = total + part.astype(jnp.float32)
    return total.astype(jnp.bfloat16)


def after(value, *events):
    return lax.optimization_barrier((value,) + events)[0]


def per_device(
    tokens_in,
    first_gain,
    joint_projection,
    out_projection,
    bias_table,
    second_gain,
    router_weight,
    expert_up,
    expert_down,
    expert_index,
    keep_mask,
    buckets,
    cotangent,
):
    layout = Layout()
    shards = layout.exp_count
    seq_count, block_len, model_width = tokens_in.shape
    token_count = seq_count * block_len
    expert_count = router_weight.shape[1]
    bucket_count = bias_table.shape[0] * shards
    head_count = bias_table.shape[1]

    small = [first_gain, second_gain, router_weight, bias_table]
    small_sizes = [part.size for part in small]
    small_cuts = [sum(small_sizes[:place]) for place in range(1, len(small))]
    small_count = sum(small_sizes)
    small_padded = -(-small_count // TILE) * TILE
    small_full = layout.gather_small(
        jnp.pad(
            jnp.concatenate([part.reshape(-1) for part in small]), (0, small_padded - small_count)
        )
    )[:, :small_count]
    gain_one, gain_two, weight_router, table = jnp.split(small_full, small_cuts, axis=1)
    weight_router = weight_router.reshape(model_width, expert_count)
    table = table.reshape(bucket_count, head_count)
    gain_first = gain_one.reshape(model_width).astype(jnp.float32)
    gain_second = gain_two.reshape(model_width).astype(jnp.float32)
    weight_joint = lax.all_gather(joint_projection, "exp", axis=0, tiled=True)
    weight_out = lax.all_gather(out_projection, "exp", axis=0, tiled=True)

    tokens = layout.gather_blocks(tokens_in)
    codes = layout.gather_blocks(expert_index.reshape(seq_count, block_len) * 2 + keep_mask)
    grad_out_low = layout.gather_blocks(cotangent)
    every_token = layout.all_rows(tokens)
    chosen = codes // 2
    kept = codes % 2

    distances = list(range(2, layout.ctx_count, 2))
    half_width = model_width // 2

    def remote_pieces(piece, event):
        held = after(piece, event)
        return [layout.swap(held, step) for step in distances]

    up_first = remote_pieces(expert_up[0, :half_width], tokens)
    up_second = remote_pieces(expert_up[0, half_width:], up_first[-1])
    down_first = remote_pieces(expert_down[0, :, :half_width], up_second[-1])
    down_second = remote_pieces(expert_down[0, :, half_width:], down_first[-1])

    offset_count = buckets.shape[0]
    bucket_hot = buckets[None, :] == jnp.arange(bucket_count, dtype=jnp.int32)[:, None]
    offset_values = lax.dot_general(
        table,
        bucket_hot.astype(jnp.bfloat16),
        (((0,), (0,)), ((), ())),
        preferred_element_type=jnp.float32,
    )
    skew = make_skew(jnp.pad(offset_values, ((0, 0), (0, 1))))

    is_choice = chosen[:, None] == jnp.arange(expert_count, dtype=jnp.int32)
    most_rows = max(2, (5 * block_len + 4 * expert_count - 1) // (4 * expert_count))
    capacity = seq_count * most_rows
    place = jnp.arange(token_count, dtype=jnp.int32)
    earlier = (place[:, None] >= place[None, :]) & (
        place[:, None] // block_len == place[None, :] // block_len
    )
    running = jnp.dot(
        earlier.astype(jnp.bfloat16),
        is_choice.astype(jnp.bfloat16),
        preferred_element_type=jnp.float32,
    )
    slot_rank = (jnp.sum(running * is_choice.astype(jnp.float32), axis=-1) - 1.0).astype(jnp.int32)
    token_slot = chosen * capacity + place // block_len * most_rows + slot_rank
    slot_hot = (
        (token_slot[:, None] == jnp.arange(expert_count * capacity, dtype=jnp.int32))
        & (kept[:, None] > 0)
    ).astype(jnp.bfloat16)

    def exchange(row_data):
        return lax.all_to_all(
            row_data.reshape(shards, -1, model_width), "exp", split_axis=0, concat_axis=0, tiled=True
        ).reshape(-1, model_width)

    def to_experts(row_data):
        sent = lax.dot_general(
            slot_hot, row_data, (((0,), (0,)), ((), ())), preferred_element_type=jnp.float32
        ).astype(jnp.bfloat16)
        return exchange(sent)

    def from_experts(own_part, other_part):
        other = layout.swap(other_part.astype(jnp.bfloat16), 1)
        summed = (own_part + other.astype(jnp.float32)).astype(jnp.bfloat16)
        return jnp.dot(slot_hot, exchange(summed), preferred_element_type=jnp.float32)

    grad_own = to_experts(grad_out_low)
    grad_other = layout.swap(grad_own, 1)

    every_float = every_token.astype(jnp.float32)
    tokens_f = every_float[:token_count]
    normed_one, every_inverse = rms_forward(every_float, gain_first)
    inverse_one = every_inverse[:token_count]
    hidden_one = after(normed_one.astype(jnp.bfloat16), grad_out_low)
    queries = jnp.dot(
        hidden_one[:token_count], weight_joint[:, :model_width], preferred_element_type=jnp.float32
    ).astype(jnp.bfloat16) * jnp.bfloat16(SCORE_SCALE)
    key_values = jnp.dot(
        hidden_one, weight_joint[:, model_width:], preferred_element_type=jnp.float32
    ).astype(jnp.bfloat16)
    queries = after(queries, *up_first)
    bases = layout.bases(token_count)
    attended, logsum = attend_forward(bases, queries, key_values, skew)
    attended = after(attended, grad_own, *up_second)
    attended_low = attended.astype(jnp.bfloat16)
    residual = tokens_f + jnp.dot(attended_low, weight_out, preferred_element_type=jnp.float32)
    normed_two, inverse_two = rms_forward(residual, gain_second)
    hidden_two = normed_two.astype(jnp.bfloat16)

    row_own = after(to_experts(hidden_two), grad_other, *down_first)
    row_other = layout.swap(row_own, 1)
    ups = [expert_up[0]] + [
        jnp.concatenate(pieces, axis=0) for pieces in zip(up_first, up_second)
    ]
    downs = [expert_down[0]] + [
        jnp.concatenate(pieces, axis=1) for pieces in zip(down_first, down_second)
    ]

    expert_here = jnp.arange(expert_count, dtype=jnp.int32) == lax.axis_index("exp")
    expert_here = expert_here.astype(jnp.float32)[None, :]

    def contract_rows(left, right):
        return lax.dot_general(
            left, right, (((0,), (0,)), ((), ())), preferred_element_type=jnp.float32
        )

    results, grad_inputs = [], []
    grad_router = 0.0
    grad_ups, grad_downs = [0.0] * len(ups), [0.0] * len(ups)
    for rows, grad_rows in ((row_own, grad_own), (row_other, grad_other)):
        logits = jnp.dot(rows, weight_router, preferred_element_type=jnp.float32)
        router_prob = jax.nn.softmax(logits, axis=-1)
        picked = jnp.sum(router_prob * expert_here, axis=-1, keepdims=True)
        grad_float = grad_rows.astype(jnp.float32)
        grad_result = (picked * grad_float).astype(jnp.bfloat16)
        produced, grad_input = 0.0, 0.0
        for part, (matrix_up, matrix_down) in enumerate(zip(ups, downs)):
            before = jnp.dot(rows, matrix_up, preferred_element_type=jnp.float32)
            activated, gelu_back = jax.vjp(jax.nn.gelu, before)
            acted = activated.astype(jnp.bfloat16)
            produced = produced + jnp.dot(acted, matrix_down, preferred_element_type=jnp.float32)
            grad_acted = contract_last(grad_result, matrix_down)
            grad_before = gelu_back(grad_acted)[0].astype(jnp.bfloat16)
            grad_input = grad_input + contract_last(grad_before, matrix_up)
            grad_ups[part] = grad_ups[part] + contract_rows(rows, grad_before)
            grad_downs[part] = grad_downs[part] + contract_rows(acted, grad_result)
        grad_picked = jnp.sum(grad_float * produced, axis=-1, keepdims=True)
        grad_logits = (picked * (expert_here - router_prob) * grad_picked).astype(jnp.bfloat16)
        grad_router = grad_router + contract_rows(rows, grad_logits)
        grad_inputs.append(grad_input + contract_last(grad_logits, weight_router))
        results.append(picked * produced)

    grad_back = from_experts(*grad_inputs)
    layer_rows = residual + from_experts(*results)
    layer_out = layout.return_blocks(layer_rows.astype(jnp.bfloat16))

    down_low = [part.astype(jnp.bfloat16) for part in grad_downs[1:]]
    up_low = [part.astype(jnp.bfloat16) for part in grad_ups[1:]]

    def moved(parts):
        return [layout.swap(part, step) for part, step in zip(parts, distances)]

    def cut(part, second):
        middle = part.shape[0] // 2
        return part[middle:] if second else part[:middle]

    down_moved_first = moved([cut(part, False) for part in down_low])
    down_moved_second = moved([after(cut(part, True), *down_moved_first) for part in down_low])
    up_moved_first = moved([after(cut(part, False), *down_moved_second) for part in up_low])
    up_moved_second = moved([after(cut(part, True), *up_moved_first) for part in up_low])

    def own_slice(own, first, second):
        total = own
        for pieces in zip(first, second):
            total = total + jnp.concatenate(pieces, axis=0).astype(jnp.float32)
        return total[None]

    grad_expert_up = own_slice(grad_ups[0], up_moved_first, up_moved_second)
    grad_expert_down = own_slice(grad_downs[0], down_moved_first, down_moved_second)

    grad_back = after(grad_back, *down_moved_first)
    grad_residual, grad_gain_two = rms_backward(residual, inverse_two, gain_second, grad_back)
    grad_residual = grad_residual + grad_out_low.astype(jnp.float32)
    grad_mixed = grad_residual.astype(jnp.bfloat16)
    grad_weight_out = contract_rows(attended_low, grad_mixed)
    grad_attended = contract_last(grad_mixed, weight_out).astype(jnp.bfloat16)
    out_sum = layout.reduce_dense(grad_weight_out.astype(jnp.bfloat16))
    grad_q, grad_k, grad_v, grad_off = attend_backward(
        bases, queries, grad_attended, attended, key_values, skew, logsum
    )
    grad_off = after(grad_off, *down_moved_second)

    def back_through(grad_part, first_column):
        return contract_last(
            grad_part, weight_joint[:, first_column : first_column + model_width]
        )

    partial_one = back_through(grad_k, model_width) + back_through(grad_v, 2 * model_width)
    partial_own = back_through(grad_q, 0)
    every_normed = every_float * every_inverse
    grad_gain_one = jnp.sum(partial_one * every_normed, axis=0) + jnp.sum(
        partial_own * every_normed[:token_count], axis=0
    )
    grad_hidden_one = layout.sum_rows(partial_one) + partial_own
    grad_input_norm, _ = rms_backward(tokens_f, inverse_one, gain_first, grad_hidden_one)
    grad_tokens = layout.return_blocks((grad_input_norm + grad_residual).astype(jnp.bfloat16)).astype(
        jnp.float32
    )
    joint_parts = [
        contract_rows(hidden_one[: part.shape[0]], part).astype(jnp.bfloat16)
        for part in (grad_q, grad_k, grad_v)
    ]
    grad_table = jnp.dot(
        bucket_hot.astype(jnp.float32),
        grad_off.reshape(head_count, -1)[:, :offset_count].T,
        precision=HIGHEST,
    )
    small_grads = [grad_gain_one, grad_gain_two, grad_router, grad_table]
    shard_rows = joint_projection.shape[0]
    side_width = -(-small_count // (shard_rows * TILE)) * TILE
    small_grads = jnp.concatenate([part.reshape(shards, -1) for part in small_grads], axis=1)
    small_grads = jnp.pad(small_grads, ((0, 0), (0, shard_rows * side_width - small_count)))
    side = small_grads.reshape(shards * shard_rows, side_width).astype(jnp.bfloat16)
    joint_sum = layout.reduce_dense(jnp.concatenate(joint_parts + [side], axis=1))
    side_sum = joint_sum[:, 3 * model_width :].reshape(-1)[:small_count].astype(jnp.float32)
    sum_gain_one, sum_gain_two, sum_router, sum_table = jnp.split(side_sum, small_cuts)
    return (
        layer_out,
        grad_tokens,
        sum_gain_one,
        joint_sum[:, : 3 * model_width].astype(jnp.float32),
        out_sum.astype(jnp.float32),
        sum_table.reshape(bias_table.shape),
        sum_gain_two,
        sum_router.reshape(router_weight.shape),
        grad_expert_up,
        grad_expert_down,
    )


def solution(mesh):
    in_specs = (
        P("exp", "ctx", None),
        P("exp"),
        P("exp", None),
        P("exp", None),
        P("exp", None),
        P("exp"),
        P("exp", None),
        P("exp", None, "ctx"),
        P("exp", "ctx", None),
        P("exp", "ctx", None),
        P("exp", "ctx"),
        P(),
        P("exp", "ctx", None),
    )
    out_specs = (
        P("exp", "ctx", None),
        P("exp", "ctx", None),
        P("exp"),
        P("exp", None),
        P("exp", None),
        P("exp", None),
        P("exp"),
        P("exp", None),
        P("exp", None, "ctx"),
        P("exp", "ctx", None),
    )
    return jax.shard_map(
        per_device, mesh=mesh, in_specs=in_specs, out_specs=out_specs, check_vma=False
    )
```

```python
import functools

import jax
import jax.numpy as jnp
from jax import lax
from jax.experimental import pallas as pl
from jax.experimental.pallas import tpu as pltpu
from jax.sharding import PartitionSpec as P

EPSILON = 1e-06
HALF = 64
TILE = 128
GROUP = 256
VMEM_BYTES = 50 * 1024 * 1024
SCORE_SCALE = 0.125
HIGHEST = lax.Precision.HIGHEST
BOTH = ("ctx", "exp")


def contract_last(left, right):
    return lax.dot_general(
        left, right, (((1,), (1,)), ((), ())), preferred_element_type=jnp.float32
    )


def matmul(left, right):
    return lax.dot_general(
        left, right, (((1,), (0,)), ((), ())), preferred_element_type=jnp.float32
    )


def skew_kernel(offset_ref, skew_ref):
    padded = offset_ref.shape[-1]
    kept = skew_ref.shape[1]
    rows = jnp.broadcast_to(offset_ref[0], (TILE, padded))
    rolled = pltpu.roll(rows, padded - (TILE - 1), 1, stride=1, stride_axis=0)
    skew_ref[0] = rolled[:, :kept].T.astype(skew_ref.dtype)


def make_skew(offset_values):
    head_count, padded = offset_values.shape
    kept = padded - TILE
    return pl.pallas_call(
        skew_kernel,
        grid=(head_count,),
        in_specs=[pl.BlockSpec((1, 1, padded), lambda h: (h, 0, 0))],
        out_specs=pl.BlockSpec((1, kept, TILE), lambda h: (h, 0, 0)),
        out_shape=jax.ShapeDtypeStruct((head_count, kept, TILE), jnp.bfloat16),
        compiler_params=pltpu.CompilerParams(vmem_limit_bytes=VMEM_BYTES),
        name="skew_bias",
    )(offset_values.reshape(head_count, 1, padded))


def half_mask(rows, half):
    lanes = lax.broadcasted_iota(jnp.int32, (rows, TILE), 1)
    return (lanes // HALF) == half


def bias_rows(key_base, query_base, seq_len):
    return key_base - query_base + seq_len - TILE


def forward_kernel(
    base_ref, q_ref, k_ref, v_ref, skew_ref, out_ref, lse_ref, score_ref, prob_ref, *, chunk
):
    query_rows = q_ref.shape[0]
    key_rows = k_ref.shape[0]
    seq_len = key_rows
    mask = [half_mask(GROUP, 0), half_mask(GROUP, 1)]
    value_t = v_ref[...].T
    for group in range(query_rows // GROUP):
        rows = slice(group * GROUP, (group + 1) * GROUP)
        query_base = base_ref[0] + group * GROUP
        halves = []
        for half in range(2):
            queries = jnp.where(mask[half], q_ref[rows], 0).astype(jnp.bfloat16)
            score_ref[half] = contract_last(k_ref[...], queries)
            top = jnp.full((8, GROUP), -jnp.inf, jnp.float32)
            for start in range(0, key_rows, chunk):
                key_base = base_ref[start // query_rows] + start % query_rows
                place = pl.multiple_of(bias_rows(key_base, query_base, seq_len), TILE)
                left = skew_ref[half, pl.ds(place, chunk), :]
                right = skew_ref[half, pl.ds(place - TILE, chunk), :]
                bias = jnp.concatenate([left, right], axis=1).astype(jnp.float32)
                piece = score_ref[half, start : start + chunk] + bias
                score_ref[half, start : start + chunk] = piece
                top = jnp.maximum(top, jnp.max(piece.reshape(chunk // 8, 8, GROUP), axis=0))
            top = jnp.max(top, axis=0, keepdims=True)
            total = jnp.zeros((8, GROUP), jnp.float32)
            for start in range(0, key_rows, chunk):
                piece = jnp.exp(score_ref[half, start : start + chunk] - top)
                total = total + jnp.sum(piece.reshape(chunk // 8, 8, GROUP), axis=0)
                prob_ref[half, start : start + chunk] = piece.astype(jnp.bfloat16)
            total = jnp.sum(total, axis=0, keepdims=True)
            lse_ref[0, half : half + 1, rows] = top + jnp.log(total)
            mixed = matmul(value_t[half * HALF : (half + 1) * HALF], prob_ref[half])
            halves.append(mixed / total)
        out_ref[rows] = jnp.concatenate(halves, axis=0).T


def attend_forward(bases, queries, key_values, skew):
    query_rows, width = queries.shape
    key_rows = key_values.shape[0]
    kept = skew.shape[1]
    pairs = width // TILE
    chunk = TILE
    return pl.pallas_call(
        functools.partial(forward_kernel, chunk=chunk),
        grid_spec=pltpu.PrefetchScalarGridSpec(
            num_scalar_prefetch=1,
            grid=(pairs,),
            in_specs=[
                pl.BlockSpec((query_rows, TILE), lambda p, _: (0, p)),
                pl.BlockSpec((key_rows, TILE), lambda p, _: (0, p)),
                pl.BlockSpec((key_rows, TILE), lambda p, _: (0, p + pairs)),
                pl.BlockSpec((2, kept, TILE), lambda p, _: (p, 0, 0)),
            ],
            out_specs=[
                pl.BlockSpec((query_rows, TILE), lambda p, _: (0, p)),
                pl.BlockSpec((1, 2, query_rows), lambda p, _: (p, 0, 0)),
            ],
            scratch_shapes=[
                pltpu.VMEM((2, key_rows, GROUP), jnp.float32),
                pltpu.VMEM((2, key_rows, GROUP), jnp.bfloat16),
            ],
        ),
        out_shape=[
            jax.ShapeDtypeStruct((query_rows, width), jnp.float32),
            jax.ShapeDtypeStruct((pairs, 2, query_rows), jnp.float32),
        ],
        compiler_params=pltpu.CompilerParams(vmem_limit_bytes=VMEM_BYTES),
        name="attend_forward",
    )(bases, queries, key_values, key_values, skew)


def backward_kernel(
    base_ref, q_ref, do_ref, o_ref, k_ref, v_ref, skew_ref, lse_ref,
    dq_ref, dk_ref, dv_ref, off_ref,
    score_ref, gradp_ref, prob_ref, grads_ref, accum_k, accum_v, accum_skew,
    *, chunk,
):
    query_rows = q_ref.shape[0]
    key_rows = k_ref.shape[0]
    seq_len = key_rows
    mask = [half_mask(GROUP, 0), half_mask(GROUP, 1)]
    key_t = k_ref[...].T
    accum_skew[...] = jnp.zeros_like(accum_skew)
    for group in range(query_rows // GROUP):
        rows = slice(group * GROUP, (group + 1) * GROUP)
        query_base = base_ref[0] + group * GROUP
        product = (do_ref[rows].astype(jnp.float32) * o_ref[rows]).T
        halves = []
        sum_k = None
        for half in range(2):
            queries = jnp.where(mask[half], q_ref[rows], 0).astype(jnp.bfloat16)
            grads_out = jnp.where(mask[half], do_ref[rows], 0).astype(jnp.bfloat16)
            score_ref[half] = contract_last(k_ref[...], queries)
            gradp_ref[half] = contract_last(v_ref[...], grads_out)
            logsum = lse_ref[0, half : half + 1, rows]
            delta = jnp.sum(product[half * HALF : (half + 1) * HALF], axis=0, keepdims=True)
            for start in range(0, key_rows, chunk):
                key_base = base_ref[start // query_rows] + start % query_rows
                place = pl.multiple_of(bias_rows(key_base, query_base, seq_len), TILE)
                here = pl.ds(start, chunk)
                left = skew_ref[half, pl.ds(place, chunk), :]
                right = skew_ref[half, pl.ds(place - TILE, chunk), :]
                bias = jnp.concatenate([left, right], axis=1).astype(jnp.float32)
                prob = jnp.exp(score_ref[half, here] + bias - logsum)
                grads = prob * (gradp_ref[half, here] - delta)
                prob_ref[half, here] = prob.astype(jnp.bfloat16)
                grads_ref[half, here] = grads.astype(jnp.bfloat16)
                accum_skew[half, pl.ds(place, chunk), :] += grads[:, :TILE]
                accum_skew[half, pl.ds(place - TILE, chunk), :] += grads[:, TILE:]
            part_k = matmul(grads_ref[half], queries)
            part_v = matmul(prob_ref[half], grads_out)
            sum_k = part_k if sum_k is None else sum_k + part_k
            sum_v = part_v if half == 0 else sum_v + part_v
            halves.append(matmul(key_t[half * HALF : (half + 1) * HALF], grads_ref[half]))
        if group == 0:
            accum_k[...] = sum_k
            accum_v[...] = sum_v
        else:
            accum_k[...] += sum_k
            accum_v[...] += sum_v
        dq_ref[rows] = (jnp.concatenate(halves, axis=0) * 0.125).T.astype(dq_ref.dtype)
    dk_ref[...] = accum_k[...].astype(dk_ref.dtype)
    dv_ref[...] = accum_v[...].astype(dv_ref.dtype)
    for half in range(2):
        turned = accum_skew[half].T
        padded = turned.shape[1]
        count = TILE // 2
        while count:
            turned = turned[:count] + pltpu.roll(turned[count : 2 * count], padded - count, 1)
            count //= 2
        off_ref[0, half : half + 1] = pltpu.roll(turned, TILE - 1, 1)


def attend_backward(bases, queries, grads_out, outputs, key_values, skew, logsum):
    query_rows, width = queries.shape
    key_rows = key_values.shape[0]
    kept = skew.shape[1]
    pairs = width // TILE
    chunk = TILE
    column = lambda count: pl.BlockSpec((count, TILE), lambda p, _: (0, p))
    return pl.pallas_call(
        functools.partial(backward_kernel, chunk=chunk),
        grid_spec=pltpu.PrefetchScalarGridSpec(
            num_scalar_prefetch=1,
            grid=(pairs,),
            in_specs=[
                column(query_rows), column(query_rows), column(query_rows),
                column(key_rows),
                pl.BlockSpec((key_rows, TILE), lambda p, _: (0, p + pairs)),
                pl.BlockSpec((2, kept, TILE), lambda p, _: (p, 0, 0)),
                pl.BlockSpec((1, 2, query_rows), lambda p, _: (p, 0, 0)),
            ],
            out_specs=[
                column(query_rows), column(key_rows), column(key_rows),
                pl.BlockSpec((1, 2, kept + TILE), lambda p, _: (p, 0, 0)),
            ],
            scratch_shapes=[
                pltpu.VMEM((2, key_rows, GROUP), jnp.float32),
                pltpu.VMEM((2, key_rows, GROUP), jnp.float32),
                pltpu.VMEM((2, key_rows, GROUP), jnp.bfloat16),
                pltpu.VMEM((2, key_rows, GROUP), jnp.bfloat16),
                pltpu.VMEM((key_rows, TILE), jnp.float32),
                pltpu.VMEM((key_rows, TILE), jnp.float32),
                pltpu.VMEM((2, kept + TILE, TILE), jnp.float32),
            ],
        ),
        out_shape=[
            jax.ShapeDtypeStruct((query_rows, width), jnp.bfloat16),
            jax.ShapeDtypeStruct((key_rows, width), jnp.bfloat16),
            jax.ShapeDtypeStruct((key_rows, width), jnp.bfloat16),
            jax.ShapeDtypeStruct((pairs, 2, kept + TILE), jnp.float32),
        ],
        compiler_params=pltpu.CompilerParams(vmem_limit_bytes=VMEM_BYTES),
        name="attend_backward",
    )(bases, queries, grads_out, outputs, key_values, key_values, skew, logsum)


def rms_forward(row_data, gain_vec):
    inverse = lax.rsqrt(jnp.mean(row_data * row_data, axis=-1, keepdims=True) + EPSILON)
    return (row_data * inverse * gain_vec, inverse)


def rms_backward(row_data, inverse, gain_vec, grad_out):
    normed = row_data * inverse
    grad_gain = jnp.sum(grad_out * normed, axis=0)
    scaled = grad_out * gain_vec
    spread = jnp.mean(scaled * normed, axis=-1, keepdims=True)
    return (inverse * (scaled - normed * spread), grad_gain)


class Layout:
    def __init__(self):
        self.ctx_count = lax.axis_size("ctx")
        self.exp_count = lax.axis_size("exp")
        self.span = self.ctx_count // 4
        self.members = 2 * self.span
        self.ctx = lax.axis_index("ctx")
        self.core = lax.axis_index("exp") % 2
        self.member = (self.ctx % self.span) * 2 + self.core
        self.side = (self.ctx // self.span) % 2

    def number(self, ctx, exp):
        return ctx * self.exp_count + exp

    def round_pairs(self, turn):
        pairs = []
        for ctx in range(self.ctx_count):
            for exp in range(self.exp_count):
                seq = 2 * (exp % 2) + (turn + ctx) % 2
                member = ctx // 2
                target = self.number(seq * self.span + member // 2, exp // 2 * 2 + member % 2)
                pairs.append((self.number(ctx, exp), target))
        return pairs

    def member_pairs(self, shift):
        pairs = []
        for ctx in range(self.ctx_count):
            for exp in range(self.exp_count):
                start = ctx // self.span * self.span
                member = ((ctx - start) * 2 + exp % 2 + shift) % self.members
                target = self.number(start + member // 2, exp // 2 * 2 + member % 2)
                pairs.append((self.number(ctx, exp), target))
        return pairs

    def gather_blocks(self, blocks):
        got = [
            lax.ppermute(
                lax.dynamic_index_in_dim(blocks, (turn + self.ctx) % 2, 0, keepdims=False),
                BOTH,
                self.round_pairs(turn),
            )
            for turn in range(2)
        ]
        first = jnp.where(self.side == 0, got[0], got[1])
        second = jnp.where(self.side == 0, got[1], got[0])
        return jnp.concatenate([first, second], axis=0)

    def return_blocks(self, rows):
        blocks = rows.reshape((2, rows.shape[0] // 2) + rows.shape[1:])
        got = [
            lax.ppermute(
                lax.dynamic_index_in_dim(blocks, (turn + self.side) % 2, 0, keepdims=False),
                BOTH,
                [(target, source) for source, target in self.round_pairs(turn)],
            )
            for turn in range(2)
        ]
        even = self.ctx % 2 == 0
        return jnp.stack([jnp.where(even, got[0], got[1]), jnp.where(even, got[1], got[0])])

    def all_rows(self, rows):
        return jnp.concatenate(
            [rows]
            + [lax.ppermute(rows, BOTH, self.member_pairs(shift)) for shift in range(1, self.members)],
            axis=0,
        )

    def sum_rows(self, partial):
        parts = partial.reshape((self.members, partial.shape[0] // self.members) + partial.shape[1:])
        total = parts[0]
        for shift in range(1, self.members):
            moved = lax.ppermute(
                parts[shift].astype(jnp.bfloat16), BOTH, self.member_pairs(self.members - shift)
            )
            total = total + moved.astype(jnp.float32)
        return total

    def bases(self, row_count):
        return jnp.stack(
            [(self.member - shift) % self.members * row_count for shift in range(self.members)]
        ).astype(jnp.int32)

    def swap(self, rows, distance, axis="ctx"):
        pairs = [(place, place ^ distance) for place in range(lax.axis_size(axis))]
        return lax.ppermute(rows, axis, pairs)

    def gather_small(self, part):
        held = part[None]
        place = lax.axis_index("exp")
        distance = 1
        while distance < self.exp_count:
            other = self.swap(held, distance, "exp")
            upper = (place // distance) % 2 == 1
            held = jnp.where(
                upper,
                jnp.concatenate([other, held], axis=0),
                jnp.concatenate([held, other], axis=0),
            )
            distance *= 2
        return held

    def reduce_dense(self, part):
        rows = part.shape[0] // self.exp_count
        pair_count = self.exp_count // 2
        blocks = part.reshape(pair_count, 2, rows, part.shape[1])
        sent = lax.dynamic_index_in_dim(blocks, 1 - self.core, 1, keepdims=False)
        kept = lax.dynamic_index_in_dim(blocks, self.core, 1, keepdims=False)
        both = add_low([kept, self.swap(sent, 1, "exp")])
        pair = lax.axis_index("exp") // 2
        parts = [lax.dynamic_index_in_dim(both, pair, 0, keepdims=False)]
        for step in range(1, pair_count):
            block = lax.dynamic_index_in_dim(both, pair ^ step, 0, keepdims=False)
            parts.append(self.swap(block, 2 * step, "exp"))
        total = add_low(parts)
        cuts = total.reshape(self.ctx_count, rows // self.ctx_count, part.shape[1])
        parts = [lax.dynamic_index_in_dim(cuts, self.ctx, 0, keepdims=False)]
        for step in range(1, self.ctx_count):
            block = lax.dynamic_index_in_dim(cuts, self.ctx ^ step, 0, keepdims=False)
            parts.append(self.swap(block, step))
        own = add_low(parts)
        every = jnp.stack([own] + [self.swap(own, step) for step in range(1, self.ctx_count)])
        return jnp.concatenate(
            [
                lax.dynamic_index_in_dim(every, self.ctx ^ place, 0, keepdims=False)
                for place in range(self.ctx_count)
            ],
            axis=0,
        )


def add_low(parts):
    total = parts[0].astype(jnp.float32)
    for part in parts[1:]:
        total = total + part.astype(jnp.float32)
    return total.astype(jnp.bfloat16)


def after(value, *events):
    return lax.optimization_barrier((value,) + events)[0]


def per_device(
    tokens_in,
    first_gain,
    joint_projection,
    out_projection,
    bias_table,
    second_gain,
    router_weight,
    expert_up,
    expert_down,
    expert_index,
    keep_mask,
    buckets,
    cotangent,
):
    layout = Layout()
    shards = layout.exp_count
    seq_count, block_len, model_width = tokens_in.shape
    token_count = seq_count * block_len
    expert_count = router_weight.shape[1]
    bucket_count = bias_table.shape[0] * shards
    head_count = bias_table.shape[1]

    small = [first_gain, second_gain, router_weight, bias_table]
    small_sizes = [part.size for part in small]
    small_cuts = [sum(small_sizes[:place]) for place in range(1, len(small))]
    small_count = sum(small_sizes)
    small_padded = -(-small_count // TILE) * TILE
    small_full = layout.gather_small(
        jnp.pad(
            jnp.concatenate([part.reshape(-1) for part in small]), (0, small_padded - small_count)
        )
    )[:, :small_count]
    gain_one, gain_two, weight_router, table = jnp.split(small_full, small_cuts, axis=1)
    weight_router = weight_router.reshape(model_width, expert_count)
    table = table.reshape(bucket_count, head_count)
    gain_first = gain_one.reshape(model_width).astype(jnp.float32)
    gain_second = gain_two.reshape(model_width).astype(jnp.float32)
    weight_joint = lax.all_gather(joint_projection, "exp", axis=0, tiled=True)
    weight_out = lax.all_gather(out_projection, "exp", axis=0, tiled=True)

    tokens = layout.gather_blocks(tokens_in)
    codes = layout.gather_blocks(expert_index.reshape(seq_count, block_len) * 2 + keep_mask)
    grad_out_low = layout.gather_blocks(cotangent)
    every_token = layout.all_rows(tokens)
    chosen = codes // 2
    kept = codes % 2

    distances = list(range(2, layout.ctx_count, 2))
    up_moved = [layout.swap(expert_up[0], step) for step in distances]
    down_moved = [layout.swap(expert_down[0], step) for step in distances]

    offset_count = buckets.shape[0]
    bucket_hot = buckets[None, :] == jnp.arange(bucket_count, dtype=jnp.int32)[:, None]
    offset_values = lax.dot_general(
        table,
        bucket_hot.astype(jnp.bfloat16),
        (((0,), (0,)), ((), ())),
        preferred_element_type=jnp.float32,
    )
    skew = make_skew(jnp.pad(offset_values, ((0, 0), (0, 1))))

    is_choice = chosen[:, None] == jnp.arange(expert_count, dtype=jnp.int32)
    most_rows = max(2, (5 * block_len + 4 * expert_count - 1) // (4 * expert_count))
    capacity = seq_count * most_rows
    place = jnp.arange(token_count, dtype=jnp.int32)
    earlier = (place[:, None] >= place[None, :]) & (
        place[:, None] // block_len == place[None, :] // block_len
    )
    running = jnp.dot(
        earlier.astype(jnp.bfloat16),
        is_choice.astype(jnp.bfloat16),
        preferred_element_type=jnp.float32,
    )
    slot_rank = (jnp.sum(running * is_choice.astype(jnp.float32), axis=-1) - 1.0).astype(jnp.int32)
    token_slot = chosen * capacity + place // block_len * most_rows + slot_rank
    slot_hot = (
        (token_slot[:, None] == jnp.arange(expert_count * capacity, dtype=jnp.int32))
        & (kept[:, None] > 0)
    ).astype(jnp.bfloat16)

    def exchange(row_data):
        return lax.all_to_all(
            row_data.reshape(shards, -1, model_width), "exp", split_axis=0, concat_axis=0, tiled=True
        ).reshape(-1, model_width)

    def to_experts(row_data):
        sent = lax.dot_general(
            slot_hot, row_data, (((0,), (0,)), ((), ())), preferred_element_type=jnp.float32
        ).astype(jnp.bfloat16)
        return exchange(sent)

    def sum_halves(own_part, other_part):
        other = layout.swap(other_part, 1)
        return (own_part + other.astype(jnp.float32)).astype(jnp.bfloat16)

    def from_experts(summed):
        return jnp.dot(slot_hot, exchange(summed), preferred_element_type=jnp.float32)

    grad_own = to_experts(grad_out_low)
    grad_other = layout.swap(grad_own, 1)

    every_float = every_token.astype(jnp.float32)
    tokens_f = every_float[:token_count]
    normed_one, every_inverse = rms_forward(every_float, gain_first)
    inverse_one = every_inverse[:token_count]
    hidden_one = after(normed_one.astype(jnp.bfloat16), grad_out_low)
    queries = jnp.dot(
        hidden_one[:token_count], weight_joint[:, :model_width], preferred_element_type=jnp.float32
    ).astype(jnp.bfloat16) * jnp.bfloat16(SCORE_SCALE)
    key_values = jnp.dot(
        hidden_one, weight_joint[:, model_width:], preferred_element_type=jnp.float32
    ).astype(jnp.bfloat16)
    bases = layout.bases(token_count)
    attended, logsum = attend_forward(bases, queries, key_values, skew)
    attended = after(attended, grad_own)
    attended_low = attended.astype(jnp.bfloat16)
    residual = tokens_f + jnp.dot(attended_low, weight_out, preferred_element_type=jnp.float32)
    normed_two, inverse_two = rms_forward(residual, gain_second)
    hidden_two = normed_two.astype(jnp.bfloat16)

    row_own = after(to_experts(hidden_two), grad_other, *up_moved, *down_moved)
    row_other = layout.swap(row_own, 1)
    ups = [expert_up[0]] + up_moved
    downs = [expert_down[0]] + down_moved

    expert_here = jnp.arange(expert_count, dtype=jnp.int32) == lax.axis_index("exp")
    expert_here = expert_here.astype(jnp.float32)[None, :]

    def contract_rows(left, right):
        return lax.dot_general(
            left, right, (((0,), (0,)), ((), ())), preferred_element_type=jnp.float32
        )

    results, grad_inputs = [], []
    grad_router = 0.0
    grad_ups, grad_downs = [0.0] * len(ups), [0.0] * len(ups)
    for rows, grad_rows in ((row_own, grad_own), (row_other, grad_other)):
        logits = jnp.dot(rows, weight_router, preferred_element_type=jnp.float32)
        router_prob = jax.nn.softmax(logits, axis=-1)
        picked = jnp.sum(router_prob * expert_here, axis=-1, keepdims=True)
        grad_float = grad_rows.astype(jnp.float32)
        grad_result = (picked * grad_float).astype(jnp.bfloat16)
        produced, grad_input = 0.0, 0.0
        for part, (matrix_up, matrix_down) in enumerate(zip(ups, downs)):
            before = jnp.dot(rows, matrix_up, preferred_element_type=jnp.float32)
            activated, gelu_back = jax.vjp(jax.nn.gelu, before)
            acted = activated.astype(jnp.bfloat16)
            produced = produced + jnp.dot(acted, matrix_down, preferred_element_type=jnp.float32)
            grad_acted = contract_last(grad_result, matrix_down)
            grad_before = gelu_back(grad_acted)[0].astype(jnp.bfloat16)
            grad_input = grad_input + contract_last(grad_before, matrix_up)
            grad_ups[part] = grad_ups[part] + contract_rows(rows, grad_before)
            grad_downs[part] = grad_downs[part] + contract_rows(acted, grad_result)
        grad_picked = jnp.sum(grad_float * produced, axis=-1, keepdims=True)
        grad_logits = (picked * (expert_here - router_prob) * grad_picked).astype(jnp.bfloat16)
        grad_router = grad_router + contract_rows(rows, grad_logits)
        grad_inputs.append(grad_input + contract_last(grad_logits, weight_router))
        results.append(picked * produced)

    grad_summed = sum_halves(grad_inputs[0], grad_inputs[1].astype(jnp.bfloat16))
    grad_back = from_experts(grad_summed)
    result_other = after(results[1].astype(jnp.bfloat16), grad_summed)
    layer_rows = residual + from_experts(sum_halves(results[0], result_other))
    layer_out = layout.return_blocks(layer_rows.astype(jnp.bfloat16))

    down_low = [part.astype(jnp.bfloat16) for part in grad_downs[1:]]
    up_low = [part.astype(jnp.bfloat16) for part in grad_ups[1:]]

    def moved(parts):
        return [layout.swap(part, step) for part, step in zip(parts, distances)]

    grads_down_moved = moved(down_low)
    grads_up_moved = moved(up_low)

    def own_slice(own, others):
        total = own
        for other in others:
            total = total + other.astype(jnp.float32)
        return total[None]

    grad_residual, grad_gain_two = rms_backward(residual, inverse_two, gain_second, grad_back)
    grad_residual = grad_residual + grad_out_low.astype(jnp.float32)
    grad_mixed = grad_residual.astype(jnp.bfloat16)
    grad_weight_out = contract_rows(attended_low, grad_mixed)
    grad_attended = contract_last(grad_mixed, weight_out).astype(jnp.bfloat16)
    out_sum = layout.reduce_dense(grad_weight_out.astype(jnp.bfloat16))
    grad_q, grad_k, grad_v, grad_off = attend_backward(
        bases, queries, grad_attended, attended, key_values, skew, logsum
    )
    grad_k, *grads_down_moved = lax.optimization_barrier((grad_k, *grads_down_moved))
    grad_kv = jnp.concatenate([grad_k, grad_v], axis=1)
    partial_one = contract_last(grad_kv, weight_joint[:, model_width:])
    partial_own = contract_last(grad_q, weight_joint[:, :model_width])
    every_normed = every_float * every_inverse
    grad_gain_one = jnp.sum(partial_one * every_normed, axis=0) + jnp.sum(
        partial_own * every_normed[:token_count], axis=0
    )
    grad_hidden_one = layout.sum_rows(partial_one) + partial_own
    grad_input_norm, _ = rms_backward(tokens_f, inverse_one, gain_first, grad_hidden_one)
    grad_tokens = layout.return_blocks((grad_input_norm + grad_residual).astype(jnp.bfloat16)).astype(
        jnp.float32
    )
    kv_sum = layout.reduce_dense(contract_rows(hidden_one, grad_kv).astype(jnp.bfloat16))
    query_part = contract_rows(hidden_one[:token_count], grad_q).astype(jnp.bfloat16)
    query_part, *grads_up_moved = lax.optimization_barrier((query_part, *grads_up_moved))
    grad_expert_up = own_slice(grad_ups[0], grads_up_moved)
    grad_expert_down = own_slice(grad_downs[0], grads_down_moved)
    grad_table = jnp.dot(
        bucket_hot.astype(jnp.float32),
        grad_off.reshape(head_count, -1)[:, :offset_count].T,
        precision=HIGHEST,
    )
    small_grads = [grad_gain_one, grad_gain_two, grad_router, grad_table]
    shard_rows = joint_projection.shape[0]
    side_width = -(-small_count // (shard_rows * TILE)) * TILE
    small_grads = jnp.concatenate([part.reshape(shards, -1) for part in small_grads], axis=1)
    small_grads = jnp.pad(small_grads, ((0, 0), (0, shard_rows * side_width - small_count)))
    side = small_grads.reshape(shards * shard_rows, side_width).astype(jnp.bfloat16)
    query_sum = layout.reduce_dense(jnp.concatenate([query_part, side], axis=1))
    side_sum = query_sum[:, model_width:].reshape(-1)[:small_count].astype(jnp.float32)
    joint_sum = jnp.concatenate([query_sum[:, :model_width], kv_sum], axis=1)
    sum_gain_one, sum_gain_two, sum_router, sum_table = jnp.split(side_sum, small_cuts)
    return (
        layer_out,
        grad_tokens,
        sum_gain_one,
        joint_sum.astype(jnp.float32),
        out_sum.astype(jnp.float32),
        sum_table.reshape(bias_table.shape),
        sum_gain_two,
        sum_router.reshape(router_weight.shape),
        grad_expert_up,
        grad_expert_down,
    )


def solution(mesh):
    in_specs = (
        P("exp", "ctx", None),
        P("exp"),
        P("exp", None),
        P("exp", None),
        P("exp", None),
        P("exp"),
        P("exp", None),
        P("exp", None, "ctx"),
        P("exp", "ctx", None),
        P("exp", "ctx", None),
        P("exp", "ctx"),
        P(),
        P("exp", "ctx", None),
    )
    out_specs = (
        P("exp", "ctx", None),
        P("exp", "ctx", None),
        P("exp"),
        P("exp", None),
        P("exp", None),
        P("exp", None),
        P("exp"),
        P("exp", None),
        P("exp", None, "ctx"),
        P("exp", "ctx", None),
    )
    return jax.shard_map(
        per_device, mesh=mesh, in_specs=in_specs, out_specs=out_specs, check_vma=False
    )
```

```python
import functools

import jax
import jax.numpy as jnp
from jax import lax
from jax.experimental import pallas as pl
from jax.experimental.pallas import tpu as pltpu
from jax.sharding import PartitionSpec as P

EPSILON = 1e-06
HALF = 64
TILE = 128
GROUP = 256
VMEM_BYTES = 50 * 1024 * 1024
SCORE_SCALE = 0.125
HIGHEST = lax.Precision.HIGHEST
BOTH = ("ctx", "exp")


def contract_last(left, right):
    return lax.dot_general(
        left, right, (((1,), (1,)), ((), ())), preferred_element_type=jnp.float32
    )


def matmul(left, right):
    return lax.dot_general(
        left, right, (((1,), (0,)), ((), ())), preferred_element_type=jnp.float32
    )


def skew_kernel(offset_ref, skew_ref):
    padded = offset_ref.shape[-1]
    kept = skew_ref.shape[1]
    rows = jnp.broadcast_to(offset_ref[0], (TILE, padded))
    rolled = pltpu.roll(rows, padded - (TILE - 1), 1, stride=1, stride_axis=0)
    skew_ref[0] = rolled[:, :kept].T.astype(skew_ref.dtype)


def make_skew(offset_values):
    head_count, padded = offset_values.shape
    kept = padded - TILE
    return pl.pallas_call(
        skew_kernel,
        grid=(head_count,),
        in_specs=[pl.BlockSpec((1, 1, padded), lambda h: (h, 0, 0))],
        out_specs=pl.BlockSpec((1, kept, TILE), lambda h: (h, 0, 0)),
        out_shape=jax.ShapeDtypeStruct((head_count, kept, TILE), jnp.bfloat16),
        compiler_params=pltpu.CompilerParams(vmem_limit_bytes=VMEM_BYTES),
        name="skew_bias",
    )(offset_values.reshape(head_count, 1, padded))


def half_mask(rows, half):
    lanes = lax.broadcasted_iota(jnp.int32, (rows, TILE), 1)
    return (lanes // HALF) == half


def bias_rows(key_base, query_base, seq_len):
    return key_base - query_base + seq_len - TILE


def forward_kernel(
    base_ref, q_ref, k_ref, v_ref, skew_ref, out_ref, lse_ref, score_ref, prob_ref, *, chunk
):
    query_rows = q_ref.shape[0]
    key_rows = k_ref.shape[0]
    seq_len = key_rows
    mask = [half_mask(GROUP, 0), half_mask(GROUP, 1)]
    value_t = v_ref[...].T
    for group in range(query_rows // GROUP):
        rows = slice(group * GROUP, (group + 1) * GROUP)
        query_base = base_ref[0] + group * GROUP
        halves = []
        for half in range(2):
            queries = jnp.where(mask[half], q_ref[rows], 0).astype(jnp.bfloat16)
            score_ref[half] = contract_last(k_ref[...], queries)
            top = jnp.full((8, GROUP), -jnp.inf, jnp.float32)
            for start in range(0, key_rows, chunk):
                key_base = base_ref[start // query_rows] + start % query_rows
                place = pl.multiple_of(bias_rows(key_base, query_base, seq_len), TILE)
                left = skew_ref[half, pl.ds(place, chunk), :]
                right = skew_ref[half, pl.ds(place - TILE, chunk), :]
                bias = jnp.concatenate([left, right], axis=1).astype(jnp.float32)
                piece = score_ref[half, start : start + chunk] + bias
                score_ref[half, start : start + chunk] = piece
                top = jnp.maximum(top, jnp.max(piece.reshape(chunk // 8, 8, GROUP), axis=0))
            top = jnp.max(top, axis=0, keepdims=True)
            total = jnp.zeros((8, GROUP), jnp.float32)
            for start in range(0, key_rows, chunk):
                piece = jnp.exp(score_ref[half, start : start + chunk] - top)
                total = total + jnp.sum(piece.reshape(chunk // 8, 8, GROUP), axis=0)
                prob_ref[half, start : start + chunk] = piece.astype(jnp.bfloat16)
            total = jnp.sum(total, axis=0, keepdims=True)
            lse_ref[0, half : half + 1, rows] = top + jnp.log(total)
            mixed = matmul(value_t[half * HALF : (half + 1) * HALF], prob_ref[half])
            halves.append(mixed / total)
        out_ref[rows] = jnp.concatenate(halves, axis=0).T


def attend_forward(bases, queries, key_values, skew):
    query_rows, width = queries.shape
    key_rows = key_values.shape[0]
    kept = skew.shape[1]
    pairs = width // TILE
    chunk = TILE
    return pl.pallas_call(
        functools.partial(forward_kernel, chunk=chunk),
        grid_spec=pltpu.PrefetchScalarGridSpec(
            num_scalar_prefetch=1,
            grid=(pairs,),
            in_specs=[
                pl.BlockSpec((query_rows, TILE), lambda p, _: (0, p)),
                pl.BlockSpec((key_rows, TILE), lambda p, _: (0, p)),
                pl.BlockSpec((key_rows, TILE), lambda p, _: (0, p + pairs)),
                pl.BlockSpec((2, kept, TILE), lambda p, _: (p, 0, 0)),
            ],
            out_specs=[
                pl.BlockSpec((query_rows, TILE), lambda p, _: (0, p)),
                pl.BlockSpec((1, 2, query_rows), lambda p, _: (p, 0, 0)),
            ],
            scratch_shapes=[
                pltpu.VMEM((2, key_rows, GROUP), jnp.float32),
                pltpu.VMEM((2, key_rows, GROUP), jnp.bfloat16),
            ],
        ),
        out_shape=[
            jax.ShapeDtypeStruct((query_rows, width), jnp.float32),
            jax.ShapeDtypeStruct((pairs, 2, query_rows), jnp.float32),
        ],
        compiler_params=pltpu.CompilerParams(vmem_limit_bytes=VMEM_BYTES),
        name="attend_forward",
    )(bases, queries, key_values, key_values, skew)


def backward_kernel(
    base_ref, q_ref, do_ref, o_ref, k_ref, v_ref, skew_ref, lse_ref,
    dq_ref, dk_ref, dv_ref, off_ref,
    score_ref, gradp_ref, prob_ref, grads_ref, accum_k, accum_v, accum_skew,
    *, chunk,
):
    query_rows = q_ref.shape[0]
    key_rows = k_ref.shape[0]
    seq_len = key_rows
    mask = [half_mask(GROUP, 0), half_mask(GROUP, 1)]
    key_t = k_ref[...].T
    accum_skew[...] = jnp.zeros_like(accum_skew)
    for group in range(query_rows // GROUP):
        rows = slice(group * GROUP, (group + 1) * GROUP)
        query_base = base_ref[0] + group * GROUP
        product = (do_ref[rows].astype(jnp.float32) * o_ref[rows]).T
        halves = []
        sum_k = None
        for half in range(2):
            queries = jnp.where(mask[half], q_ref[rows], 0).astype(jnp.bfloat16)
            grads_out = jnp.where(mask[half], do_ref[rows], 0).astype(jnp.bfloat16)
            score_ref[half] = contract_last(k_ref[...], queries)
            gradp_ref[half] = contract_last(v_ref[...], grads_out)
            logsum = lse_ref[0, half : half + 1, rows]
            delta = jnp.sum(product[half * HALF : (half + 1) * HALF], axis=0, keepdims=True)
            for start in range(0, key_rows, chunk):
                key_base = base_ref[start // query_rows] + start % query_rows
                place = pl.multiple_of(bias_rows(key_base, query_base, seq_len), TILE)
                here = pl.ds(start, chunk)
                left = skew_ref[half, pl.ds(place, chunk), :]
                right = skew_ref[half, pl.ds(place - TILE, chunk), :]
                bias = jnp.concatenate([left, right], axis=1).astype(jnp.float32)
                prob = jnp.exp(score_ref[half, here] + bias - logsum)
                grads = prob * (gradp_ref[half, here] - delta)
                prob_ref[half, here] = prob.astype(jnp.bfloat16)
                grads_ref[half, here] = grads.astype(jnp.bfloat16)
                accum_skew[half, pl.ds(place, chunk), :] += grads[:, :TILE]
                accum_skew[half, pl.ds(place - TILE, chunk), :] += grads[:, TILE:]
            part_k = matmul(grads_ref[half], queries)
            part_v = matmul(prob_ref[half], grads_out)
            sum_k = part_k if sum_k is None else sum_k + part_k
            sum_v = part_v if half == 0 else sum_v + part_v
            halves.append(matmul(key_t[half * HALF : (half + 1) * HALF], grads_ref[half]))
        if group == 0:
            accum_k[...] = sum_k
            accum_v[...] = sum_v
        else:
            accum_k[...] += sum_k
            accum_v[...] += sum_v
        dq_ref[rows] = (jnp.concatenate(halves, axis=0) * 0.125).T.astype(dq_ref.dtype)
    dk_ref[...] = accum_k[...].astype(dk_ref.dtype)
    dv_ref[...] = accum_v[...].astype(dv_ref.dtype)
    for half in range(2):
        turned = accum_skew[half].T
        padded = turned.shape[1]
        count = TILE // 2
        while count:
            turned = turned[:count] + pltpu.roll(turned[count : 2 * count], padded - count, 1)
            count //= 2
        off_ref[0, half : half + 1] = pltpu.roll(turned, TILE - 1, 1)


def attend_backward(bases, queries, grads_out, outputs, key_values, skew, logsum):
    query_rows, width = queries.shape
    key_rows = key_values.shape[0]
    kept = skew.shape[1]
    pairs = width // TILE
    chunk = TILE
    column = lambda count: pl.BlockSpec((count, TILE), lambda p, _: (0, p))
    return pl.pallas_call(
        functools.partial(backward_kernel, chunk=chunk),
        grid_spec=pltpu.PrefetchScalarGridSpec(
            num_scalar_prefetch=1,
            grid=(pairs,),
            in_specs=[
                column(query_rows), column(query_rows), column(query_rows),
                column(key_rows),
                pl.BlockSpec((key_rows, TILE), lambda p, _: (0, p + pairs)),
                pl.BlockSpec((2, kept, TILE), lambda p, _: (p, 0, 0)),
                pl.BlockSpec((1, 2, query_rows), lambda p, _: (p, 0, 0)),
            ],
            out_specs=[
                column(query_rows), column(key_rows), column(key_rows),
                pl.BlockSpec((1, 2, kept + TILE), lambda p, _: (p, 0, 0)),
            ],
            scratch_shapes=[
                pltpu.VMEM((2, key_rows, GROUP), jnp.float32),
                pltpu.VMEM((2, key_rows, GROUP), jnp.float32),
                pltpu.VMEM((2, key_rows, GROUP), jnp.bfloat16),
                pltpu.VMEM((2, key_rows, GROUP), jnp.bfloat16),
                pltpu.VMEM((key_rows, TILE), jnp.float32),
                pltpu.VMEM((key_rows, TILE), jnp.float32),
                pltpu.VMEM((2, kept + TILE, TILE), jnp.float32),
            ],
        ),
        out_shape=[
            jax.ShapeDtypeStruct((query_rows, width), jnp.bfloat16),
            jax.ShapeDtypeStruct((key_rows, width), jnp.bfloat16),
            jax.ShapeDtypeStruct((key_rows, width), jnp.bfloat16),
            jax.ShapeDtypeStruct((pairs, 2, kept + TILE), jnp.float32),
        ],
        compiler_params=pltpu.CompilerParams(vmem_limit_bytes=VMEM_BYTES),
        name="attend_backward",
    )(bases, queries, grads_out, outputs, key_values, key_values, skew, logsum)


def rms_forward(row_data, gain_vec):
    inverse = lax.rsqrt(jnp.mean(row_data * row_data, axis=-1, keepdims=True) + EPSILON)
    return (row_data * inverse * gain_vec, inverse)


def rms_backward(row_data, inverse, gain_vec, grad_out):
    normed = row_data * inverse
    grad_gain = jnp.sum(grad_out * normed, axis=0)
    scaled = grad_out * gain_vec
    spread = jnp.mean(scaled * normed, axis=-1, keepdims=True)
    return (inverse * (scaled - normed * spread), grad_gain)


class Layout:
    def __init__(self):
        self.ctx_count = lax.axis_size("ctx")
        self.exp_count = lax.axis_size("exp")
        self.span = self.ctx_count // 4
        self.members = 2 * self.span
        self.ctx = lax.axis_index("ctx")
        self.core = lax.axis_index("exp") % 2
        self.member = (self.ctx % self.span) * 2 + self.core
        self.side = (self.ctx // self.span) % 2

    def number(self, ctx, exp):
        return ctx * self.exp_count + exp

    def round_pairs(self, turn):
        pairs = []
        for ctx in range(self.ctx_count):
            for exp in range(self.exp_count):
                seq = 2 * (exp % 2) + (turn + ctx) % 2
                member = ctx // 2
                target = self.number(seq * self.span + member // 2, exp // 2 * 2 + member % 2)
                pairs.append((self.number(ctx, exp), target))
        return pairs

    def member_pairs(self, shift):
        pairs = []
        for ctx in range(self.ctx_count):
            for exp in range(self.exp_count):
                start = ctx // self.span * self.span
                member = ((ctx - start) * 2 + exp % 2 + shift) % self.members
                target = self.number(start + member // 2, exp // 2 * 2 + member % 2)
                pairs.append((self.number(ctx, exp), target))
        return pairs

    def gather_blocks(self, blocks):
        got = [
            lax.ppermute(
                lax.dynamic_index_in_dim(blocks, (turn + self.ctx) % 2, 0, keepdims=False),
                BOTH,
                self.round_pairs(turn),
            )
            for turn in range(2)
        ]
        first = jnp.where(self.side == 0, got[0], got[1])
        second = jnp.where(self.side == 0, got[1], got[0])
        return jnp.concatenate([first, second], axis=0)

    def return_blocks(self, rows):
        blocks = rows.reshape((2, rows.shape[0] // 2) + rows.shape[1:])
        got = [
            lax.ppermute(
                lax.dynamic_index_in_dim(blocks, (turn + self.side) % 2, 0, keepdims=False),
                BOTH,
                [(target, source) for source, target in self.round_pairs(turn)],
            )
            for turn in range(2)
        ]
        return got

    def place_blocks(self, got):
        even = self.ctx % 2 == 0
        return jnp.stack([jnp.where(even, got[0], got[1]), jnp.where(even, got[1], got[0])])

    def all_rows(self, rows):
        return jnp.concatenate(
            [rows]
            + [lax.ppermute(rows, BOTH, self.member_pairs(shift)) for shift in range(1, self.members)],
            axis=0,
        )

    def sum_rows(self, partial):
        parts = partial.reshape((self.members, partial.shape[0] // self.members) + partial.shape[1:])
        total = parts[0]
        for shift in range(1, self.members):
            moved = lax.ppermute(
                parts[shift].astype(jnp.bfloat16), BOTH, self.member_pairs(self.members - shift)
            )
            total = total + moved.astype(jnp.float32)
        return total

    def bases(self, row_count):
        return jnp.stack(
            [(self.member - shift) % self.members * row_count for shift in range(self.members)]
        ).astype(jnp.int32)

    def swap(self, rows, distance, axis="ctx"):
        pairs = [(place, place ^ distance) for place in range(lax.axis_size(axis))]
        return lax.ppermute(rows, axis, pairs)

    def gather_small(self, part):
        held = part[None]
        place = lax.axis_index("exp")
        distance = 1
        while distance < self.exp_count:
            other = self.swap(held, distance, "exp")
            upper = (place // distance) % 2 == 1
            held = jnp.where(
                upper,
                jnp.concatenate([other, held], axis=0),
                jnp.concatenate([held, other], axis=0),
            )
            distance *= 2
        return held

    def sum_cores(self, part):
        rows = part.shape[0] // self.exp_count
        blocks = part.reshape(self.exp_count // 2, 2, rows, part.shape[1])
        sent = lax.dynamic_index_in_dim(blocks, 1 - self.core, 1, keepdims=False)
        kept = lax.dynamic_index_in_dim(blocks, self.core, 1, keepdims=False)
        return add_low([kept, self.swap(sent, 1, "exp")])

    def sum_chips(self, blocks):
        pair = lax.axis_index("exp") // 2
        parts = [lax.dynamic_index_in_dim(blocks, pair, 0, keepdims=False)]
        for step in range(1, self.exp_count // 2):
            block = lax.dynamic_index_in_dim(blocks, pair ^ step, 0, keepdims=False)
            parts.append(self.swap(block, 2 * step, "exp"))
        return add_low(parts)

    def sum_ctx(self, total):
        cuts = total.reshape(self.ctx_count, total.shape[0] // self.ctx_count, total.shape[1])
        parts = [lax.dynamic_index_in_dim(cuts, self.ctx, 0, keepdims=False)]
        for step in range(1, self.ctx_count):
            block = lax.dynamic_index_in_dim(cuts, self.ctx ^ step, 0, keepdims=False)
            parts.append(self.swap(block, step))
        return add_low(parts)

    def spread_ctx(self, own):
        every = jnp.stack([own] + [self.swap(own, step) for step in range(1, self.ctx_count)])
        return jnp.concatenate(
            [
                lax.dynamic_index_in_dim(every, self.ctx ^ place, 0, keepdims=False)
                for place in range(self.ctx_count)
            ],
            axis=0,
        )


def add_low(parts):
    total = parts[0].astype(jnp.float32)
    for part in parts[1:]:
        total = total + part.astype(jnp.float32)
    return total.astype(jnp.bfloat16)


def after(value, *events):
    return lax.optimization_barrier((value,) + events)[0]


def per_device(
    tokens_in,
    first_gain,
    joint_projection,
    out_projection,
    bias_table,
    second_gain,
    router_weight,
    expert_up,
    expert_down,
    expert_index,
    keep_mask,
    buckets,
    cotangent,
):
    layout = Layout()
    shards = layout.exp_count
    seq_count, block_len, model_width = tokens_in.shape
    token_count = seq_count * block_len
    expert_count = router_weight.shape[1]
    bucket_count = bias_table.shape[0] * shards
    head_count = bias_table.shape[1]

    small = [first_gain, second_gain, router_weight, bias_table]
    small_sizes = [part.size for part in small]
    small_cuts = [sum(small_sizes[:place]) for place in range(1, len(small))]
    small_count = sum(small_sizes)
    small_padded = -(-small_count // TILE) * TILE
    small_full = layout.gather_small(
        jnp.pad(
            jnp.concatenate([part.reshape(-1) for part in small]), (0, small_padded - small_count)
        )
    )[:, :small_count]
    gain_one, gain_two, weight_router, table = jnp.split(small_full, small_cuts, axis=1)
    weight_router = weight_router.reshape(model_width, expert_count)
    table = table.reshape(bucket_count, head_count)
    gain_first = gain_one.reshape(model_width).astype(jnp.float32)
    gain_second = gain_two.reshape(model_width).astype(jnp.float32)
    weight_joint = lax.all_gather(joint_projection, "exp", axis=0, tiled=True)
    weight_out = lax.all_gather(out_projection, "exp", axis=0, tiled=True)

    tokens = layout.gather_blocks(tokens_in)
    codes = layout.gather_blocks(expert_index.reshape(seq_count, block_len) * 2 + keep_mask)
    grad_out_low = layout.gather_blocks(cotangent)
    every_token = layout.all_rows(tokens)
    chosen = codes // 2
    kept = codes % 2

    distances = list(range(2, layout.ctx_count, 2))
    held_up, held_down = lax.optimization_barrier((expert_up[0], expert_down[0], grad_out_low))[:2]
    up_moved = [layout.swap(held_up, step) for step in distances]
    down_moved = [layout.swap(held_down, step) for step in distances]

    offset_count = buckets.shape[0]
    bucket_hot = buckets[None, :] == jnp.arange(bucket_count, dtype=jnp.int32)[:, None]
    offset_values = lax.dot_general(
        table,
        bucket_hot.astype(jnp.bfloat16),
        (((0,), (0,)), ((), ())),
        preferred_element_type=jnp.float32,
    )
    skew = make_skew(jnp.pad(offset_values, ((0, 0), (0, 1))))

    is_choice = chosen[:, None] == jnp.arange(expert_count, dtype=jnp.int32)
    most_rows = max(2, (5 * block_len + 4 * expert_count - 1) // (4 * expert_count))
    capacity = seq_count * most_rows
    place = jnp.arange(token_count, dtype=jnp.int32)
    earlier = (place[:, None] >= place[None, :]) & (
        place[:, None] // block_len == place[None, :] // block_len
    )
    running = jnp.dot(
        earlier.astype(jnp.bfloat16),
        is_choice.astype(jnp.bfloat16),
        preferred_element_type=jnp.float32,
    )
    slot_rank = (jnp.sum(running * is_choice.astype(jnp.float32), axis=-1) - 1.0).astype(jnp.int32)
    token_slot = chosen * capacity + place // block_len * most_rows + slot_rank
    slot_hot = (
        (token_slot[:, None] == jnp.arange(expert_count * capacity, dtype=jnp.int32))
        & (kept[:, None] > 0)
    ).astype(jnp.bfloat16)

    def exchange(row_data):
        return lax.all_to_all(
            row_data.reshape(shards, -1, model_width), "exp", split_axis=0, concat_axis=0, tiled=True
        ).reshape(-1, model_width)

    def to_experts(row_data):
        sent = lax.dot_general(
            slot_hot, row_data, (((0,), (0,)), ((), ())), preferred_element_type=jnp.float32
        ).astype(jnp.bfloat16)
        return exchange(sent)

    def sum_halves(own_part, other_part):
        other = layout.swap(other_part, 1)
        return (own_part + other.astype(jnp.float32)).astype(jnp.bfloat16)

    def from_experts(summed):
        return jnp.dot(slot_hot, exchange(summed), preferred_element_type=jnp.float32)

    every_float = every_token.astype(jnp.float32)
    tokens_f = every_float[:token_count]
    normed_one, every_inverse = rms_forward(every_float, gain_first)
    inverse_one = every_inverse[:token_count]
    hidden_one = normed_one.astype(jnp.bfloat16)
    queries = jnp.dot(
        hidden_one[:token_count], weight_joint[:, :model_width], preferred_element_type=jnp.float32
    ).astype(jnp.bfloat16) * jnp.bfloat16(SCORE_SCALE)
    key_values = jnp.dot(
        hidden_one, weight_joint[:, model_width:], preferred_element_type=jnp.float32
    ).astype(jnp.bfloat16)
    grad_own = to_experts(after(grad_out_low, key_values))
    grad_other = layout.swap(grad_own, 1)
    bases = layout.bases(token_count)
    attended, logsum = attend_forward(bases, queries, key_values, skew)
    attended = after(attended, grad_own, *up_moved)
    attended_low = attended.astype(jnp.bfloat16)
    residual = tokens_f + jnp.dot(attended_low, weight_out, preferred_element_type=jnp.float32)
    normed_two, inverse_two = rms_forward(residual, gain_second)
    hidden_two = normed_two.astype(jnp.bfloat16)

    row_own = after(to_experts(hidden_two), grad_other, *down_moved)
    row_other = layout.swap(row_own, 1)
    ups = [expert_up[0]] + up_moved
    downs = [expert_down[0]] + down_moved

    expert_here = jnp.arange(expert_count, dtype=jnp.int32) == lax.axis_index("exp")
    expert_here = expert_here.astype(jnp.float32)[None, :]

    def contract_rows(left, right):
        return lax.dot_general(
            left, right, (((0,), (0,)), ((), ())), preferred_element_type=jnp.float32
        )

    results, grad_inputs = [], []
    grad_router = 0.0
    grad_ups, grad_downs = [0.0] * len(ups), [0.0] * len(ups)
    for rows, grad_rows in ((row_own, grad_own), (row_other, grad_other)):
        logits = jnp.dot(rows, weight_router, preferred_element_type=jnp.float32)
        router_prob = jax.nn.softmax(logits, axis=-1)
        picked = jnp.sum(router_prob * expert_here, axis=-1, keepdims=True)
        grad_float = grad_rows.astype(jnp.float32)
        grad_result = (picked * grad_float).astype(jnp.bfloat16)
        produced, grad_input = 0.0, 0.0
        for part, (matrix_up, matrix_down) in enumerate(zip(ups, downs)):
            before = jnp.dot(rows, matrix_up, preferred_element_type=jnp.float32)
            activated, gelu_back = jax.vjp(jax.nn.gelu, before)
            acted = activated.astype(jnp.bfloat16)
            produced = produced + jnp.dot(acted, matrix_down, preferred_element_type=jnp.float32)
            grad_acted = contract_last(grad_result, matrix_down)
            grad_before = gelu_back(grad_acted)[0].astype(jnp.bfloat16)
            grad_input = grad_input + contract_last(grad_before, matrix_up)
            grad_ups[part] = grad_ups[part] + contract_rows(rows, grad_before)
            grad_downs[part] = grad_downs[part] + contract_rows(acted, grad_result)
        grad_picked = jnp.sum(grad_float * produced, axis=-1, keepdims=True)
        grad_logits = (picked * (expert_here - router_prob) * grad_picked).astype(jnp.bfloat16)
        grad_router = grad_router + contract_rows(rows, grad_logits)
        grad_inputs.append(grad_input + contract_last(grad_logits, weight_router))
        results.append(picked * produced)

    grad_summed = sum_halves(grad_inputs[0], grad_inputs[1].astype(jnp.bfloat16))
    grad_back = from_experts(grad_summed)
    result_other = after(results[1].astype(jnp.bfloat16), grad_summed)
    result_summed = sum_halves(results[0], result_other)

    down_low = [part.astype(jnp.bfloat16) for part in grad_downs[1:]]
    up_low = [part.astype(jnp.bfloat16) for part in grad_ups[1:]]

    def moved(parts):
        return [layout.swap(part, step) for part, step in zip(parts, distances)]

    grads_down_moved = moved(down_low)
    grads_up_moved = moved(up_low)

    def own_slice(own, others):
        total = own
        for other in others:
            total = total + other.astype(jnp.float32)
        return total[None]

    grad_residual, grad_gain_two = rms_backward(residual, inverse_two, gain_second, grad_back)
    grad_residual = grad_residual + grad_out_low.astype(jnp.float32)
    grad_mixed = grad_residual.astype(jnp.bfloat16)
    grad_weight_out = contract_rows(attended_low, grad_mixed)
    grad_attended = contract_last(grad_mixed, weight_out).astype(jnp.bfloat16)
    grad_q, grad_k, grad_v, grad_off = attend_backward(
        bases, queries, grad_attended, attended, key_values, skew, logsum
    )
    grad_k, result_summed = lax.optimization_barrier((grad_k, result_summed))
    layer_rows = residual + from_experts(result_summed)
    layer_sent = layout.return_blocks(layer_rows.astype(jnp.bfloat16))

    grad_kv = jnp.concatenate([grad_k, grad_v], axis=1)
    kv_out_part = jnp.concatenate(
        [
            contract_rows(hidden_one, grad_kv).astype(jnp.bfloat16),
            grad_weight_out.astype(jnp.bfloat16),
        ],
        axis=1,
    )
    kv_out_cores = layout.sum_cores(kv_out_part)
    partial_one = contract_last(grad_kv, weight_joint[:, model_width:])
    partial_own = contract_last(grad_q, weight_joint[:, :model_width])
    every_normed = every_float * every_inverse
    grad_gain_one = jnp.sum(partial_one * every_normed, axis=0) + jnp.sum(
        partial_own * every_normed[:token_count], axis=0
    )
    grad_hidden_one = layout.sum_rows(partial_one) + partial_own
    grad_hidden_one, *grads_down_moved = lax.optimization_barrier(
        (grad_hidden_one, *grads_down_moved)
    )
    grad_expert_down = own_slice(grad_downs[0], grads_down_moved)
    kv_out_chips = layout.sum_chips(after(kv_out_cores, layer_rows, grad_hidden_one))
    grad_input_norm, _ = rms_backward(tokens_f, inverse_one, gain_first, grad_hidden_one)
    tokens_sent = layout.return_blocks((grad_input_norm + grad_residual).astype(jnp.bfloat16))
    query_part = contract_rows(hidden_one[:token_count], grad_q).astype(jnp.bfloat16)
    grad_table = jnp.dot(
        bucket_hot.astype(jnp.float32),
        grad_off.reshape(head_count, -1)[:, :offset_count].T,
        precision=HIGHEST,
    )
    small_grads = [grad_gain_one, grad_gain_two, grad_router, grad_table]
    shard_rows = joint_projection.shape[0]
    side_width = -(-small_count // (shard_rows * TILE)) * TILE
    small_grads = jnp.concatenate([part.reshape(shards, -1) for part in small_grads], axis=1)
    small_grads = jnp.pad(small_grads, ((0, 0), (0, shard_rows * side_width - small_count)))
    side = small_grads.reshape(shards * shard_rows, side_width).astype(jnp.bfloat16)
    query_cores = layout.sum_cores(jnp.concatenate([query_part, side], axis=1))
    kv_out_chips, query_cores, *grads_up_moved = lax.optimization_barrier(
        (kv_out_chips, query_cores, *grads_up_moved)
    )
    grad_expert_up = own_slice(grad_ups[0], grads_up_moved)
    kv_out_own = layout.sum_ctx(kv_out_chips)
    query_chips = layout.sum_chips(query_cores)
    kv_out_own, query_chips = lax.optimization_barrier((kv_out_own, query_chips))
    kv_out_sum = layout.spread_ctx(kv_out_own)
    query_own = layout.sum_ctx(query_chips)
    kv_out_sum, query_own = lax.optimization_barrier((kv_out_sum, query_own))
    query_sum = layout.spread_ctx(query_own)
    layer_out = layout.place_blocks([after(part, kv_out_own) for part in layer_sent])
    grad_tokens = layout.place_blocks([after(part, kv_out_sum) for part in tokens_sent]).astype(
        jnp.float32
    )
    kv_sum = kv_out_sum[:, : 2 * model_width]
    out_sum = kv_out_sum[:, 2 * model_width :]
    side_sum = query_sum[:, model_width:].reshape(-1)[:small_count].astype(jnp.float32)
    joint_sum = jnp.concatenate([query_sum[:, :model_width], kv_sum], axis=1)
    sum_gain_one, sum_gain_two, sum_router, sum_table = jnp.split(side_sum, small_cuts)
    return (
        layer_out,
        grad_tokens,
        sum_gain_one,
        joint_sum.astype(jnp.float32),
        out_sum.astype(jnp.float32),
        sum_table.reshape(bias_table.shape),
        sum_gain_two,
        sum_router.reshape(router_weight.shape),
        grad_expert_up,
        grad_expert_down,
    )


def solution(mesh):
    in_specs = (
        P("exp", "ctx", None),
        P("exp"),
        P("exp", None),
        P("exp", None),
        P("exp", None),
        P("exp"),
        P("exp", None),
        P("exp", None, "ctx"),
        P("exp", "ctx", None),
        P("exp", "ctx", None),
        P("exp", "ctx"),
        P(),
        P("exp", "ctx", None),
    )
    out_specs = (
        P("exp", "ctx", None),
        P("exp", "ctx", None),
        P("exp"),
        P("exp", None),
        P("exp", None),
        P("exp", None),
        P("exp"),
        P("exp", None),
        P("exp", None, "ctx"),
        P("exp", "ctx", None),
    )
    return jax.shard_map(
        per_device, mesh=mesh, in_specs=in_specs, out_specs=out_specs, check_vma=False
    )
```

```python
import functools

import jax
import jax.numpy as jnp
from jax import lax
from jax.experimental import pallas as pl
from jax.experimental.pallas import tpu as pltpu
from jax.sharding import PartitionSpec as P

EPSILON = 1e-06
HALF = 64
TILE = 128
GROUP = 256
VMEM_BYTES = 50 * 1024 * 1024
SCORE_SCALE = 0.125
HIGHEST = lax.Precision.HIGHEST
BOTH = ("ctx", "exp")


def contract_last(left, right):
    return lax.dot_general(
        left, right, (((1,), (1,)), ((), ())), preferred_element_type=jnp.float32
    )


def matmul(left, right):
    return lax.dot_general(
        left, right, (((1,), (0,)), ((), ())), preferred_element_type=jnp.float32
    )


def skew_kernel(offset_ref, skew_ref):
    padded = offset_ref.shape[-1]
    kept = skew_ref.shape[1]
    rows = jnp.broadcast_to(offset_ref[0], (TILE, padded))
    rolled = pltpu.roll(rows, padded - (TILE - 1), 1, stride=1, stride_axis=0)
    skew_ref[0] = rolled[:, :kept].T.astype(skew_ref.dtype)


def make_skew(offset_values):
    head_count, padded = offset_values.shape
    kept = padded - TILE
    return pl.pallas_call(
        skew_kernel,
        grid=(head_count,),
        in_specs=[pl.BlockSpec((1, 1, padded), lambda h: (h, 0, 0))],
        out_specs=pl.BlockSpec((1, kept, TILE), lambda h: (h, 0, 0)),
        out_shape=jax.ShapeDtypeStruct((head_count, kept, TILE), jnp.bfloat16),
        compiler_params=pltpu.CompilerParams(vmem_limit_bytes=VMEM_BYTES),
        name="skew_bias",
    )(offset_values.reshape(head_count, 1, padded))


def half_mask(rows, half):
    lanes = lax.broadcasted_iota(jnp.int32, (rows, TILE), 1)
    return (lanes // HALF) == half


def bias_rows(key_base, query_base, seq_len):
    return key_base - query_base + seq_len - TILE


def forward_kernel(
    base_ref, q_ref, k_ref, v_ref, skew_ref, out_ref, lse_ref, score_ref, prob_ref, *, chunk
):
    query_rows = q_ref.shape[0]
    key_rows = k_ref.shape[0]
    seq_len = key_rows
    mask = [half_mask(GROUP, 0), half_mask(GROUP, 1)]
    value_t = v_ref[...].T
    for group in range(query_rows // GROUP):
        rows = slice(group * GROUP, (group + 1) * GROUP)
        query_base = base_ref[0] + group * GROUP
        halves = []
        for half in range(2):
            queries = jnp.where(mask[half], q_ref[rows], 0).astype(jnp.bfloat16)
            score_ref[half] = contract_last(k_ref[...], queries)
            top = jnp.full((8, GROUP), -jnp.inf, jnp.float32)
            for start in range(0, key_rows, chunk):
                key_base = base_ref[start // query_rows] + start % query_rows
                place = pl.multiple_of(bias_rows(key_base, query_base, seq_len), TILE)
                left = skew_ref[half, pl.ds(place, chunk), :]
                right = skew_ref[half, pl.ds(place - TILE, chunk), :]
                bias = jnp.concatenate([left, right], axis=1).astype(jnp.float32)
                piece = score_ref[half, start : start + chunk] + bias
                score_ref[half, start : start + chunk] = piece
                top = jnp.maximum(top, jnp.max(piece.reshape(chunk // 8, 8, GROUP), axis=0))
            top = jnp.max(top, axis=0, keepdims=True)
            total = jnp.zeros((8, GROUP), jnp.float32)
            for start in range(0, key_rows, chunk):
                piece = jnp.exp(score_ref[half, start : start + chunk] - top)
                total = total + jnp.sum(piece.reshape(chunk // 8, 8, GROUP), axis=0)
                prob_ref[half, start : start + chunk] = piece.astype(jnp.bfloat16)
            total = jnp.sum(total, axis=0, keepdims=True)
            lse_ref[0, half : half + 1, rows] = top + jnp.log(total)
            mixed = matmul(value_t[half * HALF : (half + 1) * HALF], prob_ref[half])
            halves.append(mixed / total)
        out_ref[rows] = jnp.concatenate(halves, axis=0).T


def attend_forward(bases, queries, key_values, skew):
    query_rows, width = queries.shape
    key_rows = key_values.shape[0]
    kept = skew.shape[1]
    pairs = width // TILE
    chunk = TILE
    return pl.pallas_call(
        functools.partial(forward_kernel, chunk=chunk),
        grid_spec=pltpu.PrefetchScalarGridSpec(
            num_scalar_prefetch=1,
            grid=(pairs,),
            in_specs=[
                pl.BlockSpec((query_rows, TILE), lambda p, _: (0, p)),
                pl.BlockSpec((key_rows, TILE), lambda p, _: (0, p)),
                pl.BlockSpec((key_rows, TILE), lambda p, _: (0, p + pairs)),
                pl.BlockSpec((2, kept, TILE), lambda p, _: (p, 0, 0)),
            ],
            out_specs=[
                pl.BlockSpec((query_rows, TILE), lambda p, _: (0, p)),
                pl.BlockSpec((1, 2, query_rows), lambda p, _: (p, 0, 0)),
            ],
            scratch_shapes=[
                pltpu.VMEM((2, key_rows, GROUP), jnp.float32),
                pltpu.VMEM((2, key_rows, GROUP), jnp.bfloat16),
            ],
        ),
        out_shape=[
            jax.ShapeDtypeStruct((query_rows, width), jnp.float32),
            jax.ShapeDtypeStruct((pairs, 2, query_rows), jnp.float32),
        ],
        compiler_params=pltpu.CompilerParams(vmem_limit_bytes=VMEM_BYTES),
        name="attend_forward",
    )(bases, queries, key_values, key_values, skew)


def backward_kernel(
    base_ref, q_ref, do_ref, o_ref, k_ref, v_ref, skew_ref, lse_ref,
    dq_ref, dk_ref, dv_ref, off_ref,
    score_ref, gradp_ref, prob_ref, grads_ref, accum_k, accum_v, accum_skew,
    *, chunk,
):
    query_rows = q_ref.shape[0]
    key_rows = k_ref.shape[0]
    seq_len = key_rows
    mask = [half_mask(GROUP, 0), half_mask(GROUP, 1)]
    key_t = k_ref[...].T
    accum_skew[...] = jnp.zeros_like(accum_skew)
    for group in range(query_rows // GROUP):
        rows = slice(group * GROUP, (group + 1) * GROUP)
        query_base = base_ref[0] + group * GROUP
        product = (do_ref[rows].astype(jnp.float32) * o_ref[rows]).T
        halves = []
        sum_k = None
        for half in range(2):
            queries = jnp.where(mask[half], q_ref[rows], 0).astype(jnp.bfloat16)
            grads_out = jnp.where(mask[half], do_ref[rows], 0).astype(jnp.bfloat16)
            score_ref[half] = contract_last(k_ref[...], queries)
            gradp_ref[half] = contract_last(v_ref[...], grads_out)
            logsum = lse_ref[0, half : half + 1, rows]
            delta = jnp.sum(product[half * HALF : (half + 1) * HALF], axis=0, keepdims=True)
            for start in range(0, key_rows, chunk):
                key_base = base_ref[start // query_rows] + start % query_rows
                place = pl.multiple_of(bias_rows(key_base, query_base, seq_len), TILE)
                here = pl.ds(start, chunk)
                left = skew_ref[half, pl.ds(place, chunk), :]
                right = skew_ref[half, pl.ds(place - TILE, chunk), :]
                bias = jnp.concatenate([left, right], axis=1).astype(jnp.float32)
                prob = jnp.exp(score_ref[half, here] + bias - logsum)
                grads = prob * (gradp_ref[half, here] - delta)
                prob_ref[half, here] = prob.astype(jnp.bfloat16)
                grads_ref[half, here] = grads.astype(jnp.bfloat16)
                accum_skew[half, pl.ds(place, chunk), :] += grads[:, :TILE]
                accum_skew[half, pl.ds(place - TILE, chunk), :] += grads[:, TILE:]
            part_k = matmul(grads_ref[half], queries)
            part_v = matmul(prob_ref[half], grads_out)
            sum_k = part_k if sum_k is None else sum_k + part_k
            sum_v = part_v if half == 0 else sum_v + part_v
            halves.append(matmul(key_t[half * HALF : (half + 1) * HALF], grads_ref[half]))
        if group == 0:
            accum_k[...] = sum_k
            accum_v[...] = sum_v
        else:
            accum_k[...] += sum_k
            accum_v[...] += sum_v
        dq_ref[rows] = (jnp.concatenate(halves, axis=0) * 0.125).T.astype(dq_ref.dtype)
    dk_ref[...] = accum_k[...].astype(dk_ref.dtype)
    dv_ref[...] = accum_v[...].astype(dv_ref.dtype)
    for half in range(2):
        turned = accum_skew[half].T
        padded = turned.shape[1]
        count = TILE // 2
        while count:
            turned = turned[:count] + pltpu.roll(turned[count : 2 * count], padded - count, 1)
            count //= 2
        off_ref[0, half : half + 1] = pltpu.roll(turned, TILE - 1, 1)


def attend_backward(bases, queries, grads_out, outputs, key_values, skew, logsum):
    query_rows, width = queries.shape
    key_rows = key_values.shape[0]
    kept = skew.shape[1]
    pairs = width // TILE
    chunk = TILE
    column = lambda count: pl.BlockSpec((count, TILE), lambda p, _: (0, p))
    return pl.pallas_call(
        functools.partial(backward_kernel, chunk=chunk),
        grid_spec=pltpu.PrefetchScalarGridSpec(
            num_scalar_prefetch=1,
            grid=(pairs,),
            in_specs=[
                column(query_rows), column(query_rows), column(query_rows),
                column(key_rows),
                pl.BlockSpec((key_rows, TILE), lambda p, _: (0, p + pairs)),
                pl.BlockSpec((2, kept, TILE), lambda p, _: (p, 0, 0)),
                pl.BlockSpec((1, 2, query_rows), lambda p, _: (p, 0, 0)),
            ],
            out_specs=[
                column(query_rows), column(key_rows), column(key_rows),
                pl.BlockSpec((1, 2, kept + TILE), lambda p, _: (p, 0, 0)),
            ],
            scratch_shapes=[
                pltpu.VMEM((2, key_rows, GROUP), jnp.float32),
                pltpu.VMEM((2, key_rows, GROUP), jnp.float32),
                pltpu.VMEM((2, key_rows, GROUP), jnp.bfloat16),
                pltpu.VMEM((2, key_rows, GROUP), jnp.bfloat16),
                pltpu.VMEM((key_rows, TILE), jnp.float32),
                pltpu.VMEM((key_rows, TILE), jnp.float32),
                pltpu.VMEM((2, kept + TILE, TILE), jnp.float32),
            ],
        ),
        out_shape=[
            jax.ShapeDtypeStruct((query_rows, width), jnp.bfloat16),
            jax.ShapeDtypeStruct((key_rows, width), jnp.bfloat16),
            jax.ShapeDtypeStruct((key_rows, width), jnp.bfloat16),
            jax.ShapeDtypeStruct((pairs, 2, kept + TILE), jnp.float32),
        ],
        compiler_params=pltpu.CompilerParams(vmem_limit_bytes=VMEM_BYTES),
        name="attend_backward",
    )(bases, queries, grads_out, outputs, key_values, key_values, skew, logsum)


def rms_forward(row_data, gain_vec):
    inverse = lax.rsqrt(jnp.mean(row_data * row_data, axis=-1, keepdims=True) + EPSILON)
    return (row_data * inverse * gain_vec, inverse)


def rms_backward(row_data, inverse, gain_vec, grad_out):
    normed = row_data * inverse
    grad_gain = jnp.sum(grad_out * normed, axis=0)
    scaled = grad_out * gain_vec
    spread = jnp.mean(scaled * normed, axis=-1, keepdims=True)
    return (inverse * (scaled - normed * spread), grad_gain)


class Layout:
    def __init__(self):
        self.ctx_count = lax.axis_size("ctx")
        self.exp_count = lax.axis_size("exp")
        self.span = self.ctx_count // 4
        self.members = 2 * self.span
        self.ctx = lax.axis_index("ctx")
        self.core = lax.axis_index("exp") % 2
        self.member = (self.ctx % self.span) * 2 + self.core
        self.side = (self.ctx // self.span) % 2

    def number(self, ctx, exp):
        return ctx * self.exp_count + exp

    def round_pairs(self, turn):
        pairs = []
        for ctx in range(self.ctx_count):
            for exp in range(self.exp_count):
                seq = 2 * (exp % 2) + (turn + ctx) % 2
                member = ctx // 2
                target = self.number(seq * self.span + member // 2, exp // 2 * 2 + member % 2)
                pairs.append((self.number(ctx, exp), target))
        return pairs

    def member_pairs(self, shift):
        pairs = []
        for ctx in range(self.ctx_count):
            for exp in range(self.exp_count):
                start = ctx // self.span * self.span
                member = ((ctx - start) * 2 + exp % 2 + shift) % self.members
                target = self.number(start + member // 2, exp // 2 * 2 + member % 2)
                pairs.append((self.number(ctx, exp), target))
        return pairs

    def gather_blocks(self, blocks):
        got = [
            lax.ppermute(
                lax.dynamic_index_in_dim(blocks, (turn + self.ctx) % 2, 0, keepdims=False),
                BOTH,
                self.round_pairs(turn),
            )
            for turn in range(2)
        ]
        first = jnp.where(self.side == 0, got[0], got[1])
        second = jnp.where(self.side == 0, got[1], got[0])
        return jnp.concatenate([first, second], axis=0)

    def return_blocks(self, rows):
        blocks = rows.reshape((2, rows.shape[0] // 2) + rows.shape[1:])
        got = [
            lax.ppermute(
                lax.dynamic_index_in_dim(blocks, (turn + self.side) % 2, 0, keepdims=False),
                BOTH,
                [(target, source) for source, target in self.round_pairs(turn)],
            )
            for turn in range(2)
        ]
        return got

    def place_blocks(self, got):
        even = self.ctx % 2 == 0
        return jnp.stack([jnp.where(even, got[0], got[1]), jnp.where(even, got[1], got[0])])

    def all_rows(self, rows):
        return jnp.concatenate(
            [rows]
            + [lax.ppermute(rows, BOTH, self.member_pairs(shift)) for shift in range(1, self.members)],
            axis=0,
        )

    def sum_rows(self, partial):
        parts = partial.reshape((self.members, partial.shape[0] // self.members) + partial.shape[1:])
        total = parts[0]
        for shift in range(1, self.members):
            moved = lax.ppermute(
                parts[shift].astype(jnp.bfloat16), BOTH, self.member_pairs(self.members - shift)
            )
            total = total + moved.astype(jnp.float32)
        return total

    def bases(self, row_count):
        return jnp.stack(
            [(self.member - shift) % self.members * row_count for shift in range(self.members)]
        ).astype(jnp.int32)

    def swap(self, rows, distance, axis="ctx"):
        pairs = [(place, place ^ distance) for place in range(lax.axis_size(axis))]
        return lax.ppermute(rows, axis, pairs)

    def gather_small(self, part):
        held = part[None]
        place = lax.axis_index("exp")
        distance = 1
        while distance < self.exp_count:
            other = self.swap(held, distance, "exp")
            upper = (place // distance) % 2 == 1
            held = jnp.where(
                upper,
                jnp.concatenate([other, held], axis=0),
                jnp.concatenate([held, other], axis=0),
            )
            distance *= 2
        return held

    def sum_cores(self, part):
        rows = part.shape[0] // self.exp_count
        blocks = part.reshape(self.exp_count // 2, 2, rows, part.shape[1])
        sent = lax.dynamic_index_in_dim(blocks, 1 - self.core, 1, keepdims=False)
        kept = lax.dynamic_index_in_dim(blocks, self.core, 1, keepdims=False)
        return add_low([kept, self.swap(sent, 1, "exp")])

    def sum_chips(self, blocks):
        pair = lax.axis_index("exp") // 2
        parts = [lax.dynamic_index_in_dim(blocks, pair, 0, keepdims=False)]
        for step in range(1, self.exp_count // 2):
            block = lax.dynamic_index_in_dim(blocks, pair ^ step, 0, keepdims=False)
            parts.append(self.swap(block, 2 * step, "exp"))
        return add_low(parts)

    def sum_ctx(self, total):
        cuts = total.reshape(self.ctx_count, total.shape[0] // self.ctx_count, total.shape[1])
        parts = [lax.dynamic_index_in_dim(cuts, self.ctx, 0, keepdims=False)]
        for step in range(1, self.ctx_count):
            block = lax.dynamic_index_in_dim(cuts, self.ctx ^ step, 0, keepdims=False)
            parts.append(self.swap(block, step))
        return add_low(parts)

    def spread_ctx(self, own):
        every = jnp.stack([own] + [self.swap(own, step) for step in range(1, self.ctx_count)])
        return jnp.concatenate(
            [
                lax.dynamic_index_in_dim(every, self.ctx ^ place, 0, keepdims=False)
                for place in range(self.ctx_count)
            ],
            axis=0,
        )


def add_low(parts):
    total = parts[0].astype(jnp.float32)
    for part in parts[1:]:
        total = total + part.astype(jnp.float32)
    return total.astype(jnp.bfloat16)


def after(value, *events):
    return lax.optimization_barrier((value,) + events)[0]


def per_device(
    tokens_in,
    first_gain,
    joint_projection,
    out_projection,
    bias_table,
    second_gain,
    router_weight,
    expert_up,
    expert_down,
    expert_index,
    keep_mask,
    buckets,
    cotangent,
):
    layout = Layout()
    shards = layout.exp_count
    seq_count, block_len, model_width = tokens_in.shape
    token_count = seq_count * block_len
    expert_count = router_weight.shape[1]
    bucket_count = bias_table.shape[0] * shards
    head_count = bias_table.shape[1]

    small = [first_gain, second_gain, router_weight, bias_table]
    small_sizes = [part.size for part in small]
    small_cuts = [sum(small_sizes[:place]) for place in range(1, len(small))]
    small_count = sum(small_sizes)
    small_padded = -(-small_count // TILE) * TILE
    small_full = layout.gather_small(
        jnp.pad(
            jnp.concatenate([part.reshape(-1) for part in small]), (0, small_padded - small_count)
        )
    )[:, :small_count]
    gain_one, gain_two, weight_router, table = jnp.split(small_full, small_cuts, axis=1)
    weight_router = weight_router.reshape(model_width, expert_count)
    table = table.reshape(bucket_count, head_count)
    gain_first = gain_one.reshape(model_width).astype(jnp.float32)
    gain_second = gain_two.reshape(model_width).astype(jnp.float32)
    weight_joint = lax.all_gather(joint_projection, "exp", axis=0, tiled=True)
    weight_out = lax.all_gather(out_projection, "exp", axis=0, tiled=True)

    tokens = layout.gather_blocks(tokens_in)
    codes = layout.gather_blocks(expert_index.reshape(seq_count, block_len) * 2 + keep_mask)
    grad_out_low = layout.gather_blocks(cotangent)
    every_token = layout.all_rows(tokens)
    chosen = codes // 2
    kept = codes % 2

    distances = list(range(2, layout.ctx_count, 2))
    held_up = after(expert_up[0], tokens)
    held_down = after(expert_down[0], grad_out_low)
    up_moved = [layout.swap(held_up, step) for step in distances]
    down_moved = [layout.swap(held_down, step) for step in distances]

    offset_count = buckets.shape[0]
    bucket_hot = buckets[None, :] == jnp.arange(bucket_count, dtype=jnp.int32)[:, None]
    offset_values = lax.dot_general(
        table,
        bucket_hot.astype(jnp.bfloat16),
        (((0,), (0,)), ((), ())),
        preferred_element_type=jnp.float32,
    )
    skew = make_skew(jnp.pad(offset_values, ((0, 0), (0, 1))))

    is_choice = chosen[:, None] == jnp.arange(expert_count, dtype=jnp.int32)
    most_rows = max(2, (5 * block_len + 4 * expert_count - 1) // (4 * expert_count))
    capacity = seq_count * most_rows
    place = jnp.arange(token_count, dtype=jnp.int32)
    earlier = (place[:, None] >= place[None, :]) & (
        place[:, None] // block_len == place[None, :] // block_len
    )
    running = jnp.dot(
        earlier.astype(jnp.bfloat16),
        is_choice.astype(jnp.bfloat16),
        preferred_element_type=jnp.float32,
    )
    slot_rank = (jnp.sum(running * is_choice.astype(jnp.float32), axis=-1) - 1.0).astype(jnp.int32)
    token_slot = chosen * capacity + place // block_len * most_rows + slot_rank
    slot_hot = (
        (token_slot[:, None] == jnp.arange(expert_count * capacity, dtype=jnp.int32))
        & (kept[:, None] > 0)
    ).astype(jnp.bfloat16)

    def exchange(row_data):
        return lax.all_to_all(
            row_data.reshape(shards, -1, model_width), "exp", split_axis=0, concat_axis=0, tiled=True
        ).reshape(-1, model_width)

    def to_experts(row_data):
        sent = lax.dot_general(
            slot_hot, row_data, (((0,), (0,)), ((), ())), preferred_element_type=jnp.float32
        ).astype(jnp.bfloat16)
        return exchange(sent)

    def sum_halves(own_part, other_part):
        other = layout.swap(other_part, 1)
        return (own_part + other.astype(jnp.float32)).astype(jnp.bfloat16)

    def from_experts(summed):
        return jnp.dot(slot_hot, exchange(summed), preferred_element_type=jnp.float32)

    every_float = every_token.astype(jnp.float32)
    tokens_f = every_float[:token_count]
    normed_one, every_inverse = rms_forward(every_float, gain_first)
    inverse_one = every_inverse[:token_count]
    hidden_one = normed_one.astype(jnp.bfloat16)
    queries = jnp.dot(
        hidden_one[:token_count], weight_joint[:, :model_width], preferred_element_type=jnp.float32
    ).astype(jnp.bfloat16) * jnp.bfloat16(SCORE_SCALE)
    key_values = jnp.dot(
        hidden_one, weight_joint[:, model_width:], preferred_element_type=jnp.float32
    ).astype(jnp.bfloat16)
    grad_own = to_experts(after(grad_out_low, key_values))
    grad_other = layout.swap(grad_own, 1)
    bases = layout.bases(token_count)
    attended, logsum = attend_forward(bases, queries, key_values, skew)
    attended = after(attended, grad_own, *up_moved)
    attended_low = attended.astype(jnp.bfloat16)
    residual = tokens_f + jnp.dot(attended_low, weight_out, preferred_element_type=jnp.float32)
    normed_two, inverse_two = rms_forward(residual, gain_second)
    hidden_two = normed_two.astype(jnp.bfloat16)

    row_own = after(to_experts(hidden_two), grad_other, *down_moved)
    row_other = layout.swap(row_own, 1)
    ups = [expert_up[0]] + up_moved
    downs = [expert_down[0]] + down_moved

    expert_here = jnp.arange(expert_count, dtype=jnp.int32) == lax.axis_index("exp")
    expert_here = expert_here.astype(jnp.float32)[None, :]

    def contract_rows(left, right):
        return lax.dot_general(
            left, right, (((0,), (0,)), ((), ())), preferred_element_type=jnp.float32
        )

    results, grad_inputs = [], []
    grad_router = 0.0
    grad_ups, grad_downs = [0.0] * len(ups), [0.0] * len(ups)
    for rows, grad_rows in ((row_own, grad_own), (row_other, grad_other)):
        logits = jnp.dot(rows, weight_router, preferred_element_type=jnp.float32)
        router_prob = jax.nn.softmax(logits, axis=-1)
        picked = jnp.sum(router_prob * expert_here, axis=-1, keepdims=True)
        grad_float = grad_rows.astype(jnp.float32)
        grad_result = (picked * grad_float).astype(jnp.bfloat16)
        produced, grad_input = 0.0, 0.0
        for part, (matrix_up, matrix_down) in enumerate(zip(ups, downs)):
            before = jnp.dot(rows, matrix_up, preferred_element_type=jnp.float32)
            activated, gelu_back = jax.vjp(jax.nn.gelu, before)
            acted = activated.astype(jnp.bfloat16)
            produced = produced + jnp.dot(acted, matrix_down, preferred_element_type=jnp.float32)
            grad_acted = contract_last(grad_result, matrix_down)
            grad_before = gelu_back(grad_acted)[0].astype(jnp.bfloat16)
            grad_input = grad_input + contract_last(grad_before, matrix_up)
            grad_ups[part] = grad_ups[part] + contract_rows(rows, grad_before)
            grad_downs[part] = grad_downs[part] + contract_rows(acted, grad_result)
        grad_picked = jnp.sum(grad_float * produced, axis=-1, keepdims=True)
        grad_logits = (picked * (expert_here - router_prob) * grad_picked).astype(jnp.bfloat16)
        grad_router = grad_router + contract_rows(rows, grad_logits)
        grad_inputs.append(grad_input + contract_last(grad_logits, weight_router))
        results.append(picked * produced)

    grad_summed = sum_halves(grad_inputs[0], grad_inputs[1].astype(jnp.bfloat16))
    grad_back = from_experts(grad_summed)
    result_other = after(results[1].astype(jnp.bfloat16), grad_summed)
    result_summed = sum_halves(results[0], result_other)

    down_low = [after(part.astype(jnp.bfloat16), grad_summed) for part in grad_downs[1:]]
    up_low = [after(part.astype(jnp.bfloat16), grad_summed) for part in grad_ups[1:]]

    def moved(parts):
        return [layout.swap(part, step) for part, step in zip(parts, distances)]

    grads_down_moved = moved(down_low)
    grads_up_moved = moved(up_low)

    def own_slice(own, others):
        total = own
        for other in others:
            total = total + other.astype(jnp.float32)
        return total[None]

    grad_residual, grad_gain_two = rms_backward(residual, inverse_two, gain_second, grad_back)
    grad_residual = grad_residual + grad_out_low.astype(jnp.float32)
    grad_mixed = grad_residual.astype(jnp.bfloat16)
    grad_weight_out = contract_rows(attended_low, grad_mixed)
    grad_attended = contract_last(grad_mixed, weight_out).astype(jnp.bfloat16)
    grad_q, grad_k, grad_v, grad_off = attend_backward(
        bases, queries, grad_attended, attended, key_values, skew, logsum
    )
    grad_k, result_summed = lax.optimization_barrier((grad_k, result_summed))
    layer_rows = residual + from_experts(result_summed)
    layer_sent = layout.return_blocks(layer_rows.astype(jnp.bfloat16))

    grad_kv = jnp.concatenate([grad_k, grad_v], axis=1)
    kv_out_part = jnp.concatenate(
        [
            contract_rows(hidden_one, grad_kv).astype(jnp.bfloat16),
            grad_weight_out.astype(jnp.bfloat16),
        ],
        axis=1,
    )
    kv_out_cores = layout.sum_cores(kv_out_part)
    partial_one = contract_last(after(grad_kv, kv_out_part), weight_joint[:, model_width:])
    partial_own = contract_last(grad_q, weight_joint[:, :model_width])
    every_normed = every_float * every_inverse
    grad_gain_one = jnp.sum(partial_one * every_normed, axis=0) + jnp.sum(
        partial_own * every_normed[:token_count], axis=0
    )
    grad_hidden_one = layout.sum_rows(partial_one) + partial_own
    kv_out_chips = layout.sum_chips(after(kv_out_cores, layer_rows, partial_own))
    grad_input_norm, _ = rms_backward(tokens_f, inverse_one, gain_first, grad_hidden_one)
    tokens_sent = layout.return_blocks((grad_input_norm + grad_residual).astype(jnp.bfloat16))
    query_part = contract_rows(hidden_one[:token_count], grad_q).astype(jnp.bfloat16)
    grad_table = jnp.dot(
        bucket_hot.astype(jnp.float32),
        grad_off.reshape(head_count, -1)[:, :offset_count].T,
        precision=HIGHEST,
    )
    small_grads = [grad_gain_one, grad_gain_two, grad_router, grad_table]
    shard_rows = joint_projection.shape[0]
    side_width = -(-small_count // (shard_rows * TILE)) * TILE
    small_grads = jnp.concatenate([part.reshape(shards, -1) for part in small_grads], axis=1)
    small_grads = jnp.pad(small_grads, ((0, 0), (0, shard_rows * side_width - small_count)))
    side = small_grads.reshape(shards * shard_rows, side_width).astype(jnp.bfloat16)
    query_cores = layout.sum_cores(jnp.concatenate([query_part, side], axis=1))
    kv_out_chips, query_cores, grads_down_moved, grads_up_moved = lax.optimization_barrier(
        (kv_out_chips, query_cores, grads_down_moved, grads_up_moved)
    )
    grad_expert_down = own_slice(grad_downs[0], grads_down_moved)
    kv_out_own = layout.sum_ctx(kv_out_chips)
    query_chips = layout.sum_chips(query_cores)
    kv_out_own, query_chips = lax.optimization_barrier((kv_out_own, query_chips))
    kv_out_sum = layout.spread_ctx(kv_out_own)
    query_own = layout.sum_ctx(query_chips)
    kv_out_sum, query_own = lax.optimization_barrier((kv_out_sum, query_own))
    grad_expert_up = own_slice(grad_ups[0], grads_up_moved)
    query_sum = layout.spread_ctx(query_own)
    layer_out = layout.place_blocks([after(part, kv_out_own) for part in layer_sent])
    grad_tokens = layout.place_blocks([after(part, kv_out_sum) for part in tokens_sent]).astype(
        jnp.float32
    )
    kv_sum = kv_out_sum[:, : 2 * model_width]
    out_sum = kv_out_sum[:, 2 * model_width :]
    side_sum = query_sum[:, model_width:].reshape(-1)[:small_count].astype(jnp.float32)
    joint_sum = jnp.concatenate([query_sum[:, :model_width], kv_sum], axis=1)
    sum_gain_one, sum_gain_two, sum_router, sum_table = jnp.split(side_sum, small_cuts)
    return (
        layer_out,
        grad_tokens,
        sum_gain_one,
        joint_sum.astype(jnp.float32),
        out_sum.astype(jnp.float32),
        sum_table.reshape(bias_table.shape),
        sum_gain_two,
        sum_router.reshape(router_weight.shape),
        grad_expert_up,
        grad_expert_down,
    )


def solution(mesh):
    in_specs = (
        P("exp", "ctx", None),
        P("exp"),
        P("exp", None),
        P("exp", None),
        P("exp", None),
        P("exp"),
        P("exp", None),
        P("exp", None, "ctx"),
        P("exp", "ctx", None),
        P("exp", "ctx", None),
        P("exp", "ctx"),
        P(),
        P("exp", "ctx", None),
    )
    out_specs = (
        P("exp", "ctx", None),
        P("exp", "ctx", None),
        P("exp"),
        P("exp", None),
        P("exp", None),
        P("exp", None),
        P("exp"),
        P("exp", None),
        P("exp", None, "ctx"),
        P("exp", "ctx", None),
    )
    return jax.shard_map(
        per_device, mesh=mesh, in_specs=in_specs, out_specs=out_specs, check_vma=False
    )
```

```python
import functools

import jax
import jax.numpy as jnp
from jax import lax
from jax.experimental import pallas as pl
from jax.experimental.pallas import tpu as pltpu
from jax.sharding import PartitionSpec as P

EPSILON = 1e-06
HALF = 64
TILE = 128
GROUP = 256
VMEM_BYTES = 50 * 1024 * 1024
SCORE_SCALE = 0.125
HIGHEST = lax.Precision.HIGHEST
BOTH = ("ctx", "exp")


def contract_last(left, right):
    return lax.dot_general(
        left, right, (((1,), (1,)), ((), ())), preferred_element_type=jnp.float32
    )


def matmul(left, right):
    return lax.dot_general(
        left, right, (((1,), (0,)), ((), ())), preferred_element_type=jnp.float32
    )


def skew_kernel(offset_ref, skew_ref):
    padded = offset_ref.shape[-1]
    kept = skew_ref.shape[1]
    rows = jnp.broadcast_to(offset_ref[0], (TILE, padded))
    rolled = pltpu.roll(rows, padded - (TILE - 1), 1, stride=1, stride_axis=0)
    skew_ref[0] = rolled[:, :kept].T.astype(skew_ref.dtype)


def make_skew(offset_values):
    head_count, padded = offset_values.shape
    kept = padded - TILE
    return pl.pallas_call(
        skew_kernel,
        grid=(head_count,),
        in_specs=[pl.BlockSpec((1, 1, padded), lambda h: (h, 0, 0))],
        out_specs=pl.BlockSpec((1, kept, TILE), lambda h: (h, 0, 0)),
        out_shape=jax.ShapeDtypeStruct((head_count, kept, TILE), jnp.bfloat16),
        compiler_params=pltpu.CompilerParams(vmem_limit_bytes=VMEM_BYTES),
        name="skew_bias",
    )(offset_values.reshape(head_count, 1, padded))


def half_mask(rows, half):
    lanes = lax.broadcasted_iota(jnp.int32, (rows, TILE), 1)
    return (lanes // HALF) == half


def bias_rows(key_base, query_base, seq_len):
    return key_base - query_base + seq_len - TILE


def forward_kernel(
    base_ref, q_ref, k_ref, v_ref, skew_ref, out_ref, lse_ref, score_ref, prob_ref, *, chunk
):
    query_rows = q_ref.shape[0]
    key_rows = k_ref.shape[0]
    seq_len = key_rows
    mask = [half_mask(GROUP, 0), half_mask(GROUP, 1)]
    value_t = v_ref[...].T
    for group in range(query_rows // GROUP):
        rows = slice(group * GROUP, (group + 1) * GROUP)
        query_base = base_ref[0] + group * GROUP
        halves = []
        for half in range(2):
            queries = jnp.where(mask[half], q_ref[rows], 0).astype(jnp.bfloat16)
            score_ref[half] = contract_last(k_ref[...], queries)
            top = jnp.full((8, GROUP), -jnp.inf, jnp.float32)
            for start in range(0, key_rows, chunk):
                key_base = base_ref[start // query_rows] + start % query_rows
                place = pl.multiple_of(bias_rows(key_base, query_base, seq_len), TILE)
                left = skew_ref[half, pl.ds(place, chunk), :]
                right = skew_ref[half, pl.ds(place - TILE, chunk), :]
                bias = jnp.concatenate([left, right], axis=1).astype(jnp.float32)
                piece = score_ref[half, start : start + chunk] + bias
                score_ref[half, start : start + chunk] = piece
                top = jnp.maximum(top, jnp.max(piece.reshape(chunk // 8, 8, GROUP), axis=0))
            top = jnp.max(top, axis=0, keepdims=True)
            total = jnp.zeros((8, GROUP), jnp.float32)
            for start in range(0, key_rows, chunk):
                piece = jnp.exp(score_ref[half, start : start + chunk] - top)
                total = total + jnp.sum(piece.reshape(chunk // 8, 8, GROUP), axis=0)
                prob_ref[half, start : start + chunk] = piece.astype(jnp.bfloat16)
            total = jnp.sum(total, axis=0, keepdims=True)
            lse_ref[0, half : half + 1, rows] = top + jnp.log(total)
            mixed = matmul(value_t[half * HALF : (half + 1) * HALF], prob_ref[half])
            halves.append(mixed / total)
        out_ref[rows] = jnp.concatenate(halves, axis=0).T


def attend_forward(bases, queries, key_values, skew):
    query_rows, width = queries.shape
    key_rows = key_values.shape[0]
    kept = skew.shape[1]
    pairs = width // TILE
    chunk = TILE
    return pl.pallas_call(
        functools.partial(forward_kernel, chunk=chunk),
        grid_spec=pltpu.PrefetchScalarGridSpec(
            num_scalar_prefetch=1,
            grid=(pairs,),
            in_specs=[
                pl.BlockSpec((query_rows, TILE), lambda p, _: (0, p)),
                pl.BlockSpec((key_rows, TILE), lambda p, _: (0, p)),
                pl.BlockSpec((key_rows, TILE), lambda p, _: (0, p + pairs)),
                pl.BlockSpec((2, kept, TILE), lambda p, _: (p, 0, 0)),
            ],
            out_specs=[
                pl.BlockSpec((query_rows, TILE), lambda p, _: (0, p)),
                pl.BlockSpec((1, 2, query_rows), lambda p, _: (p, 0, 0)),
            ],
            scratch_shapes=[
                pltpu.VMEM((2, key_rows, GROUP), jnp.float32),
                pltpu.VMEM((2, key_rows, GROUP), jnp.bfloat16),
            ],
        ),
        out_shape=[
            jax.ShapeDtypeStruct((query_rows, width), jnp.float32),
            jax.ShapeDtypeStruct((pairs, 2, query_rows), jnp.float32),
        ],
        compiler_params=pltpu.CompilerParams(vmem_limit_bytes=VMEM_BYTES),
        name="attend_forward",
    )(bases, queries, key_values, key_values, skew)


def backward_kernel(
    base_ref, q_ref, do_ref, o_ref, k_ref, v_ref, skew_ref, lse_ref,
    dq_ref, dk_ref, dv_ref, off_ref,
    score_ref, gradp_ref, prob_ref, grads_ref, accum_k, accum_v, accum_skew,
    *, chunk,
):
    query_rows = q_ref.shape[0]
    key_rows = k_ref.shape[0]
    seq_len = key_rows
    mask = [half_mask(GROUP, 0), half_mask(GROUP, 1)]
    key_t = k_ref[...].T
    accum_skew[...] = jnp.zeros_like(accum_skew)
    for group in range(query_rows // GROUP):
        rows = slice(group * GROUP, (group + 1) * GROUP)
        query_base = base_ref[0] + group * GROUP
        product = (do_ref[rows].astype(jnp.float32) * o_ref[rows]).T
        halves = []
        sum_k = None
        for half in range(2):
            queries = jnp.where(mask[half], q_ref[rows], 0).astype(jnp.bfloat16)
            grads_out = jnp.where(mask[half], do_ref[rows], 0).astype(jnp.bfloat16)
            score_ref[half] = contract_last(k_ref[...], queries)
            gradp_ref[half] = contract_last(v_ref[...], grads_out)
            logsum = lse_ref[0, half : half + 1, rows]
            delta = jnp.sum(product[half * HALF : (half + 1) * HALF], axis=0, keepdims=True)
            for start in range(0, key_rows, chunk):
                key_base = base_ref[start // query_rows] + start % query_rows
                place = pl.multiple_of(bias_rows(key_base, query_base, seq_len), TILE)
                here = pl.ds(start, chunk)
                left = skew_ref[half, pl.ds(place, chunk), :]
                right = skew_ref[half, pl.ds(place - TILE, chunk), :]
                bias = jnp.concatenate([left, right], axis=1).astype(jnp.float32)
                prob = jnp.exp(score_ref[half, here] + bias - logsum)
                grads = prob * (gradp_ref[half, here] - delta)
                prob_ref[half, here] = prob.astype(jnp.bfloat16)
                grads_ref[half, here] = grads.astype(jnp.bfloat16)
                accum_skew[half, pl.ds(place, chunk), :] += grads[:, :TILE]
                accum_skew[half, pl.ds(place - TILE, chunk), :] += grads[:, TILE:]
            part_k = matmul(grads_ref[half], queries)
            part_v = matmul(prob_ref[half], grads_out)
            sum_k = part_k if sum_k is None else sum_k + part_k
            sum_v = part_v if half == 0 else sum_v + part_v
            halves.append(matmul(key_t[half * HALF : (half + 1) * HALF], grads_ref[half]))
        if group == 0:
            accum_k[...] = sum_k
            accum_v[...] = sum_v
        else:
            accum_k[...] += sum_k
            accum_v[...] += sum_v
        dq_ref[rows] = (jnp.concatenate(halves, axis=0) * 0.125).T.astype(dq_ref.dtype)
    dk_ref[...] = accum_k[...].astype(dk_ref.dtype)
    dv_ref[...] = accum_v[...].astype(dv_ref.dtype)
    for half in range(2):
        turned = accum_skew[half].T
        padded = turned.shape[1]
        count = TILE // 2
        while count:
            turned = turned[:count] + pltpu.roll(turned[count : 2 * count], padded - count, 1)
            count //= 2
        off_ref[0, half : half + 1] = pltpu.roll(turned, TILE - 1, 1)


def attend_backward(bases, queries, grads_out, outputs, key_values, skew, logsum):
    query_rows, width = queries.shape
    key_rows = key_values.shape[0]
    kept = skew.shape[1]
    pairs = width // TILE
    chunk = TILE
    column = lambda count: pl.BlockSpec((count, TILE), lambda p, _: (0, p))
    return pl.pallas_call(
        functools.partial(backward_kernel, chunk=chunk),
        grid_spec=pltpu.PrefetchScalarGridSpec(
            num_scalar_prefetch=1,
            grid=(pairs,),
            in_specs=[
                column(query_rows), column(query_rows), column(query_rows),
                column(key_rows),
                pl.BlockSpec((key_rows, TILE), lambda p, _: (0, p + pairs)),
                pl.BlockSpec((2, kept, TILE), lambda p, _: (p, 0, 0)),
                pl.BlockSpec((1, 2, query_rows), lambda p, _: (p, 0, 0)),
            ],
            out_specs=[
                column(query_rows), column(key_rows), column(key_rows),
                pl.BlockSpec((1, 2, kept + TILE), lambda p, _: (p, 0, 0)),
            ],
            scratch_shapes=[
                pltpu.VMEM((2, key_rows, GROUP), jnp.float32),
                pltpu.VMEM((2, key_rows, GROUP), jnp.float32),
                pltpu.VMEM((2, key_rows, GROUP), jnp.bfloat16),
                pltpu.VMEM((2, key_rows, GROUP), jnp.bfloat16),
                pltpu.VMEM((key_rows, TILE), jnp.float32),
                pltpu.VMEM((key_rows, TILE), jnp.float32),
                pltpu.VMEM((2, kept + TILE, TILE), jnp.float32),
            ],
        ),
        out_shape=[
            jax.ShapeDtypeStruct((query_rows, width), jnp.bfloat16),
            jax.ShapeDtypeStruct((key_rows, width), jnp.bfloat16),
            jax.ShapeDtypeStruct((key_rows, width), jnp.bfloat16),
            jax.ShapeDtypeStruct((pairs, 2, kept + TILE), jnp.float32),
        ],
        compiler_params=pltpu.CompilerParams(vmem_limit_bytes=VMEM_BYTES),
        name="attend_backward",
    )(bases, queries, grads_out, outputs, key_values, key_values, skew, logsum)


def rms_forward(row_data, gain_vec):
    inverse = lax.rsqrt(jnp.mean(row_data * row_data, axis=-1, keepdims=True) + EPSILON)
    return (row_data * inverse * gain_vec, inverse)


def rms_backward(row_data, inverse, gain_vec, grad_out):
    normed = row_data * inverse
    grad_gain = jnp.sum(grad_out * normed, axis=0)
    scaled = grad_out * gain_vec
    spread = jnp.mean(scaled * normed, axis=-1, keepdims=True)
    return (inverse * (scaled - normed * spread), grad_gain)


class Layout:
    def __init__(self):
        self.ctx_count = lax.axis_size("ctx")
        self.exp_count = lax.axis_size("exp")
        self.span = self.ctx_count // 4
        self.members = 2 * self.span
        self.ctx = lax.axis_index("ctx")
        self.core = lax.axis_index("exp") % 2
        self.member = (self.ctx % self.span) * 2 + self.core
        self.side = (self.ctx // self.span) % 2

    def number(self, ctx, exp):
        return ctx * self.exp_count + exp

    def round_pairs(self, turn):
        pairs = []
        for ctx in range(self.ctx_count):
            for exp in range(self.exp_count):
                seq = 2 * (exp % 2) + (turn + ctx) % 2
                member = ctx // 2
                target = self.number(seq * self.span + member // 2, exp // 2 * 2 + member % 2)
                pairs.append((self.number(ctx, exp), target))
        return pairs

    def member_pairs(self, shift):
        pairs = []
        for ctx in range(self.ctx_count):
            for exp in range(self.exp_count):
                start = ctx // self.span * self.span
                member = ((ctx - start) * 2 + exp % 2 + shift) % self.members
                target = self.number(start + member // 2, exp // 2 * 2 + member % 2)
                pairs.append((self.number(ctx, exp), target))
        return pairs

    def gather_blocks(self, blocks):
        got = [
            lax.ppermute(
                lax.dynamic_index_in_dim(blocks, (turn + self.ctx) % 2, 0, keepdims=False),
                BOTH,
                self.round_pairs(turn),
            )
            for turn in range(2)
        ]
        first = jnp.where(self.side == 0, got[0], got[1])
        second = jnp.where(self.side == 0, got[1], got[0])
        return jnp.concatenate([first, second], axis=0)

    def return_blocks(self, rows):
        blocks = rows.reshape((2, rows.shape[0] // 2) + rows.shape[1:])
        got = [
            lax.ppermute(
                lax.dynamic_index_in_dim(blocks, (turn + self.side) % 2, 0, keepdims=False),
                BOTH,
                [(target, source) for source, target in self.round_pairs(turn)],
            )
            for turn in range(2)
        ]
        return got

    def place_blocks(self, got):
        even = self.ctx % 2 == 0
        return jnp.stack([jnp.where(even, got[0], got[1]), jnp.where(even, got[1], got[0])])

    def all_rows(self, rows):
        return jnp.concatenate(
            [rows]
            + [lax.ppermute(rows, BOTH, self.member_pairs(shift)) for shift in range(1, self.members)],
            axis=0,
        )

    def sum_rows(self, partial):
        parts = partial.reshape((self.members, partial.shape[0] // self.members) + partial.shape[1:])
        total = parts[0]
        for shift in range(1, self.members):
            moved = lax.ppermute(
                parts[shift].astype(jnp.bfloat16), BOTH, self.member_pairs(self.members - shift)
            )
            total = total + moved.astype(jnp.float32)
        return total

    def bases(self, row_count):
        return jnp.stack(
            [(self.member - shift) % self.members * row_count for shift in range(self.members)]
        ).astype(jnp.int32)

    def swap(self, rows, distance, axis="ctx"):
        pairs = [(place, place ^ distance) for place in range(lax.axis_size(axis))]
        return lax.ppermute(rows, axis, pairs)

    def gather_small(self, part):
        held = part[None]
        place = lax.axis_index("exp")
        distance = 1
        while distance < self.exp_count:
            other = self.swap(held, distance, "exp")
            upper = (place // distance) % 2 == 1
            held = jnp.where(
                upper,
                jnp.concatenate([other, held], axis=0),
                jnp.concatenate([held, other], axis=0),
            )
            distance *= 2
        return held

    def sum_cores(self, part):
        rows = part.shape[0] // self.exp_count
        blocks = part.reshape(self.exp_count // 2, 2, rows, part.shape[1])
        sent = lax.dynamic_index_in_dim(blocks, 1 - self.core, 1, keepdims=False)
        kept = lax.dynamic_index_in_dim(blocks, self.core, 1, keepdims=False)
        return add_low([kept, self.swap(sent, 1, "exp")])

    def sum_chips(self, blocks):
        pair = lax.axis_index("exp") // 2
        parts = [lax.dynamic_index_in_dim(blocks, pair, 0, keepdims=False)]
        for step in range(1, self.exp_count // 2):
            block = lax.dynamic_index_in_dim(blocks, pair ^ step, 0, keepdims=False)
            parts.append(self.swap(block, 2 * step, "exp"))
        return add_low(parts)

    def sum_ctx(self, total):
        cuts = total.reshape(self.ctx_count, total.shape[0] // self.ctx_count, total.shape[1])
        parts = [lax.dynamic_index_in_dim(cuts, self.ctx, 0, keepdims=False)]
        for step in range(1, self.ctx_count):
            block = lax.dynamic_index_in_dim(cuts, self.ctx ^ step, 0, keepdims=False)
            parts.append(self.swap(block, step))
        return add_low(parts)

    def spread_ctx(self, own):
        every = jnp.stack([own] + [self.swap(own, step) for step in range(1, self.ctx_count)])
        return jnp.concatenate(
            [
                lax.dynamic_index_in_dim(every, self.ctx ^ place, 0, keepdims=False)
                for place in range(self.ctx_count)
            ],
            axis=0,
        )


def add_low(parts):
    total = parts[0].astype(jnp.float32)
    for part in parts[1:]:
        total = total + part.astype(jnp.float32)
    return total.astype(jnp.bfloat16)


def after(value, *events):
    return lax.optimization_barrier((value,) + events)[0]


def per_device(
    tokens_in,
    first_gain,
    joint_projection,
    out_projection,
    bias_table,
    second_gain,
    router_weight,
    expert_up,
    expert_down,
    expert_index,
    keep_mask,
    buckets,
    cotangent,
):
    layout = Layout()
    shards = layout.exp_count
    seq_count, block_len, model_width = tokens_in.shape
    token_count = seq_count * block_len
    expert_count = router_weight.shape[1]
    bucket_count = bias_table.shape[0] * shards
    head_count = bias_table.shape[1]

    small = [first_gain, second_gain, router_weight, bias_table]
    small_sizes = [part.size for part in small]
    small_cuts = [sum(small_sizes[:place]) for place in range(1, len(small))]
    small_count = sum(small_sizes)
    small_padded = -(-small_count // TILE) * TILE
    small_full = layout.gather_small(
        jnp.pad(
            jnp.concatenate([part.reshape(-1) for part in small]), (0, small_padded - small_count)
        )
    )[:, :small_count]
    gain_one, gain_two, weight_router, table = jnp.split(small_full, small_cuts, axis=1)
    weight_router = weight_router.reshape(model_width, expert_count)
    table = table.reshape(bucket_count, head_count)
    gain_first = gain_one.reshape(model_width).astype(jnp.float32)
    gain_second = gain_two.reshape(model_width).astype(jnp.float32)
    weight_joint = lax.all_gather(joint_projection, "exp", axis=0, tiled=True)
    weight_out = lax.all_gather(out_projection, "exp", axis=0, tiled=True)

    tokens = layout.gather_blocks(tokens_in)
    codes = layout.gather_blocks(expert_index.reshape(seq_count, block_len) * 2 + keep_mask)
    grad_out_low = layout.gather_blocks(cotangent)
    every_token = layout.all_rows(tokens)
    chosen = codes // 2
    kept = codes % 2

    distances = list(range(2, layout.ctx_count, 2))
    held_up = after(expert_up[0], grad_out_low)
    held_down = after(expert_down[0], grad_out_low)
    up_moved = [layout.swap(held_up, step) for step in distances]
    down_moved = [layout.swap(held_down, step) for step in distances]

    offset_count = buckets.shape[0]
    bucket_hot = buckets[None, :] == jnp.arange(bucket_count, dtype=jnp.int32)[:, None]
    offset_values = lax.dot_general(
        table,
        bucket_hot.astype(jnp.bfloat16),
        (((0,), (0,)), ((), ())),
        preferred_element_type=jnp.float32,
    )
    skew = make_skew(jnp.pad(offset_values, ((0, 0), (0, 1))))

    is_choice = chosen[:, None] == jnp.arange(expert_count, dtype=jnp.int32)
    most_rows = max(2, (5 * block_len + 4 * expert_count - 1) // (4 * expert_count))
    capacity = seq_count * most_rows
    place = jnp.arange(token_count, dtype=jnp.int32)
    earlier = (place[:, None] >= place[None, :]) & (
        place[:, None] // block_len == place[None, :] // block_len
    )
    running = jnp.dot(
        earlier.astype(jnp.bfloat16),
        is_choice.astype(jnp.bfloat16),
        preferred_element_type=jnp.float32,
    )
    slot_rank = (jnp.sum(running * is_choice.astype(jnp.float32), axis=-1) - 1.0).astype(jnp.int32)
    token_slot = chosen * capacity + place // block_len * most_rows + slot_rank
    slot_hot = (
        (token_slot[:, None] == jnp.arange(expert_count * capacity, dtype=jnp.int32))
        & (kept[:, None] > 0)
    ).astype(jnp.bfloat16)

    def exchange(row_data):
        return lax.all_to_all(
            row_data.reshape(shards, -1, model_width), "exp", split_axis=0, concat_axis=0, tiled=True
        ).reshape(-1, model_width)

    def to_experts(row_data):
        sent = lax.dot_general(
            slot_hot, row_data, (((0,), (0,)), ((), ())), preferred_element_type=jnp.float32
        ).astype(jnp.bfloat16)
        return exchange(sent)

    def sum_halves(own_part, other_part):
        other = layout.swap(other_part, 1)
        return (own_part + other.astype(jnp.float32)).astype(jnp.bfloat16)

    def from_experts(summed):
        return jnp.dot(slot_hot, exchange(summed), preferred_element_type=jnp.float32)

    every_float = every_token.astype(jnp.float32)
    tokens_f = every_float[:token_count]
    normed_one, every_inverse = rms_forward(every_float, gain_first)
    inverse_one = every_inverse[:token_count]
    hidden_one = normed_one.astype(jnp.bfloat16)
    queries = jnp.dot(
        hidden_one[:token_count], weight_joint[:, :model_width], preferred_element_type=jnp.float32
    ).astype(jnp.bfloat16) * jnp.bfloat16(SCORE_SCALE)
    key_values = jnp.dot(
        hidden_one, weight_joint[:, model_width:], preferred_element_type=jnp.float32
    ).astype(jnp.bfloat16)
    queries = after(queries, grad_out_low)
    bases = layout.bases(token_count)
    attended, logsum = attend_forward(bases, queries, key_values, skew)
    attended_low = attended.astype(jnp.bfloat16)
    residual = tokens_f + jnp.dot(attended_low, weight_out, preferred_element_type=jnp.float32)
    normed_two, inverse_two = rms_forward(residual, gain_second)
    hidden_two = after(normed_two.astype(jnp.bfloat16), *up_moved)

    row_own = to_experts(hidden_two)
    row_other = layout.swap(row_own, 1)
    grad_own = to_experts(after(grad_out_low, row_own))
    grad_other = layout.swap(grad_own, 1)
    row_other = after(row_other, *down_moved)
    ups = [expert_up[0]] + up_moved
    downs = [expert_down[0]] + down_moved

    expert_here = jnp.arange(expert_count, dtype=jnp.int32) == lax.axis_index("exp")
    expert_here = expert_here.astype(jnp.float32)[None, :]

    def contract_rows(left, right):
        return lax.dot_general(
            left, right, (((0,), (0,)), ((), ())), preferred_element_type=jnp.float32
        )

    results, grad_inputs = [], []
    grad_router = 0.0
    grad_ups, grad_downs = [0.0] * len(ups), [0.0] * len(ups)
    for rows, grad_rows in ((row_own, grad_own), (row_other, grad_other)):
        logits = jnp.dot(rows, weight_router, preferred_element_type=jnp.float32)
        router_prob = jax.nn.softmax(logits, axis=-1)
        picked = jnp.sum(router_prob * expert_here, axis=-1, keepdims=True)
        grad_float = grad_rows.astype(jnp.float32)
        grad_result = (picked * grad_float).astype(jnp.bfloat16)
        produced, grad_input = 0.0, 0.0
        for part, (matrix_up, matrix_down) in enumerate(zip(ups, downs)):
            before = jnp.dot(rows, matrix_up, preferred_element_type=jnp.float32)
            activated, gelu_back = jax.vjp(jax.nn.gelu, before)
            acted = activated.astype(jnp.bfloat16)
            produced = produced + jnp.dot(acted, matrix_down, preferred_element_type=jnp.float32)
            grad_acted = contract_last(grad_result, matrix_down)
            grad_before = gelu_back(grad_acted)[0].astype(jnp.bfloat16)
            grad_input = grad_input + contract_last(grad_before, matrix_up)
            grad_ups[part] = grad_ups[part] + contract_rows(rows, grad_before)
            grad_downs[part] = grad_downs[part] + contract_rows(acted, grad_result)
        grad_picked = jnp.sum(grad_float * produced, axis=-1, keepdims=True)
        grad_logits = (picked * (expert_here - router_prob) * grad_picked).astype(jnp.bfloat16)
        grad_router = grad_router + contract_rows(rows, grad_logits)
        grad_inputs.append(grad_input + contract_last(grad_logits, weight_router))
        results.append(picked * produced)

    grad_summed = sum_halves(grad_inputs[0], grad_inputs[1].astype(jnp.bfloat16))
    grad_back = from_experts(grad_summed)
    result_other = after(results[1].astype(jnp.bfloat16), grad_summed)
    result_summed = sum_halves(results[0], result_other)

    down_low = [after(part.astype(jnp.bfloat16), grad_summed) for part in grad_downs[1:]]
    up_low = [after(part.astype(jnp.bfloat16), grad_summed) for part in grad_ups[1:]]

    def moved(parts):
        return [layout.swap(part, step) for part, step in zip(parts, distances)]

    grads_down_moved = moved(down_low)
    grads_up_moved = moved(up_low)

    def own_slice(own, others):
        total = own
        for other in others:
            total = total + other.astype(jnp.float32)
        return total[None]

    grad_residual, grad_gain_two = rms_backward(residual, inverse_two, gain_second, grad_back)
    grad_residual = grad_residual + grad_out_low.astype(jnp.float32)
    grad_mixed = grad_residual.astype(jnp.bfloat16)
    grad_weight_out = contract_rows(attended_low, grad_mixed)
    grad_attended = contract_last(grad_mixed, weight_out).astype(jnp.bfloat16)
    grad_q, grad_k, grad_v, grad_off = attend_backward(
        bases, queries, grad_attended, attended, key_values, skew, logsum
    )
    grad_k, result_summed = lax.optimization_barrier((grad_k, result_summed))
    layer_rows = residual + from_experts(result_summed)
    layer_sent = layout.return_blocks(layer_rows.astype(jnp.bfloat16))

    grad_kv = jnp.concatenate([grad_k, grad_v], axis=1)
    kv_out_part = jnp.concatenate(
        [
            contract_rows(hidden_one, grad_kv).astype(jnp.bfloat16),
            grad_weight_out.astype(jnp.bfloat16),
        ],
        axis=1,
    )
    kv_out_cores = layout.sum_cores(kv_out_part)
    partial_one = contract_last(
        after(grad_kv, kv_out_part, layer_rows), weight_joint[:, model_width:]
    )
    partial_own = contract_last(grad_q, weight_joint[:, :model_width])
    every_normed = every_float * every_inverse
    grad_gain_one = jnp.sum(partial_one * every_normed, axis=0) + jnp.sum(
        partial_own * every_normed[:token_count], axis=0
    )
    grad_hidden_one = layout.sum_rows(partial_one) + partial_own
    kv_out_cores, layer_sent, _ = lax.optimization_barrier((kv_out_cores, layer_sent, partial_own))
    kv_out_chips = layout.sum_chips(kv_out_cores)
    grad_input_norm, _ = rms_backward(tokens_f, inverse_one, gain_first, grad_hidden_one)
    tokens_sent = layout.return_blocks((grad_input_norm + grad_residual).astype(jnp.bfloat16))
    query_part = contract_rows(hidden_one[:token_count], grad_q).astype(jnp.bfloat16)
    grad_table = jnp.dot(
        bucket_hot.astype(jnp.float32),
        grad_off.reshape(head_count, -1)[:, :offset_count].T,
        precision=HIGHEST,
    )
    small_grads = [grad_gain_one, grad_gain_two, grad_router, grad_table]
    shard_rows = joint_projection.shape[0]
    side_width = -(-small_count // (shard_rows * TILE)) * TILE
    small_grads = jnp.concatenate([part.reshape(shards, -1) for part in small_grads], axis=1)
    small_grads = jnp.pad(small_grads, ((0, 0), (0, shard_rows * side_width - small_count)))
    side = small_grads.reshape(shards * shard_rows, side_width).astype(jnp.bfloat16)
    query_cores = layout.sum_cores(jnp.concatenate([query_part, side], axis=1))
    kv_out_chips, query_cores, grads_down_moved, grads_up_moved, tokens_sent = (
        lax.optimization_barrier(
            (kv_out_chips, query_cores, grads_down_moved, grads_up_moved, tokens_sent)
        )
    )
    grad_expert_down = own_slice(grad_downs[0], grads_down_moved)
    kv_out_own = layout.sum_ctx(kv_out_chips)
    query_chips = layout.sum_chips(query_cores)
    kv_out_own, query_chips = lax.optimization_barrier((kv_out_own, query_chips))
    kv_out_sum = layout.spread_ctx(kv_out_own)
    query_own = layout.sum_ctx(query_chips)
    kv_out_sum, query_own = lax.optimization_barrier((kv_out_sum, query_own))
    grad_expert_up = own_slice(grad_ups[0], grads_up_moved)
    query_sum = layout.spread_ctx(query_own)
    layer_out = layout.place_blocks(layer_sent)
    grad_tokens = layout.place_blocks(tokens_sent).astype(jnp.float32)
    kv_sum = kv_out_sum[:, : 2 * model_width]
    out_sum = kv_out_sum[:, 2 * model_width :]
    side_sum = query_sum[:, model_width:].reshape(-1)[:small_count].astype(jnp.float32)
    joint_sum = jnp.concatenate([query_sum[:, :model_width], kv_sum], axis=1)
    sum_gain_one, sum_gain_two, sum_router, sum_table = jnp.split(side_sum, small_cuts)
    return (
        layer_out,
        grad_tokens,
        sum_gain_one,
        joint_sum.astype(jnp.float32),
        out_sum.astype(jnp.float32),
        sum_table.reshape(bias_table.shape),
        sum_gain_two,
        sum_router.reshape(router_weight.shape),
        grad_expert_up,
        grad_expert_down,
    )


def solution(mesh):
    in_specs = (
        P("exp", "ctx", None),
        P("exp"),
        P("exp", None),
        P("exp", None),
        P("exp", None),
        P("exp"),
        P("exp", None),
        P("exp", None, "ctx"),
        P("exp", "ctx", None),
        P("exp", "ctx", None),
        P("exp", "ctx"),
        P(),
        P("exp", "ctx", None),
    )
    out_specs = (
        P("exp", "ctx", None),
        P("exp", "ctx", None),
        P("exp"),
        P("exp", None),
        P("exp", None),
        P("exp", None),
        P("exp"),
        P("exp", None),
        P("exp", None, "ctx"),
        P("exp", "ctx", None),
    )
    return jax.shard_map(
        per_device, mesh=mesh, in_specs=in_specs, out_specs=out_specs, check_vma=False
    )
```

```python
import functools

import jax
import jax.numpy as jnp
from jax import lax
from jax.experimental import pallas as pl
from jax.experimental.pallas import tpu as pltpu
from jax.sharding import PartitionSpec as P

EPSILON = 1e-06
HALF = 64
TILE = 128
GROUP = 256
VMEM_BYTES = 50 * 1024 * 1024
SCORE_SCALE = 0.125
HIGHEST = lax.Precision.HIGHEST
BOTH = ("ctx", "exp")


def contract_last(left, right):
    return lax.dot_general(
        left, right, (((1,), (1,)), ((), ())), preferred_element_type=jnp.float32
    )


def matmul(left, right):
    return lax.dot_general(
        left, right, (((1,), (0,)), ((), ())), preferred_element_type=jnp.float32
    )


def skew_kernel(offset_ref, skew_ref):
    padded = offset_ref.shape[-1]
    kept = skew_ref.shape[1]
    rows = jnp.broadcast_to(offset_ref[0], (TILE, padded))
    rolled = pltpu.roll(rows, padded - (TILE - 1), 1, stride=1, stride_axis=0)
    skew_ref[0] = rolled[:, :kept].T.astype(skew_ref.dtype)


def make_skew(offset_values):
    head_count, padded = offset_values.shape
    kept = padded - TILE
    return pl.pallas_call(
        skew_kernel,
        grid=(head_count,),
        in_specs=[pl.BlockSpec((1, 1, padded), lambda h: (h, 0, 0))],
        out_specs=pl.BlockSpec((1, kept, TILE), lambda h: (h, 0, 0)),
        out_shape=jax.ShapeDtypeStruct((head_count, kept, TILE), jnp.bfloat16),
        compiler_params=pltpu.CompilerParams(vmem_limit_bytes=VMEM_BYTES),
        name="skew_bias",
    )(offset_values.reshape(head_count, 1, padded))


def half_mask(rows, half):
    lanes = lax.broadcasted_iota(jnp.int32, (rows, TILE), 1)
    return (lanes // HALF) == half


def bias_rows(key_base, query_base, seq_len):
    return key_base - query_base + seq_len - TILE


def forward_kernel(
    base_ref, q_ref, k_ref, v_ref, skew_ref, out_ref, lse_ref, score_ref, prob_ref, *, chunk
):
    query_rows = q_ref.shape[0]
    key_rows = k_ref.shape[0]
    seq_len = key_rows
    mask = [half_mask(GROUP, 0), half_mask(GROUP, 1)]
    value_t = v_ref[...].T
    for group in range(query_rows // GROUP):
        rows = slice(group * GROUP, (group + 1) * GROUP)
        query_base = base_ref[0] + group * GROUP
        halves = []
        for half in range(2):
            queries = jnp.where(mask[half], q_ref[rows], 0).astype(jnp.bfloat16)
            score_ref[half] = contract_last(k_ref[...], queries)
            top = jnp.full((8, GROUP), -jnp.inf, jnp.float32)
            for start in range(0, key_rows, chunk):
                key_base = base_ref[start // query_rows] + start % query_rows
                place = pl.multiple_of(bias_rows(key_base, query_base, seq_len), TILE)
                left = skew_ref[half, pl.ds(place, chunk), :]
                right = skew_ref[half, pl.ds(place - TILE, chunk), :]
                bias = jnp.concatenate([left, right], axis=1).astype(jnp.float32)
                piece = score_ref[half, start : start + chunk] + bias
                score_ref[half, start : start + chunk] = piece
                top = jnp.maximum(top, jnp.max(piece.reshape(chunk // 8, 8, GROUP), axis=0))
            top = jnp.max(top, axis=0, keepdims=True)
            total = jnp.zeros((8, GROUP), jnp.float32)
            for start in range(0, key_rows, chunk):
                piece = jnp.exp(score_ref[half, start : start + chunk] - top)
                total = total + jnp.sum(piece.reshape(chunk // 8, 8, GROUP), axis=0)
                prob_ref[half, start : start + chunk] = piece.astype(jnp.bfloat16)
            total = jnp.sum(total, axis=0, keepdims=True)
            lse_ref[0, half : half + 1, rows] = top + jnp.log(total)
            mixed = matmul(value_t[half * HALF : (half + 1) * HALF], prob_ref[half])
            halves.append(mixed / total)
        out_ref[rows] = jnp.concatenate(halves, axis=0).T


def attend_forward(bases, queries, key_values, skew):
    query_rows, width = queries.shape
    key_rows = key_values.shape[0]
    kept = skew.shape[1]
    pairs = width // TILE
    chunk = TILE
    return pl.pallas_call(
        functools.partial(forward_kernel, chunk=chunk),
        grid_spec=pltpu.PrefetchScalarGridSpec(
            num_scalar_prefetch=1,
            grid=(pairs,),
            in_specs=[
                pl.BlockSpec((query_rows, TILE), lambda p, _: (0, p)),
                pl.BlockSpec((key_rows, TILE), lambda p, _: (0, p)),
                pl.BlockSpec((key_rows, TILE), lambda p, _: (0, p + pairs)),
                pl.BlockSpec((2, kept, TILE), lambda p, _: (p, 0, 0)),
            ],
            out_specs=[
                pl.BlockSpec((query_rows, TILE), lambda p, _: (0, p)),
                pl.BlockSpec((1, 2, query_rows), lambda p, _: (p, 0, 0)),
            ],
            scratch_shapes=[
                pltpu.VMEM((2, key_rows, GROUP), jnp.float32),
                pltpu.VMEM((2, key_rows, GROUP), jnp.bfloat16),
            ],
        ),
        out_shape=[
            jax.ShapeDtypeStruct((query_rows, width), jnp.float32),
            jax.ShapeDtypeStruct((pairs, 2, query_rows), jnp.float32),
        ],
        compiler_params=pltpu.CompilerParams(vmem_limit_bytes=VMEM_BYTES),
        name="attend_forward",
    )(bases, queries, key_values, key_values, skew)


def backward_kernel(
    base_ref, q_ref, do_ref, o_ref, k_ref, v_ref, skew_ref, lse_ref,
    dq_ref, dk_ref, dv_ref, off_ref,
    score_ref, gradp_ref, prob_ref, grads_ref, accum_k, accum_v, accum_skew,
    *, chunk,
):
    query_rows = q_ref.shape[0]
    key_rows = k_ref.shape[0]
    seq_len = key_rows
    mask = [half_mask(GROUP, 0), half_mask(GROUP, 1)]
    key_t = k_ref[...].T
    accum_skew[...] = jnp.zeros_like(accum_skew)
    for group in range(query_rows // GROUP):
        rows = slice(group * GROUP, (group + 1) * GROUP)
        query_base = base_ref[0] + group * GROUP
        product = (do_ref[rows].astype(jnp.float32) * o_ref[rows]).T
        halves = []
        sum_k = None
        for half in range(2):
            queries = jnp.where(mask[half], q_ref[rows], 0).astype(jnp.bfloat16)
            grads_out = jnp.where(mask[half], do_ref[rows], 0).astype(jnp.bfloat16)
            score_ref[half] = contract_last(k_ref[...], queries)
            gradp_ref[half] = contract_last(v_ref[...], grads_out)
            logsum = lse_ref[0, half : half + 1, rows]
            delta = jnp.sum(product[half * HALF : (half + 1) * HALF], axis=0, keepdims=True)
            for start in range(0, key_rows, chunk):
                key_base = base_ref[start // query_rows] + start % query_rows
                place = pl.multiple_of(bias_rows(key_base, query_base, seq_len), TILE)
                here = pl.ds(start, chunk)
                left = skew_ref[half, pl.ds(place, chunk), :]
                right = skew_ref[half, pl.ds(place - TILE, chunk), :]
                bias = jnp.concatenate([left, right], axis=1).astype(jnp.float32)
                prob = jnp.exp(score_ref[half, here] + bias - logsum)
                grads = prob * (gradp_ref[half, here] - delta)
                prob_ref[half, here] = prob.astype(jnp.bfloat16)
                grads_ref[half, here] = grads.astype(jnp.bfloat16)
                accum_skew[half, pl.ds(place, chunk), :] += grads[:, :TILE]
                accum_skew[half, pl.ds(place - TILE, chunk), :] += grads[:, TILE:]
            part_k = matmul(grads_ref[half], queries)
            part_v = matmul(prob_ref[half], grads_out)
            sum_k = part_k if sum_k is None else sum_k + part_k
            sum_v = part_v if half == 0 else sum_v + part_v
            halves.append(matmul(key_t[half * HALF : (half + 1) * HALF], grads_ref[half]))
        if group == 0:
            accum_k[...] = sum_k
            accum_v[...] = sum_v
        else:
            accum_k[...] += sum_k
            accum_v[...] += sum_v
        dq_ref[rows] = (jnp.concatenate(halves, axis=0) * 0.125).T.astype(dq_ref.dtype)
    dk_ref[...] = accum_k[...].astype(dk_ref.dtype)
    dv_ref[...] = accum_v[...].astype(dv_ref.dtype)
    for half in range(2):
        turned = accum_skew[half].T
        padded = turned.shape[1]
        count = TILE // 2
        while count:
            turned = turned[:count] + pltpu.roll(turned[count : 2 * count], padded - count, 1)
            count //= 2
        off_ref[0, half : half + 1] = pltpu.roll(turned, TILE - 1, 1)


def attend_backward(bases, queries, grads_out, outputs, key_values, skew, logsum):
    query_rows, width = queries.shape
    key_rows = key_values.shape[0]
    kept = skew.shape[1]
    pairs = width // TILE
    chunk = TILE
    column = lambda count: pl.BlockSpec((count, TILE), lambda p, _: (0, p))
    return pl.pallas_call(
        functools.partial(backward_kernel, chunk=chunk),
        grid_spec=pltpu.PrefetchScalarGridSpec(
            num_scalar_prefetch=1,
            grid=(pairs,),
            in_specs=[
                column(query_rows), column(query_rows), column(query_rows),
                column(key_rows),
                pl.BlockSpec((key_rows, TILE), lambda p, _: (0, p + pairs)),
                pl.BlockSpec((2, kept, TILE), lambda p, _: (p, 0, 0)),
                pl.BlockSpec((1, 2, query_rows), lambda p, _: (p, 0, 0)),
            ],
            out_specs=[
                column(query_rows), column(key_rows), column(key_rows),
                pl.BlockSpec((1, 2, kept + TILE), lambda p, _: (p, 0, 0)),
            ],
            scratch_shapes=[
                pltpu.VMEM((2, key_rows, GROUP), jnp.float32),
                pltpu.VMEM((2, key_rows, GROUP), jnp.float32),
                pltpu.VMEM((2, key_rows, GROUP), jnp.bfloat16),
                pltpu.VMEM((2, key_rows, GROUP), jnp.bfloat16),
                pltpu.VMEM((key_rows, TILE), jnp.float32),
                pltpu.VMEM((key_rows, TILE), jnp.float32),
                pltpu.VMEM((2, kept + TILE, TILE), jnp.float32),
            ],
        ),
        out_shape=[
            jax.ShapeDtypeStruct((query_rows, width), jnp.bfloat16),
            jax.ShapeDtypeStruct((key_rows, width), jnp.bfloat16),
            jax.ShapeDtypeStruct((key_rows, width), jnp.bfloat16),
            jax.ShapeDtypeStruct((pairs, 2, kept + TILE), jnp.float32),
        ],
        compiler_params=pltpu.CompilerParams(vmem_limit_bytes=VMEM_BYTES),
        name="attend_backward",
    )(bases, queries, grads_out, outputs, key_values, key_values, skew, logsum)


def rms_forward(row_data, gain_vec):
    inverse = lax.rsqrt(jnp.mean(row_data * row_data, axis=-1, keepdims=True) + EPSILON)
    return (row_data * inverse * gain_vec, inverse)


def rms_backward(row_data, inverse, gain_vec, grad_out):
    normed = row_data * inverse
    grad_gain = jnp.sum(grad_out * normed, axis=0)
    scaled = grad_out * gain_vec
    spread = jnp.mean(scaled * normed, axis=-1, keepdims=True)
    return (inverse * (scaled - normed * spread), grad_gain)


class Layout:
    def __init__(self):
        self.ctx_count = lax.axis_size("ctx")
        self.exp_count = lax.axis_size("exp")
        self.span = self.ctx_count // 4
        self.members = 2 * self.span
        self.ctx = lax.axis_index("ctx")
        self.core = lax.axis_index("exp") % 2
        self.member = (self.ctx % self.span) * 2 + self.core
        self.side = (self.ctx // self.span) % 2

    def number(self, ctx, exp):
        return ctx * self.exp_count + exp

    def round_pairs(self, turn):
        pairs = []
        for ctx in range(self.ctx_count):
            for exp in range(self.exp_count):
                seq = 2 * (exp % 2) + (turn + ctx) % 2
                member = ctx // 2
                target = self.number(seq * self.span + member // 2, exp // 2 * 2 + member % 2)
                pairs.append((self.number(ctx, exp), target))
        return pairs

    def member_pairs(self, shift):
        pairs = []
        for ctx in range(self.ctx_count):
            for exp in range(self.exp_count):
                start = ctx // self.span * self.span
                member = ((ctx - start) * 2 + exp % 2 + shift) % self.members
                target = self.number(start + member // 2, exp // 2 * 2 + member % 2)
                pairs.append((self.number(ctx, exp), target))
        return pairs

    def gather_blocks(self, blocks):
        got = [
            lax.ppermute(
                lax.dynamic_index_in_dim(blocks, (turn + self.ctx) % 2, 0, keepdims=False),
                BOTH,
                self.round_pairs(turn),
            )
            for turn in range(2)
        ]
        first = jnp.where(self.side == 0, got[0], got[1])
        second = jnp.where(self.side == 0, got[1], got[0])
        return jnp.concatenate([first, second], axis=0)

    def return_blocks(self, rows):
        blocks = rows.reshape((2, rows.shape[0] // 2) + rows.shape[1:])
        got = [
            lax.ppermute(
                lax.dynamic_index_in_dim(blocks, (turn + self.side) % 2, 0, keepdims=False),
                BOTH,
                [(target, source) for source, target in self.round_pairs(turn)],
            )
            for turn in range(2)
        ]
        return got

    def place_blocks(self, got):
        even = self.ctx % 2 == 0
        return jnp.stack([jnp.where(even, got[0], got[1]), jnp.where(even, got[1], got[0])])

    def all_rows(self, rows):
        return jnp.concatenate(
            [rows]
            + [lax.ppermute(rows, BOTH, self.member_pairs(shift)) for shift in range(1, self.members)],
            axis=0,
        )

    def sum_rows(self, partial):
        parts = partial.reshape((self.members, partial.shape[0] // self.members) + partial.shape[1:])
        total = parts[0]
        for shift in range(1, self.members):
            moved = lax.ppermute(
                parts[shift].astype(jnp.bfloat16), BOTH, self.member_pairs(self.members - shift)
            )
            total = total + moved.astype(jnp.float32)
        return total

    def bases(self, row_count):
        return jnp.stack(
            [(self.member - shift) % self.members * row_count for shift in range(self.members)]
        ).astype(jnp.int32)

    def swap(self, rows, distance, axis="ctx"):
        pairs = [(place, place ^ distance) for place in range(lax.axis_size(axis))]
        return lax.ppermute(rows, axis, pairs)

    def gather_small(self, part):
        held = part[None]
        place = lax.axis_index("exp")
        distance = 1
        while distance < self.exp_count:
            other = self.swap(held, distance, "exp")
            upper = (place // distance) % 2 == 1
            held = jnp.where(
                upper,
                jnp.concatenate([other, held], axis=0),
                jnp.concatenate([held, other], axis=0),
            )
            distance *= 2
        return held

    def sum_cores(self, part):
        rows = part.shape[0] // self.exp_count
        blocks = part.reshape(self.exp_count // 2, 2, rows, part.shape[1])
        sent = lax.dynamic_index_in_dim(blocks, 1 - self.core, 1, keepdims=False)
        kept = lax.dynamic_index_in_dim(blocks, self.core, 1, keepdims=False)
        return add_low([kept, self.swap(sent, 1, "exp")])

    def sum_chips(self, blocks):
        pair = lax.axis_index("exp") // 2
        parts = [lax.dynamic_index_in_dim(blocks, pair, 0, keepdims=False)]
        for step in range(1, self.exp_count // 2):
            block = lax.dynamic_index_in_dim(blocks, pair ^ step, 0, keepdims=False)
            parts.append(self.swap(block, 2 * step, "exp"))
        return add_low(parts)

    def sum_ctx(self, total):
        cuts = total.reshape(self.ctx_count, total.shape[0] // self.ctx_count, total.shape[1])
        parts = [lax.dynamic_index_in_dim(cuts, self.ctx, 0, keepdims=False)]
        for step in range(1, self.ctx_count):
            block = lax.dynamic_index_in_dim(cuts, self.ctx ^ step, 0, keepdims=False)
            parts.append(self.swap(block, step))
        return add_low(parts)

    def spread_ctx(self, own):
        every = jnp.stack([own] + [self.swap(own, step) for step in range(1, self.ctx_count)])
        return jnp.concatenate(
            [
                lax.dynamic_index_in_dim(every, self.ctx ^ place, 0, keepdims=False)
                for place in range(self.ctx_count)
            ],
            axis=0,
        )


def add_low(parts):
    total = parts[0].astype(jnp.float32)
    for part in parts[1:]:
        total = total + part.astype(jnp.float32)
    return total.astype(jnp.bfloat16)


def after(value, *events):
    return lax.optimization_barrier((value,) + events)[0]


def per_device(
    tokens_in,
    first_gain,
    joint_projection,
    out_projection,
    bias_table,
    second_gain,
    router_weight,
    expert_up,
    expert_down,
    expert_index,
    keep_mask,
    buckets,
    cotangent,
):
    layout = Layout()
    shards = layout.exp_count
    seq_count, block_len, model_width = tokens_in.shape
    token_count = seq_count * block_len
    expert_count = router_weight.shape[1]
    bucket_count = bias_table.shape[0] * shards
    head_count = bias_table.shape[1]

    small = [first_gain, second_gain, router_weight, bias_table]
    small_sizes = [part.size for part in small]
    small_cuts = [sum(small_sizes[:place]) for place in range(1, len(small))]
    small_count = sum(small_sizes)
    small_padded = -(-small_count // TILE) * TILE
    small_full = layout.gather_small(
        jnp.pad(
            jnp.concatenate([part.reshape(-1) for part in small]), (0, small_padded - small_count)
        )
    )[:, :small_count]
    gain_one, gain_two, weight_router, table = jnp.split(small_full, small_cuts, axis=1)
    weight_router = weight_router.reshape(model_width, expert_count)
    table = table.reshape(bucket_count, head_count)
    gain_first = gain_one.reshape(model_width).astype(jnp.float32)
    gain_second = gain_two.reshape(model_width).astype(jnp.float32)
    weight_joint = lax.all_gather(joint_projection, "exp", axis=0, tiled=True)
    weight_out = lax.all_gather(out_projection, "exp", axis=0, tiled=True)

    tokens = layout.gather_blocks(tokens_in)
    codes = layout.gather_blocks(expert_index.reshape(seq_count, block_len) * 2 + keep_mask)
    grad_out_low = layout.gather_blocks(cotangent)
    every_token = layout.all_rows(tokens)
    chosen = codes // 2
    kept = codes % 2

    distances = list(range(2, layout.ctx_count, 2))
    held_up = after(expert_up[0], grad_out_low)
    held_down = after(expert_down[0], grad_out_low)
    up_moved = [layout.swap(held_up, step) for step in distances]
    down_moved = [layout.swap(held_down, step) for step in distances]

    offset_count = buckets.shape[0]
    bucket_hot = buckets[None, :] == jnp.arange(bucket_count, dtype=jnp.int32)[:, None]
    offset_values = lax.dot_general(
        table,
        bucket_hot.astype(jnp.bfloat16),
        (((0,), (0,)), ((), ())),
        preferred_element_type=jnp.float32,
    )
    skew = make_skew(jnp.pad(offset_values, ((0, 0), (0, 1))))

    is_choice = chosen[:, None] == jnp.arange(expert_count, dtype=jnp.int32)
    most_rows = max(2, (5 * block_len + 4 * expert_count - 1) // (4 * expert_count))
    capacity = seq_count * most_rows
    place = jnp.arange(token_count, dtype=jnp.int32)
    earlier = (place[:, None] >= place[None, :]) & (
        place[:, None] // block_len == place[None, :] // block_len
    )
    running = jnp.dot(
        earlier.astype(jnp.bfloat16),
        is_choice.astype(jnp.bfloat16),
        preferred_element_type=jnp.float32,
    )
    slot_rank = (jnp.sum(running * is_choice.astype(jnp.float32), axis=-1) - 1.0).astype(jnp.int32)
    token_slot = chosen * capacity + place // block_len * most_rows + slot_rank
    slot_hot = (
        (token_slot[:, None] == jnp.arange(expert_count * capacity, dtype=jnp.int32))
        & (kept[:, None] > 0)
    ).astype(jnp.bfloat16)

    def exchange(row_data):
        return lax.all_to_all(
            row_data.reshape(shards, -1, model_width), "exp", split_axis=0, concat_axis=0, tiled=True
        ).reshape(-1, model_width)

    def to_experts(row_data):
        sent = lax.dot_general(
            slot_hot, row_data, (((0,), (0,)), ((), ())), preferred_element_type=jnp.float32
        ).astype(jnp.bfloat16)
        return exchange(sent)

    def sum_halves(own_part, other_part):
        other = layout.swap(other_part, 1)
        return (own_part + other.astype(jnp.float32)).astype(jnp.bfloat16)

    def from_experts(summed):
        return jnp.dot(slot_hot, exchange(summed), preferred_element_type=jnp.float32)

    every_float = every_token.astype(jnp.float32)
    tokens_f = every_float[:token_count]
    normed_one, every_inverse = rms_forward(every_float, gain_first)
    inverse_one = every_inverse[:token_count]
    hidden_one = normed_one.astype(jnp.bfloat16)
    queries = jnp.dot(
        hidden_one[:token_count], weight_joint[:, :model_width], preferred_element_type=jnp.float32
    ).astype(jnp.bfloat16) * jnp.bfloat16(SCORE_SCALE)
    key_values = jnp.dot(
        hidden_one, weight_joint[:, model_width:], preferred_element_type=jnp.float32
    ).astype(jnp.bfloat16)
    queries = after(queries, grad_out_low)
    bases = layout.bases(token_count)
    attended, logsum = attend_forward(bases, queries, key_values, skew)
    attended_low = attended.astype(jnp.bfloat16)
    residual = tokens_f + jnp.dot(attended_low, weight_out, preferred_element_type=jnp.float32)
    normed_two, inverse_two = rms_forward(residual, gain_second)
    hidden_two = after(normed_two.astype(jnp.bfloat16), *up_moved)

    row_own = to_experts(hidden_two)
    row_other = layout.swap(row_own, 1)
    grad_own = to_experts(after(grad_out_low, row_own))
    grad_other = layout.swap(grad_own, 1)
    ups = [expert_up[0]] + up_moved
    downs = [expert_down[0]] + down_moved

    expert_here = jnp.arange(expert_count, dtype=jnp.int32) == lax.axis_index("exp")
    expert_here = expert_here.astype(jnp.float32)[None, :]

    def contract_rows(left, right):
        return lax.dot_general(
            left, right, (((0,), (0,)), ((), ())), preferred_element_type=jnp.float32
        )

    results, grad_inputs = [], []
    grad_router = 0.0
    grad_ups, grad_downs = [0.0] * len(ups), [0.0] * len(ups)
    for turn in range(2):
        rows, grad_rows = ((row_own, grad_own), (row_other, grad_other))[turn]
        logits = jnp.dot(rows, weight_router, preferred_element_type=jnp.float32)
        router_prob = jax.nn.softmax(logits, axis=-1)
        picked = jnp.sum(router_prob * expert_here, axis=-1, keepdims=True)
        grad_float = grad_rows.astype(jnp.float32)
        grad_result = (picked * grad_float).astype(jnp.bfloat16)
        produced, grad_input = 0.0, 0.0
        for part in range(len(ups)):
            matrix_up, matrix_down = ups[part], downs[part]
            before = jnp.dot(rows, matrix_up, preferred_element_type=jnp.float32)
            activated, gelu_back = jax.vjp(jax.nn.gelu, before)
            acted = activated.astype(jnp.bfloat16)
            produced = produced + jnp.dot(acted, matrix_down, preferred_element_type=jnp.float32)
            grad_acted = contract_last(grad_result, matrix_down)
            grad_before = gelu_back(grad_acted)[0].astype(jnp.bfloat16)
            grad_input = grad_input + contract_last(grad_before, matrix_up)
            grad_ups[part] = grad_ups[part] + contract_rows(rows, grad_before)
            grad_downs[part] = grad_downs[part] + contract_rows(acted, grad_result)
            if turn == 0 and part == 0:
                produced, grad_input, row_other, grad_other, downs[1:], _ = lax.optimization_barrier(
                    (produced, grad_input, row_other, grad_other, downs[1:], grad_ups[0])
                )
        grad_picked = jnp.sum(grad_float * produced, axis=-1, keepdims=True)
        grad_logits = (picked * (expert_here - router_prob) * grad_picked).astype(jnp.bfloat16)
        grad_router = grad_router + contract_rows(rows, grad_logits)
        grad_inputs.append(grad_input + contract_last(grad_logits, weight_router))
        results.append(picked * produced)

    grad_summed = sum_halves(grad_inputs[0], grad_inputs[1].astype(jnp.bfloat16))
    grad_back = from_experts(grad_summed)
    result_other = after(results[1].astype(jnp.bfloat16), grad_summed)
    result_summed = sum_halves(results[0], result_other)

    down_low = [after(part.astype(jnp.bfloat16), grad_summed) for part in grad_downs[1:]]
    up_low = [after(part.astype(jnp.bfloat16), grad_summed) for part in grad_ups[1:]]

    def moved(parts):
        return [layout.swap(part, step) for part, step in zip(parts, distances)]

    grads_down_moved = moved(down_low)
    grads_up_moved = moved(up_low)

    def own_slice(own, others):
        total = own
        for other in others:
            total = total + other.astype(jnp.float32)
        return total[None]

    grad_residual, grad_gain_two = rms_backward(residual, inverse_two, gain_second, grad_back)
    grad_residual = grad_residual + grad_out_low.astype(jnp.float32)
    grad_mixed = grad_residual.astype(jnp.bfloat16)
    grad_weight_out = contract_rows(attended_low, grad_mixed)
    grad_attended = contract_last(grad_mixed, weight_out).astype(jnp.bfloat16)
    grad_q, grad_k, grad_v, grad_off = attend_backward(
        bases, queries, grad_attended, attended, key_values, skew, logsum
    )
    grad_k, result_summed = lax.optimization_barrier((grad_k, result_summed))
    layer_rows = residual + from_experts(result_summed)
    layer_sent = layout.return_blocks(layer_rows.astype(jnp.bfloat16))

    grad_kv = jnp.concatenate([grad_k, grad_v], axis=1)
    kv_out_part = jnp.concatenate(
        [
            contract_rows(hidden_one, grad_kv).astype(jnp.bfloat16),
            grad_weight_out.astype(jnp.bfloat16),
        ],
        axis=1,
    )
    kv_out_cores = layout.sum_cores(kv_out_part)
    partial_one = contract_last(
        after(grad_kv, kv_out_part, layer_rows), weight_joint[:, model_width:]
    )
    partial_own = contract_last(grad_q, weight_joint[:, :model_width])
    every_normed = every_float * every_inverse
    grad_gain_one = jnp.sum(partial_one * every_normed, axis=0) + jnp.sum(
        partial_own * every_normed[:token_count], axis=0
    )
    grad_hidden_one = layout.sum_rows(partial_one) + partial_own
    kv_out_chips = layout.sum_chips(after(kv_out_cores, layer_rows, partial_own))
    grad_input_norm, _ = rms_backward(tokens_f, inverse_one, gain_first, grad_hidden_one)
    tokens_sent = layout.return_blocks((grad_input_norm + grad_residual).astype(jnp.bfloat16))
    query_part = contract_rows(hidden_one[:token_count], grad_q).astype(jnp.bfloat16)
    grad_table = jnp.dot(
        bucket_hot.astype(jnp.float32),
        grad_off.reshape(head_count, -1)[:, :offset_count].T,
        precision=HIGHEST,
    )
    small_grads = [grad_gain_one, grad_gain_two, grad_router, grad_table]
    shard_rows = joint_projection.shape[0]
    side_width = -(-small_count // (shard_rows * TILE)) * TILE
    small_grads = jnp.concatenate([part.reshape(shards, -1) for part in small_grads], axis=1)
    small_grads = jnp.pad(small_grads, ((0, 0), (0, shard_rows * side_width - small_count)))
    side = small_grads.reshape(shards * shard_rows, side_width).astype(jnp.bfloat16)
    query_cores = layout.sum_cores(jnp.concatenate([query_part, side], axis=1))
    kv_out_chips, query_cores, grads_down_moved, grads_up_moved, layer_sent = (
        lax.optimization_barrier(
            (kv_out_chips, query_cores, grads_down_moved, grads_up_moved, layer_sent)
        )
    )
    grad_expert_down = own_slice(grad_downs[0], grads_down_moved)
    kv_out_own = layout.sum_ctx(kv_out_chips)
    query_chips = layout.sum_chips(query_cores)
    kv_out_own, query_chips, tokens_sent = lax.optimization_barrier(
        (kv_out_own, query_chips, tokens_sent)
    )
    kv_out_sum = layout.spread_ctx(kv_out_own)
    query_own = layout.sum_ctx(query_chips)
    kv_out_sum, query_own = lax.optimization_barrier((kv_out_sum, query_own))
    grad_expert_up = own_slice(grad_ups[0], grads_up_moved)
    query_sum = layout.spread_ctx(query_own)
    layer_out = layout.place_blocks(layer_sent)
    grad_tokens = layout.place_blocks(tokens_sent).astype(jnp.float32)
    kv_sum = kv_out_sum[:, : 2 * model_width]
    out_sum = kv_out_sum[:, 2 * model_width :]
    side_sum = query_sum[:, model_width:].reshape(-1)[:small_count].astype(jnp.float32)
    joint_sum = jnp.concatenate([query_sum[:, :model_width], kv_sum], axis=1)
    sum_gain_one, sum_gain_two, sum_router, sum_table = jnp.split(side_sum, small_cuts)
    return (
        layer_out,
        grad_tokens,
        sum_gain_one,
        joint_sum.astype(jnp.float32),
        out_sum.astype(jnp.float32),
        sum_table.reshape(bias_table.shape),
        sum_gain_two,
        sum_router.reshape(router_weight.shape),
        grad_expert_up,
        grad_expert_down,
    )


def solution(mesh):
    in_specs = (
        P("exp", "ctx", None),
        P("exp"),
        P("exp", None),
        P("exp", None),
        P("exp", None),
        P("exp"),
        P("exp", None),
        P("exp", None, "ctx"),
        P("exp", "ctx", None),
        P("exp", "ctx", None),
        P("exp", "ctx"),
        P(),
        P("exp", "ctx", None),
    )
    out_specs = (
        P("exp", "ctx", None),
        P("exp", "ctx", None),
        P("exp"),
        P("exp", None),
        P("exp", None),
        P("exp", None),
        P("exp"),
        P("exp", None),
        P("exp", None, "ctx"),
        P("exp", "ctx", None),
    )
    return jax.shard_map(
        per_device, mesh=mesh, in_specs=in_specs, out_specs=out_specs, check_vma=False
    )
```

```python
import functools

import jax
import jax.numpy as jnp
from jax import lax
from jax.experimental import pallas as pl
from jax.experimental.pallas import tpu as pltpu
from jax.sharding import PartitionSpec as P

EPSILON = 1e-06
HALF = 64
TILE = 128
GROUP = 256
VMEM_BYTES = 50 * 1024 * 1024
SCORE_SCALE = 0.125
HIGHEST = lax.Precision.HIGHEST
BOTH = ("ctx", "exp")


def contract_last(left, right):
    return lax.dot_general(
        left, right, (((1,), (1,)), ((), ())), preferred_element_type=jnp.float32
    )


def matmul(left, right):
    return lax.dot_general(
        left, right, (((1,), (0,)), ((), ())), preferred_element_type=jnp.float32
    )


def skew_kernel(offset_ref, skew_ref):
    padded = offset_ref.shape[-1]
    kept = skew_ref.shape[1]
    rows = jnp.broadcast_to(offset_ref[0], (TILE, padded))
    rolled = pltpu.roll(rows, padded - (TILE - 1), 1, stride=1, stride_axis=0)
    skew_ref[0] = rolled[:, :kept].T.astype(skew_ref.dtype)


def make_skew(offset_values):
    head_count, padded = offset_values.shape
    kept = padded - TILE
    return pl.pallas_call(
        skew_kernel,
        grid=(head_count,),
        in_specs=[pl.BlockSpec((1, 1, padded), lambda h: (h, 0, 0))],
        out_specs=pl.BlockSpec((1, kept, TILE), lambda h: (h, 0, 0)),
        out_shape=jax.ShapeDtypeStruct((head_count, kept, TILE), jnp.bfloat16),
        compiler_params=pltpu.CompilerParams(vmem_limit_bytes=VMEM_BYTES),
        name="skew_bias",
    )(offset_values.reshape(head_count, 1, padded))


def half_mask(rows, half):
    lanes = lax.broadcasted_iota(jnp.int32, (rows, TILE), 1)
    return (lanes // HALF) == half


def bias_rows(key_base, query_base, seq_len):
    return key_base - query_base + seq_len - TILE


def forward_kernel(
    base_ref, q_ref, k_ref, v_ref, skew_ref, out_ref, lse_ref, score_ref, prob_ref, *, chunk
):
    query_rows = q_ref.shape[0]
    key_rows = k_ref.shape[0]
    seq_len = key_rows
    mask = [half_mask(GROUP, 0), half_mask(GROUP, 1)]
    value_t = v_ref[...].T
    for group in range(query_rows // GROUP):
        rows = slice(group * GROUP, (group + 1) * GROUP)
        query_base = base_ref[0] + group * GROUP
        halves = []
        for half in range(2):
            queries = jnp.where(mask[half], q_ref[rows], 0).astype(jnp.bfloat16)
            score_ref[half] = contract_last(k_ref[...], queries)
            top = jnp.full((8, GROUP), -jnp.inf, jnp.float32)
            for start in range(0, key_rows, chunk):
                key_base = base_ref[start // query_rows] + start % query_rows
                place = pl.multiple_of(bias_rows(key_base, query_base, seq_len), TILE)
                left = skew_ref[half, pl.ds(place, chunk), :]
                right = skew_ref[half, pl.ds(place - TILE, chunk), :]
                bias = jnp.concatenate([left, right], axis=1).astype(jnp.float32)
                piece = score_ref[half, start : start + chunk] + bias
                score_ref[half, start : start + chunk] = piece
                top = jnp.maximum(top, jnp.max(piece.reshape(chunk // 8, 8, GROUP), axis=0))
            top = jnp.max(top, axis=0, keepdims=True)
            total = jnp.zeros((8, GROUP), jnp.float32)
            for start in range(0, key_rows, chunk):
                piece = jnp.exp(score_ref[half, start : start + chunk] - top)
                total = total + jnp.sum(piece.reshape(chunk // 8, 8, GROUP), axis=0)
                prob_ref[half, start : start + chunk] = piece.astype(jnp.bfloat16)
            total = jnp.sum(total, axis=0, keepdims=True)
            lse_ref[0, half : half + 1, rows] = top + jnp.log(total)
            mixed = matmul(value_t[half * HALF : (half + 1) * HALF], prob_ref[half])
            halves.append(mixed / total)
        out_ref[rows] = jnp.concatenate(halves, axis=0).T


def attend_forward(bases, queries, key_values, skew):
    query_rows, width = queries.shape
    key_rows = key_values.shape[0]
    kept = skew.shape[1]
    pairs = width // TILE
    chunk = TILE
    return pl.pallas_call(
        functools.partial(forward_kernel, chunk=chunk),
        grid_spec=pltpu.PrefetchScalarGridSpec(
            num_scalar_prefetch=1,
            grid=(pairs,),
            in_specs=[
                pl.BlockSpec((query_rows, TILE), lambda p, _: (0, p)),
                pl.BlockSpec((key_rows, TILE), lambda p, _: (0, p)),
                pl.BlockSpec((key_rows, TILE), lambda p, _: (0, p + pairs)),
                pl.BlockSpec((2, kept, TILE), lambda p, _: (p, 0, 0)),
            ],
            out_specs=[
                pl.BlockSpec((query_rows, TILE), lambda p, _: (0, p)),
                pl.BlockSpec((1, 2, query_rows), lambda p, _: (p, 0, 0)),
            ],
            scratch_shapes=[
                pltpu.VMEM((2, key_rows, GROUP), jnp.float32),
                pltpu.VMEM((2, key_rows, GROUP), jnp.bfloat16),
            ],
        ),
        out_shape=[
            jax.ShapeDtypeStruct((query_rows, width), jnp.float32),
            jax.ShapeDtypeStruct((pairs, 2, query_rows), jnp.float32),
        ],
        compiler_params=pltpu.CompilerParams(vmem_limit_bytes=VMEM_BYTES),
        name="attend_forward",
    )(bases, queries, key_values, key_values, skew)


def backward_kernel(
    base_ref, q_ref, do_ref, o_ref, k_ref, v_ref, skew_ref, lse_ref,
    dq_ref, dk_ref, dv_ref, off_ref,
    score_ref, gradp_ref, prob_ref, grads_ref, accum_k, accum_v, accum_skew,
    *, chunk,
):
    query_rows = q_ref.shape[0]
    key_rows = k_ref.shape[0]
    seq_len = key_rows
    mask = [half_mask(GROUP, 0), half_mask(GROUP, 1)]
    key_t = k_ref[...].T
    accum_skew[...] = jnp.zeros_like(accum_skew)
    for group in range(query_rows // GROUP):
        rows = slice(group * GROUP, (group + 1) * GROUP)
        query_base = base_ref[0] + group * GROUP
        product = (do_ref[rows].astype(jnp.float32) * o_ref[rows]).T
        halves = []
        sum_k = None
        for half in range(2):
            queries = jnp.where(mask[half], q_ref[rows], 0).astype(jnp.bfloat16)
            grads_out = jnp.where(mask[half], do_ref[rows], 0).astype(jnp.bfloat16)
            score_ref[half] = contract_last(k_ref[...], queries)
            gradp_ref[half] = contract_last(v_ref[...], grads_out)
            logsum = lse_ref[0, half : half + 1, rows]
            delta = jnp.sum(product[half * HALF : (half + 1) * HALF], axis=0, keepdims=True)
            for start in range(0, key_rows, chunk):
                key_base = base_ref[start // query_rows] + start % query_rows
                place = pl.multiple_of(bias_rows(key_base, query_base, seq_len), TILE)
                here = pl.ds(start, chunk)
                left = skew_ref[half, pl.ds(place, chunk), :]
                right = skew_ref[half, pl.ds(place - TILE, chunk), :]
                bias = jnp.concatenate([left, right], axis=1).astype(jnp.float32)
                prob = jnp.exp(score_ref[half, here] + bias - logsum)
                grads = prob * (gradp_ref[half, here] - delta)
                prob_ref[half, here] = prob.astype(jnp.bfloat16)
                grads_ref[half, here] = grads.astype(jnp.bfloat16)
                accum_skew[half, pl.ds(place, chunk), :] += grads[:, :TILE]
                accum_skew[half, pl.ds(place - TILE, chunk), :] += grads[:, TILE:]
            part_k = matmul(grads_ref[half], queries)
            part_v = matmul(prob_ref[half], grads_out)
            sum_k = part_k if sum_k is None else sum_k + part_k
            sum_v = part_v if half == 0 else sum_v + part_v
            halves.append(matmul(key_t[half * HALF : (half + 1) * HALF], grads_ref[half]))
        if group == 0:
            accum_k[...] = sum_k
            accum_v[...] = sum_v
        else:
            accum_k[...] += sum_k
            accum_v[...] += sum_v
        dq_ref[rows] = (jnp.concatenate(halves, axis=0) * 0.125).T.astype(dq_ref.dtype)
    dk_ref[...] = accum_k[...].astype(dk_ref.dtype)
    dv_ref[...] = accum_v[...].astype(dv_ref.dtype)
    for half in range(2):
        turned = accum_skew[half].T
        padded = turned.shape[1]
        count = TILE // 2
        while count:
            turned = turned[:count] + pltpu.roll(turned[count : 2 * count], padded - count, 1)
            count //= 2
        off_ref[0, half : half + 1] = pltpu.roll(turned, TILE - 1, 1)


def attend_backward(bases, queries, grads_out, outputs, key_values, skew, logsum):
    query_rows, width = queries.shape
    key_rows = key_values.shape[0]
    kept = skew.shape[1]
    pairs = width // TILE
    chunk = TILE
    column = lambda count: pl.BlockSpec((count, TILE), lambda p, _: (0, p))
    return pl.pallas_call(
        functools.partial(backward_kernel, chunk=chunk),
        grid_spec=pltpu.PrefetchScalarGridSpec(
            num_scalar_prefetch=1,
            grid=(pairs,),
            in_specs=[
                column(query_rows), column(query_rows), column(query_rows),
                column(key_rows),
                pl.BlockSpec((key_rows, TILE), lambda p, _: (0, p + pairs)),
                pl.BlockSpec((2, kept, TILE), lambda p, _: (p, 0, 0)),
                pl.BlockSpec((1, 2, query_rows), lambda p, _: (p, 0, 0)),
            ],
            out_specs=[
                column(query_rows), column(key_rows), column(key_rows),
                pl.BlockSpec((1, 2, kept + TILE), lambda p, _: (p, 0, 0)),
            ],
            scratch_shapes=[
                pltpu.VMEM((2, key_rows, GROUP), jnp.float32),
                pltpu.VMEM((2, key_rows, GROUP), jnp.float32),
                pltpu.VMEM((2, key_rows, GROUP), jnp.bfloat16),
                pltpu.VMEM((2, key_rows, GROUP), jnp.bfloat16),
                pltpu.VMEM((key_rows, TILE), jnp.float32),
                pltpu.VMEM((key_rows, TILE), jnp.float32),
                pltpu.VMEM((2, kept + TILE, TILE), jnp.float32),
            ],
        ),
        out_shape=[
            jax.ShapeDtypeStruct((query_rows, width), jnp.bfloat16),
            jax.ShapeDtypeStruct((key_rows, width), jnp.bfloat16),
            jax.ShapeDtypeStruct((key_rows, width), jnp.bfloat16),
            jax.ShapeDtypeStruct((pairs, 2, kept + TILE), jnp.float32),
        ],
        compiler_params=pltpu.CompilerParams(vmem_limit_bytes=VMEM_BYTES),
        name="attend_backward",
    )(bases, queries, grads_out, outputs, key_values, key_values, skew, logsum)


def rms_forward(row_data, gain_vec):
    inverse = lax.rsqrt(jnp.mean(row_data * row_data, axis=-1, keepdims=True) + EPSILON)
    return (row_data * inverse * gain_vec, inverse)


def rms_backward(row_data, inverse, gain_vec, grad_out):
    normed = row_data * inverse
    grad_gain = jnp.sum(grad_out * normed, axis=0)
    scaled = grad_out * gain_vec
    spread = jnp.mean(scaled * normed, axis=-1, keepdims=True)
    return (inverse * (scaled - normed * spread), grad_gain)


class Layout:
    def __init__(self):
        self.ctx_count = lax.axis_size("ctx")
        self.exp_count = lax.axis_size("exp")
        self.span = self.ctx_count // 4
        self.members = 2 * self.span
        self.ctx = lax.axis_index("ctx")
        self.core = lax.axis_index("exp") % 2
        self.member = (self.ctx % self.span) * 2 + self.core
        self.side = (self.ctx // self.span) % 2

    def number(self, ctx, exp):
        return ctx * self.exp_count + exp

    def round_pairs(self, turn):
        pairs = []
        for ctx in range(self.ctx_count):
            for exp in range(self.exp_count):
                seq = 2 * (exp % 2) + (turn + ctx) % 2
                member = ctx // 2
                target = self.number(seq * self.span + member // 2, exp // 2 * 2 + member % 2)
                pairs.append((self.number(ctx, exp), target))
        return pairs

    def member_pairs(self, shift):
        pairs = []
        for ctx in range(self.ctx_count):
            for exp in range(self.exp_count):
                start = ctx // self.span * self.span
                member = ((ctx - start) * 2 + exp % 2 + shift) % self.members
                target = self.number(start + member // 2, exp // 2 * 2 + member % 2)
                pairs.append((self.number(ctx, exp), target))
        return pairs

    def gather_blocks(self, blocks):
        got = [
            lax.ppermute(
                lax.dynamic_index_in_dim(blocks, (turn + self.ctx) % 2, 0, keepdims=False),
                BOTH,
                self.round_pairs(turn),
            )
            for turn in range(2)
        ]
        first = jnp.where(self.side == 0, got[0], got[1])
        second = jnp.where(self.side == 0, got[1], got[0])
        return jnp.concatenate([first, second], axis=0)

    def return_blocks(self, rows):
        blocks = rows.reshape((2, rows.shape[0] // 2) + rows.shape[1:])
        got = [
            lax.ppermute(
                lax.dynamic_index_in_dim(blocks, (turn + self.side) % 2, 0, keepdims=False),
                BOTH,
                [(target, source) for source, target in self.round_pairs(turn)],
            )
            for turn in range(2)
        ]
        return got

    def place_blocks(self, got):
        even = self.ctx % 2 == 0
        return jnp.stack([jnp.where(even, got[0], got[1]), jnp.where(even, got[1], got[0])])

    def all_rows(self, rows):
        return jnp.concatenate(
            [rows]
            + [lax.ppermute(rows, BOTH, self.member_pairs(shift)) for shift in range(1, self.members)],
            axis=0,
        )

    def sum_rows(self, partial):
        parts = partial.reshape((self.members, partial.shape[0] // self.members) + partial.shape[1:])
        total = parts[0]
        for shift in range(1, self.members):
            moved = lax.ppermute(
                parts[shift].astype(jnp.bfloat16), BOTH, self.member_pairs(self.members - shift)
            )
            total = total + moved.astype(jnp.float32)
        return total

    def bases(self, row_count):
        return jnp.stack(
            [(self.member - shift) % self.members * row_count for shift in range(self.members)]
        ).astype(jnp.int32)

    def swap(self, rows, distance, axis="ctx"):
        pairs = [(place, place ^ distance) for place in range(lax.axis_size(axis))]
        return lax.ppermute(rows, axis, pairs)

    def gather_small(self, part):
        held = part[None]
        place = lax.axis_index("exp")
        distance = 1
        while distance < self.exp_count:
            other = self.swap(held, distance, "exp")
            upper = (place // distance) % 2 == 1
            held = jnp.where(
                upper,
                jnp.concatenate([other, held], axis=0),
                jnp.concatenate([held, other], axis=0),
            )
            distance *= 2
        return held

    def sum_cores(self, part):
        rows = part.shape[0] // self.exp_count
        blocks = part.reshape(self.exp_count // 2, 2, rows, part.shape[1])
        sent = lax.dynamic_index_in_dim(blocks, 1 - self.core, 1, keepdims=False)
        kept = lax.dynamic_index_in_dim(blocks, self.core, 1, keepdims=False)
        return add_low([kept, self.swap(sent, 1, "exp")])

    def sum_chips(self, blocks):
        pair = lax.axis_index("exp") // 2
        parts = [lax.dynamic_index_in_dim(blocks, pair, 0, keepdims=False)]
        for step in range(1, self.exp_count // 2):
            block = lax.dynamic_index_in_dim(blocks, pair ^ step, 0, keepdims=False)
            parts.append(self.swap(block, 2 * step, "exp"))
        return add_low(parts)

    def sum_ctx(self, total):
        cuts = total.reshape(self.ctx_count, total.shape[0] // self.ctx_count, total.shape[1])
        parts = [lax.dynamic_index_in_dim(cuts, self.ctx, 0, keepdims=False)]
        for step in range(1, self.ctx_count):
            block = lax.dynamic_index_in_dim(cuts, self.ctx ^ step, 0, keepdims=False)
            parts.append(self.swap(block, step))
        return add_low(parts)

    def spread_ctx(self, own):
        every = jnp.stack([own] + [self.swap(own, step) for step in range(1, self.ctx_count)])
        return jnp.concatenate(
            [
                lax.dynamic_index_in_dim(every, self.ctx ^ place, 0, keepdims=False)
                for place in range(self.ctx_count)
            ],
            axis=0,
        )


def add_low(parts):
    total = parts[0].astype(jnp.float32)
    for part in parts[1:]:
        total = total + part.astype(jnp.float32)
    return total.astype(jnp.bfloat16)


def after(value, *events):
    return lax.optimization_barrier((value,) + events)[0]


def per_device(
    tokens_in,
    first_gain,
    joint_projection,
    out_projection,
    bias_table,
    second_gain,
    router_weight,
    expert_up,
    expert_down,
    expert_index,
    keep_mask,
    buckets,
    cotangent,
):
    layout = Layout()
    shards = layout.exp_count
    seq_count, block_len, model_width = tokens_in.shape
    token_count = seq_count * block_len
    expert_count = router_weight.shape[1]
    bucket_count = bias_table.shape[0] * shards
    head_count = bias_table.shape[1]

    small = [first_gain, second_gain, router_weight, bias_table]
    small_sizes = [part.size for part in small]
    small_cuts = [sum(small_sizes[:place]) for place in range(1, len(small))]
    small_count = sum(small_sizes)
    small_padded = -(-small_count // TILE) * TILE
    small_full = layout.gather_small(
        jnp.pad(
            jnp.concatenate([part.reshape(-1) for part in small]), (0, small_padded - small_count)
        )
    )[:, :small_count]
    gain_one, gain_two, weight_router, table = jnp.split(small_full, small_cuts, axis=1)
    weight_router = weight_router.reshape(model_width, expert_count)
    table = table.reshape(bucket_count, head_count)
    gain_first = gain_one.reshape(model_width).astype(jnp.float32)
    gain_second = gain_two.reshape(model_width).astype(jnp.float32)
    weight_joint = lax.all_gather(joint_projection, "exp", axis=0, tiled=True)
    weight_out = lax.all_gather(out_projection, "exp", axis=0, tiled=True)

    tokens = layout.gather_blocks(tokens_in)
    codes = layout.gather_blocks(expert_index.reshape(seq_count, block_len) * 2 + keep_mask)
    grad_out_low = layout.gather_blocks(cotangent)
    every_token = layout.all_rows(tokens)
    chosen = codes // 2
    kept = codes % 2

    distances = list(range(2, layout.ctx_count, 2))
    held_up = after(expert_up[0], grad_out_low)
    held_down = after(expert_down[0], grad_out_low)
    up_moved = [layout.swap(held_up, step) for step in distances]
    down_moved = [layout.swap(held_down, step) for step in distances]

    offset_count = buckets.shape[0]
    bucket_hot = buckets[None, :] == jnp.arange(bucket_count, dtype=jnp.int32)[:, None]
    offset_values = lax.dot_general(
        table,
        bucket_hot.astype(jnp.bfloat16),
        (((0,), (0,)), ((), ())),
        preferred_element_type=jnp.float32,
    )
    skew = make_skew(jnp.pad(offset_values, ((0, 0), (0, 1))))

    is_choice = chosen[:, None] == jnp.arange(expert_count, dtype=jnp.int32)
    most_rows = max(2, (5 * block_len + 4 * expert_count - 1) // (4 * expert_count))
    capacity = seq_count * most_rows
    place = jnp.arange(token_count, dtype=jnp.int32)
    earlier = (place[:, None] >= place[None, :]) & (
        place[:, None] // block_len == place[None, :] // block_len
    )
    running = jnp.dot(
        earlier.astype(jnp.bfloat16),
        is_choice.astype(jnp.bfloat16),
        preferred_element_type=jnp.float32,
    )
    slot_rank = (jnp.sum(running * is_choice.astype(jnp.float32), axis=-1) - 1.0).astype(jnp.int32)
    token_slot = chosen * capacity + place // block_len * most_rows + slot_rank
    slot_hot = (
        (token_slot[:, None] == jnp.arange(expert_count * capacity, dtype=jnp.int32))
        & (kept[:, None] > 0)
    ).astype(jnp.bfloat16)

    def exchange(row_data):
        return lax.all_to_all(
            row_data.reshape(shards, -1, model_width), "exp", split_axis=0, concat_axis=0, tiled=True
        ).reshape(-1, model_width)

    def to_experts(row_data):
        sent = lax.dot_general(
            slot_hot, row_data, (((0,), (0,)), ((), ())), preferred_element_type=jnp.float32
        ).astype(jnp.bfloat16)
        return exchange(sent)

    def sum_halves(own_part, other_part):
        other = layout.swap(other_part, 1)
        return (own_part + other.astype(jnp.float32)).astype(jnp.bfloat16)

    def from_experts(summed):
        return jnp.dot(slot_hot, exchange(summed), preferred_element_type=jnp.float32)

    every_float = every_token.astype(jnp.float32)
    tokens_f = every_float[:token_count]
    normed_one, every_inverse = rms_forward(every_float, gain_first)
    inverse_one = every_inverse[:token_count]
    hidden_one = normed_one.astype(jnp.bfloat16)
    queries = jnp.dot(
        hidden_one[:token_count], weight_joint[:, :model_width], preferred_element_type=jnp.float32
    ).astype(jnp.bfloat16) * jnp.bfloat16(SCORE_SCALE)
    key_values = jnp.dot(
        hidden_one, weight_joint[:, model_width:], preferred_element_type=jnp.float32
    ).astype(jnp.bfloat16)
    queries = after(queries, grad_out_low)
    bases = layout.bases(token_count)
    attended, logsum = attend_forward(bases, queries, key_values, skew)
    attended_low = attended.astype(jnp.bfloat16)
    residual = tokens_f + jnp.dot(attended_low, weight_out, preferred_element_type=jnp.float32)
    normed_two, inverse_two = rms_forward(residual, gain_second)
    hidden_two = after(normed_two.astype(jnp.bfloat16), *up_moved)

    row_own = to_experts(hidden_two)
    row_other = layout.swap(row_own, 1)
    grad_own = to_experts(after(grad_out_low, row_own))
    grad_other = layout.swap(grad_own, 1)
    ups = [expert_up[0]] + up_moved
    downs = [expert_down[0]] + down_moved

    expert_here = jnp.arange(expert_count, dtype=jnp.int32) == lax.axis_index("exp")
    expert_here = expert_here.astype(jnp.float32)[None, :]

    def contract_rows(left, right):
        return lax.dot_general(
            left, right, (((0,), (0,)), ((), ())), preferred_element_type=jnp.float32
        )

    results, grad_inputs = [], []
    grad_router = 0.0
    grad_ups, grad_downs = [0.0] * len(ups), [0.0] * len(ups)
    for turn in range(2):
        rows, grad_rows = ((row_own, grad_own), (row_other, grad_other))[turn]
        logits = jnp.dot(rows, weight_router, preferred_element_type=jnp.float32)
        router_prob = jax.nn.softmax(logits, axis=-1)
        picked = jnp.sum(router_prob * expert_here, axis=-1, keepdims=True)
        grad_float = grad_rows.astype(jnp.float32)
        grad_result = (picked * grad_float).astype(jnp.bfloat16)
        produced, grad_input = 0.0, 0.0
        for part in range(len(ups)):
            matrix_up, matrix_down = ups[part], downs[part]
            before = jnp.dot(rows, matrix_up, preferred_element_type=jnp.float32)
            activated, gelu_back = jax.vjp(jax.nn.gelu, before)
            acted = activated.astype(jnp.bfloat16)
            produced = produced + jnp.dot(acted, matrix_down, preferred_element_type=jnp.float32)
            grad_acted = contract_last(grad_result, matrix_down)
            grad_before = gelu_back(grad_acted)[0].astype(jnp.bfloat16)
            grad_input = grad_input + contract_last(grad_before, matrix_up)
            grad_ups[part] = grad_ups[part] + contract_rows(rows, grad_before)
            grad_downs[part] = grad_downs[part] + contract_rows(acted, grad_result)
            if turn == 0 and part == 0:
                produced, grad_input, downs[1:], _ = lax.optimization_barrier(
                    (produced, grad_input, downs[1:], grad_ups[0])
                )
        if turn == 0:
            produced, grad_input, row_other, grad_other = lax.optimization_barrier(
                (produced, grad_input, row_other, grad_other)
            )
        grad_picked = jnp.sum(grad_float * produced, axis=-1, keepdims=True)
        grad_logits = (picked * (expert_here - router_prob) * grad_picked).astype(jnp.bfloat16)
        grad_router = grad_router + contract_rows(rows, grad_logits)
        grad_inputs.append(grad_input + contract_last(grad_logits, weight_router))
        results.append(picked * produced)

    grad_summed = sum_halves(grad_inputs[0], grad_inputs[1].astype(jnp.bfloat16))
    grad_back = from_experts(grad_summed)
    result_other = after(results[1].astype(jnp.bfloat16), grad_summed)
    result_summed = sum_halves(results[0], result_other)

    down_low = [after(part.astype(jnp.bfloat16), grad_summed) for part in grad_downs[1:]]
    up_low = [after(part.astype(jnp.bfloat16), grad_summed) for part in grad_ups[1:]]

    def moved(parts):
        return [layout.swap(part, step) for part, step in zip(parts, distances)]

    grads_down_moved = moved(down_low)
    grads_up_moved = moved(up_low)

    def own_slice(own, others):
        total = own
        for other in others:
            total = total + other.astype(jnp.float32)
        return total[None]

    grad_residual, grad_gain_two = rms_backward(residual, inverse_two, gain_second, grad_back)
    grad_residual = grad_residual + grad_out_low.astype(jnp.float32)
    grad_mixed = grad_residual.astype(jnp.bfloat16)
    grad_weight_out = contract_rows(attended_low, grad_mixed)
    grad_attended = contract_last(grad_mixed, weight_out).astype(jnp.bfloat16)
    grad_q, grad_k, grad_v, grad_off = attend_backward(
        bases, queries, grad_attended, attended, key_values, skew, logsum
    )
    grad_k, result_summed = lax.optimization_barrier((grad_k, result_summed))
    layer_rows = residual + from_experts(result_summed)
    layer_sent = layout.return_blocks(layer_rows.astype(jnp.bfloat16))

    grad_kv = jnp.concatenate([grad_k, grad_v], axis=1)
    kv_out_part = jnp.concatenate(
        [
            contract_rows(hidden_one, grad_kv).astype(jnp.bfloat16),
            grad_weight_out.astype(jnp.bfloat16),
        ],
        axis=1,
    )
    kv_out_cores = layout.sum_cores(kv_out_part)
    partial_one = contract_last(
        after(grad_kv, kv_out_part, layer_rows), weight_joint[:, model_width:]
    )
    partial_own = contract_last(grad_q, weight_joint[:, :model_width])
    every_normed = every_float * every_inverse
    grad_gain_one = jnp.sum(partial_one * every_normed, axis=0) + jnp.sum(
        partial_own * every_normed[:token_count], axis=0
    )
    grad_hidden_one = layout.sum_rows(partial_one) + partial_own
    kv_out_chips = layout.sum_chips(after(kv_out_cores, layer_rows, partial_own))
    grad_input_norm, _ = rms_backward(tokens_f, inverse_one, gain_first, grad_hidden_one)
    tokens_sent = layout.return_blocks((grad_input_norm + grad_residual).astype(jnp.bfloat16))
    query_part = contract_rows(hidden_one[:token_count], grad_q).astype(jnp.bfloat16)
    grad_table = jnp.dot(
        bucket_hot.astype(jnp.float32),
        grad_off.reshape(head_count, -1)[:, :offset_count].T,
        precision=HIGHEST,
    )
    small_grads = [grad_gain_one, grad_gain_two, grad_router, grad_table]
    shard_rows = joint_projection.shape[0]
    side_width = -(-small_count // (shard_rows * TILE)) * TILE
    small_grads = jnp.concatenate([part.reshape(shards, -1) for part in small_grads], axis=1)
    small_grads = jnp.pad(small_grads, ((0, 0), (0, shard_rows * side_width - small_count)))
    side = small_grads.reshape(shards * shard_rows, side_width).astype(jnp.bfloat16)
    query_cores = layout.sum_cores(jnp.concatenate([query_part, side], axis=1))
    kv_out_chips, query_cores, grads_down_moved, grads_up_moved, layer_sent = (
        lax.optimization_barrier(
            (kv_out_chips, query_cores, grads_down_moved, grads_up_moved, layer_sent)
        )
    )
    grad_expert_down = own_slice(grad_downs[0], grads_down_moved)
    kv_out_own = layout.sum_ctx(kv_out_chips)
    query_chips = layout.sum_chips(query_cores)
    kv_out_own, query_chips, tokens_sent = lax.optimization_barrier(
        (kv_out_own, query_chips, tokens_sent)
    )
    kv_out_sum = layout.spread_ctx(kv_out_own)
    query_own = layout.sum_ctx(query_chips)
    kv_out_sum, query_own = lax.optimization_barrier((kv_out_sum, query_own))
    grad_expert_up = own_slice(grad_ups[0], grads_up_moved)
    query_sum = layout.spread_ctx(query_own)
    layer_out = layout.place_blocks(layer_sent)
    grad_tokens = layout.place_blocks(tokens_sent).astype(jnp.float32)
    kv_sum = kv_out_sum[:, : 2 * model_width]
    out_sum = kv_out_sum[:, 2 * model_width :]
    side_sum = query_sum[:, model_width:].reshape(-1)[:small_count].astype(jnp.float32)
    joint_sum = jnp.concatenate([query_sum[:, :model_width], kv_sum], axis=1)
    sum_gain_one, sum_gain_two, sum_router, sum_table = jnp.split(side_sum, small_cuts)
    return (
        layer_out,
        grad_tokens,
        sum_gain_one,
        joint_sum.astype(jnp.float32),
        out_sum.astype(jnp.float32),
        sum_table.reshape(bias_table.shape),
        sum_gain_two,
        sum_router.reshape(router_weight.shape),
        grad_expert_up,
        grad_expert_down,
    )


def solution(mesh):
    in_specs = (
        P("exp", "ctx", None),
        P("exp"),
        P("exp", None),
        P("exp", None),
        P("exp", None),
        P("exp"),
        P("exp", None),
        P("exp", None, "ctx"),
        P("exp", "ctx", None),
        P("exp", "ctx", None),
        P("exp", "ctx"),
        P(),
        P("exp", "ctx", None),
    )
    out_specs = (
        P("exp", "ctx", None),
        P("exp", "ctx", None),
        P("exp"),
        P("exp", None),
        P("exp", None),
        P("exp", None),
        P("exp"),
        P("exp", None),
        P("exp", None, "ctx"),
        P("exp", "ctx", None),
    )
    return jax.shard_map(
        per_device, mesh=mesh, in_specs=in_specs, out_specs=out_specs, check_vma=False
    )
```
